32 devices in a mesh: dp: 8 (over y, x, core), tensor: 4 (over z).
Axes of the slice: x: 2, y: 2, z: 4, core: 2. Of those that a mesh axis runs over, the one named last changes fastest.
Arguments:
- tokens: bfloat16 [8192, 2048], P(('dp', 'tensor')), may hold values from -6 to 6
- lengths: int32 [8, 4], P('dp'), may hold values from 1 to 512, 1024 in all within a row
- w_attn: float32 [4, 2048, 2048], P(None, 'dp', 'tensor')
- w_mlp: float32 [3, 2048, 8192], P(None, 'dp', 'tensor')
- norm_gains: float32 [4, 2048], P(None, ('dp', 'tensor')), may hold values from 0.25 to 1.75
- moment_attn: float32 [4, 2048, 2048], P(None, 'dp', 'tensor')
- square_attn: float32 [4, 2048, 2048], P(None, 'dp', 'tensor')
- moment_mlp: float32 [3, 2048, 8192], P(None, 'dp', 'tensor')
- square_mlp: float32 [3, 2048, 8192], P(None, 'dp', 'tensor')
- moment_gains: float32 [4, 2048], P(None, ('dp', 'tensor'))
- square_gains: float32 [4, 2048], P(None, ('dp', 'tensor'))
- cotangent: bfloat16 [8192, 2048], P(('dp', 'tensor')), may hold values from -6 to 6
Outputs:
- out_tokens: bfloat16 [8192, 2048], P(('dp', 'tensor'))
- grad_tokens: bfloat16 [8192, 2048], P(('dp', 'tensor'))
- new_attn: float32 [4, 2048, 2048], P(None, 'dp', 'tensor')
- new_moment_attn: float32 [4, 2048, 2048], P(None, 'dp', 'tensor')
- new_square_attn: float32 [4, 2048, 2048], P(None, 'dp', 'tensor')
- new_mlp: float32 [3, 2048, 8192], P(None, 'dp', 'tensor')
- new_moment_mlp: float32 [3, 2048, 8192], P(None, 'dp', 'tensor')
- new_square_mlp: float32 [3, 2048, 8192], P(None, 'dp', 'tensor')
- new_gains: float32 [4, 2048], P(None, ('dp', 'tensor'))
- new_moment_gains: float32 [4, 2048], P(None, ('dp', 'tensor'))
- new_square_gains: float32 [4, 2048], P(None, ('dp', 'tensor'))
The draws below stay inside these ranges and needn't reach their ends.
All inputs are finite; a program needn't handle non-finite values.
Results may differ from the reference program's by a relative error of at most 0.018.
The reference program's roundings to bfloat16 on the way count: a program that leaves them out, or rounds other values in their place, can miss the bound.
Values may be sent and summed in bfloat16 or wider, within the bound.
No kernel may reach another device: no remote copies, remote signals or barrier semaphores. Data moves between devices by JAX's collectives and lax.ppermute only.
A program may use at most 320 MiB of HBM per device.

```python
import math
import jax
import jax.numpy as jnp
import numpy as np
from jax import lax

D = 2048
FF = 8192
HEADS = 16
HDIM = 128
SEQ = 1024
DOCS = 4
STEP = 10
NSEQ = 8
TOKENS = 8192


MOMENT_ONE = 0.111


MOMENT_TWO = 0.0526


LOG_FOUR = 1.3862944


ATTN_FACTORS = (1.0, 1.0, 1.0, 1.0)


MLP_FACTORS = (0.7, 0.7, 1.0)


GAIN_FACTORS = (1.0, 1.0, 0.5, 0.5)


def grad_sizes(factors, rank):
    sizes = jnp.asarray(factors, jnp.float32) * jnp.sqrt(jnp.float32(TOKENS))
    return sizes.reshape((len(factors),) + (1,) * (rank - 1))


def draw_w_attn(key, part):
    key = jax.random.fold_in(key, 11)
    array_shape = (4, D, D)
    columns = jnp.arange(D, dtype=jnp.float32) / D
    base_part = jax.random.truncated_normal(key, -3.0, 3.0, array_shape, jnp.float32)
    rising = 0.5 + columns
    ones_row = jnp.ones((D,), jnp.float32)
    slot_scale = jnp.stack([jnp.sqrt(rising), jnp.sqrt(rising), ones_row, ones_row])[:, None, :]
    return base_part * slot_scale / jnp.sqrt(jnp.float32(D))


def draw_w_mlp(key, part):
    key = jax.random.fold_in(key, 12)
    array_shape = (3, D, FF)
    base_part = jax.random.truncated_normal(key, -3.0, 3.0, array_shape, jnp.float32)
    fans = jnp.asarray([D, D, FF], jnp.float32)
    return base_part * lax_rsqrt(fans)[:, None, None]


def lax_rsqrt(values):
    return 1.0 / jnp.sqrt(values)


def draw_moment_attn(key, part):
    key = jax.random.fold_in(key, 21)
    array_shape = (4, D, D)
    random_part = jax.random.normal(key, array_shape, jnp.float32)
    return random_part * grad_sizes(ATTN_FACTORS, 3) * MOMENT_ONE


def draw_square_attn(key, part):
    key = jax.random.fold_in(key, 22)
    array_shape = (4, D, D)
    factor = jnp.exp(jax.random.uniform(key, array_shape, jnp.float32, 0.0, LOG_FOUR))
    sizes = grad_sizes(ATTN_FACTORS, 3)
    return factor * MOMENT_TWO * sizes * sizes


def draw_moment_mlp(key, part):
    key = jax.random.fold_in(key, 23)
    array_shape = (3, D, FF)
    random_part = jax.random.normal(key, array_shape, jnp.float32)
    return random_part * grad_sizes(MLP_FACTORS, 3) * MOMENT_ONE


def draw_square_mlp(key, part):
    key = jax.random.fold_in(key, 24)
    array_shape = (3, D, FF)
    factor = jnp.exp(jax.random.uniform(key, array_shape, jnp.float32, 0.0, LOG_FOUR))
    sizes = grad_sizes(MLP_FACTORS, 3)
    return factor * MOMENT_TWO * sizes * sizes


def draw_moment_gains(key, part):
    key = jax.random.fold_in(key, 25)
    array_shape = (4, D)
    random_part = jax.random.normal(key, array_shape, jnp.float32)
    return random_part * grad_sizes(GAIN_FACTORS, 2) * MOMENT_ONE


def draw_square_gains(key, part):
    key = jax.random.fold_in(key, 26)
    array_shape = (4, D)
    factor = jnp.exp(jax.random.uniform(key, array_shape, jnp.float32, 0.0, LOG_FOUR))
    sizes = grad_sizes(GAIN_FACTORS, 2)
    return factor * MOMENT_TWO * sizes * sizes


def shard_levels(key, shape, pieces, least, largest):
    gain = 1.0
    for axis_at, parts in pieces:
        heights = jax.random.uniform(jax.random.fold_in(jax.random.fold_in(key, 6), axis_at), (parts,), jnp.float32, least / len(pieces), largest / len(pieces))
        gain = gain * jnp.repeat(jnp.exp(heights), shape[axis_at] // parts).reshape((-1,) + (1,) * (len(shape) - 1 - axis_at))
    return gain


def profile(amount, total, limit, lean):
    portions = [(1 << 20) // math.isqrt(grade ** lean) + 1 for grade in range(2, amount + 1)]
    surplus, given = total - limit - (amount - 1), [1] * (amount - 1)
    while surplus > 0:
        movable = [i for i in range(amount - 1) if given[i] < limit]
        mass, remaining = sum([portions[i] for i in movable]), surplus
        for i in movable:
            extra = min(limit - given[i], max(1, remaining * portions[i] // mass), surplus)
            given[i] = given[i] + extra
            surplus = surplus - extra
    return np.array([limit] + given)


def ragged_sizes(rng, number_of, total, bound, slope):
    if number_of == 2:
        one = jax.random.randint(rng, (), max(1, total - bound), min(bound, total - 1) + 1)
        return jnp.stack([one, total - one])
    sizes = jnp.asarray(profile(number_of, total, bound, slope), jnp.int32)
    pairs = (number_of - 1) // 2
    giver, receiver = sizes[1:1 + 2 * pairs:2], sizes[2:2 + 2 * pairs:2]
    slack = jnp.minimum(giver - 1, bound - receiver)
    passed = jax.random.randint(jax.random.fold_in(rng, 1), (pairs,), 0, 1 << 20) % (slack + 1)
    sizes = sizes.at[1:1 + 2 * pairs:2].set(giver - passed).at[2:2 + 2 * pairs:2].set(receiver + passed)
    return sizes[jax.random.permutation(jax.random.fold_in(rng, 2), number_of)]


def centred(rng, shape, spread, most, pieces=(), kind=jnp.bfloat16):
    factor_of = shard_levels(rng, shape, pieces, -0.22, 0.18) if pieces else 1.0
    drawn = jax.random.normal(rng, shape, jnp.float32) * spread * factor_of
    return jnp.minimum(jnp.maximum(drawn, -most), most).astype(kind)


def setup_inputs(seed: int = 0) -> dict:
    keys = jax.random.split(jax.random.key(seed), 13)
    return {
        "tokens": centred(keys[0], (TOKENS, D), 1.0, 6.0, ((0, 32),)),
        "lengths": jax.vmap(lambda own: ragged_sizes(own, DOCS, SEQ, SEQ // 2, 2))(jax.random.split(keys[1], NSEQ)).reshape((NSEQ, DOCS)).astype(jnp.int32),
        "w_attn": draw_w_attn(jax.random.fold_in(keys[12], 71), 0),
        "w_mlp": draw_w_mlp(jax.random.fold_in(keys[12], 71), 0),
        "norm_gains": jnp.clip(1.0 + 0.15 * jax.random.normal(keys[4], (4, D), jnp.float32), 0.25, 1.75),
        "moment_attn": draw_moment_attn(jax.random.fold_in(keys[12], 71), 0),
        "square_attn": draw_square_attn(jax.random.fold_in(keys[12], 71), 0),
        "moment_mlp": draw_moment_mlp(jax.random.fold_in(keys[12], 71), 0),
        "square_mlp": draw_square_mlp(jax.random.fold_in(keys[12], 71), 0),
        "moment_gains": draw_moment_gains(jax.random.fold_in(keys[12], 71), 0),
        "square_gains": draw_square_gains(jax.random.fold_in(keys[12], 71), 0),
        "cotangent": centred(keys[11], (TOKENS, D), 1.0, 6.0, ((0, 32),)),
    }


@jax.custom_vjp
def low(v):
    return lax.optimization_barrier(v.astype(jnp.bfloat16)).astype(jnp.float32)

@jax.custom_vjp
def low_back(v):
    return v

def low_keep(v):
    return (low(v), None)

def low_pass(kept, grad):
    return (grad,)

def back_keep(v):
    return (v, None)

def back_low(kept, grad):
    return (low(grad),)
low.defvjp(low_keep, low_pass)
low_back.defvjp(back_keep, back_low)
NORM_EPS = 1e-06
ROPE_BASE = 500000.0
BETA_ONE = 0.9
BETA_TWO = 0.95
ADAM_EPS = 1e-08
RATE_MATRIX = 0.03
RATE_GAIN = 0.6
DECAY_MATRIX = 0.1

def matmul(left_side, right_side):
    return jnp.dot(left_side, right_side, precision=lax.Precision.HIGHEST, preferred_element_type=jnp.float32)

def doc_positions(lengths, seq_len):
    ends = jnp.cumsum(lengths, axis=-1, dtype=jnp.int32)
    starts = ends - lengths
    places = jnp.arange(seq_len, dtype=jnp.int32)
    inside = starts[:, None, :] <= places[None, :, None]
    begins = lax.optimization_barrier(jnp.max(jnp.where(inside, starts[:, None, :], jnp.int32(0)), axis=-1))
    return places[None, :] - begins

def rope_tables(positions, head_dim):
    halfway = head_dim // 2
    powers = jnp.arange(halfway, dtype=jnp.float32) * (2.0 / head_dim)
    angles = positions.astype(jnp.float32)[:, None] * jnp.power(ROPE_BASE, -powers)
    return (jnp.cos(angles), jnp.sin(angles))

def rotate(values, cos_table, sin_table):
    halfway = values.shape[-1] // 2
    first_half = values[..., :halfway]
    second_half = values[..., halfway:]
    cosine = cos_table[:, None, :]
    sine = sin_table[:, None, :]
    return jnp.concatenate([first_half * cosine - second_half * sine, second_half * cosine + first_half * sine], axis=-1)

def post_norm(raw_rows, gain_row):
    return raw_rows * lax.rsqrt(lax.optimization_barrier(jnp.mean(raw_rows * raw_rows, axis=-1, keepdims=True)) + NORM_EPS) * gain_row

def adamw(weight, gradient, moment_one, moment_two, rate, decay):
    moment_one = BETA_ONE * moment_one + (1.0 - BETA_ONE) * gradient
    moment_two = BETA_TWO * moment_two + (1.0 - BETA_TWO) * gradient * gradient
    fix_one = 1.0 - BETA_ONE ** STEP
    fix_two = 1.0 - BETA_TWO ** STEP
    update = moment_one / fix_one / (jnp.sqrt(moment_two / fix_two) + ADAM_EPS)
    return (weight * (1.0 - rate * decay) - rate * update, moment_one, moment_two)

def attend_sequence(sequence_parts):
    queries, keys_seq, values_seq = sequence_parts
    block_rows = min(512, SEQ)
    block_count = SEQ // block_rows
    score_scale = HDIM ** (-0.5)
    offsets = jnp.arange(block_count, dtype=jnp.int32) * block_rows
    query_blocks = queries.reshape(block_count, block_rows, HEADS, HDIM)

    def one_block(block_parts):
        query_block, offset = block_parts
        scores = jnp.einsum('qhd,khd->hqk', query_block, keys_seq, precision=lax.Precision.HIGHEST) * score_scale
        scores = low_back(scores)
        query_pos = offset + jnp.arange(block_rows, dtype=jnp.int32)
        key_pos = jnp.arange(SEQ, dtype=jnp.int32)
        scores = jnp.where(key_pos[None, None, :] <= query_pos[None, :, None], scores, -jnp.inf)
        probability = low(jax.nn.softmax(scores, axis=-1))
        return jnp.einsum('hqk,khd->qhd', probability, values_seq, precision=lax.Precision.HIGHEST)
    mixed_rows = lax.map(jax.checkpoint(one_block), (query_blocks, offsets))
    return mixed_rows.reshape(SEQ, HEADS, HDIM)

def forward(token_rows, places, attn_weights, mlp_weights, gain_rows):
    attn_weights = low(attn_weights)
    mlp_weights = low(mlp_weights)
    gain_rows = low(gain_rows)
    queries = low_back(matmul(token_rows, attn_weights[0]))
    keys_all = low_back(matmul(token_rows, attn_weights[1]))
    values_all = low(low_back(matmul(token_rows, attn_weights[2])))
    queries = queries * lax.rsqrt(lax.optimization_barrier(jnp.mean(queries * queries, axis=-1, keepdims=True)) + NORM_EPS) * gain_rows[2]
    keys_all = keys_all * lax.rsqrt(lax.optimization_barrier(jnp.mean(keys_all * keys_all, axis=-1, keepdims=True)) + NORM_EPS) * gain_rows[3]
    cos_table, sin_table = rope_tables(places, HDIM)
    seq_total = token_rows.shape[0] // SEQ
    queries = low(rotate(queries.reshape(-1, HEADS, HDIM), cos_table, sin_table)).reshape(seq_total, SEQ, HEADS, HDIM)
    keys_all = low(rotate(keys_all.reshape(-1, HEADS, HDIM), cos_table, sin_table)).reshape(seq_total, SEQ, HEADS, HDIM)
    values_all = values_all.reshape(seq_total, SEQ, HEADS, HDIM)
    mixed_rows = lax.map(attend_sequence, (queries, keys_all, values_all)).reshape(-1, D)
    mixed_rows = low(low_back(mixed_rows))
    raw_attn = low_back(matmul(mixed_rows, attn_weights[3].T))
    hidden = token_rows + post_norm(raw_attn, gain_rows[0])
    hidden_low = low(hidden)
    gate_rows = low_back(matmul(hidden_low, mlp_weights[0]))
    up_rows = low_back(matmul(hidden_low, mlp_weights[1]))
    inner_rows = low(jax.nn.silu(gate_rows) * up_rows)
    raw_mlp = low_back(matmul(inner_rows, mlp_weights[2].T))
    return hidden + post_norm(raw_mlp, gain_rows[1])

def reference(tokens, lengths, w_attn, w_mlp, norm_gains, moment_attn, square_attn, moment_mlp, square_mlp, moment_gains, square_gains, cotangent):
    seq_total = TOKENS // SEQ
    group_size = 1
    for candidate in range(1, seq_total + 1):
        if seq_total % candidate == 0 and candidate * SEQ <= 4096:
            group_size = candidate
    group_total = seq_total // group_size
    token_groups = tokens.astype(jnp.float32).reshape(group_total, group_size * SEQ, D)
    back_groups = cotangent.astype(jnp.float32).reshape(group_total, group_size * SEQ, D)
    place_groups = doc_positions(lengths, SEQ).reshape(group_total, group_size * SEQ)

    def group_step(totals, group_parts):
        token_rows, back_rows, places = group_parts

        def apply_layer(rows_in, attn_in, mlp_in, gain_in):
            return forward(rows_in, places, attn_in, mlp_in, gain_in)
        result, pull_back = jax.vjp(apply_layer, token_rows, w_attn, w_mlp, norm_gains)
        d_rows, d_attn, d_mlp, d_gains = pull_back(back_rows)
        new_totals = (totals[0] + d_attn, totals[1] + d_mlp, totals[2] + d_gains)
        return (new_totals, (result.astype(jnp.bfloat16), d_rows.astype(jnp.bfloat16)))
    zero_totals = (jnp.zeros_like(w_attn), jnp.zeros_like(w_mlp), jnp.zeros_like(norm_gains))
    grads_all, outputs = lax.scan(group_step, zero_totals, (token_groups, back_groups, place_groups))
    out_tokens = outputs[0].reshape(TOKENS, D)
    grad_tokens = outputs[1].reshape(TOKENS, D)
    new_attn, new_moment_attn, new_square_attn = adamw(w_attn, grads_all[0], moment_attn, square_attn, RATE_MATRIX, DECAY_MATRIX)
    new_mlp, new_moment_mlp, new_square_mlp = adamw(w_mlp, grads_all[1], moment_mlp, square_mlp, RATE_MATRIX, DECAY_MATRIX)
    new_gains, new_moment_gains, new_square_gains = adamw(norm_gains, grads_all[2], moment_gains, square_gains, RATE_GAIN, 0.0)
    return (out_tokens, grad_tokens, new_attn, new_moment_attn, new_square_attn, new_mlp, new_moment_mlp, new_square_mlp, new_gains, new_moment_gains, new_square_gains)
```

```python
import jax
import jax.numpy as jnp
from jax import lax
from jax.experimental import pallas as pl
from jax.experimental.pallas import tpu as pltpu
from jax.sharding import PartitionSpec as P

HDIM = 128
STEP = 10
CHUNKS = 2
MIB = 1 << 20


NORM_EPS = 1e-06
ROPE_BASE = 500000.0
BETA_ONE = 0.9
BETA_TWO = 0.95
ADAM_EPS = 1e-08
RATE_MATRIX = 0.03
RATE_GAIN = 0.6
DECAY_MATRIX = 0.1
ROW_CONTRACT = (((0,), (0,)), ((), ()))
COLUMN_CONTRACT = (((1,), (1,)), ((), ()))


def doc_positions(lengths, seq_len):
    ends = jnp.cumsum(lengths, axis=-1, dtype=jnp.int32)
    starts = ends - lengths
    places = jnp.arange(seq_len, dtype=jnp.int32)
    inside = starts[:, None, :] <= places[None, :, None]
    begins = jnp.max(jnp.where(inside, starts[:, None, :], jnp.int32(0)), axis=-1)
    return places[None, :] - begins


def rope_tables(positions, head_dim):
    halfway = head_dim // 2
    powers = jnp.arange(halfway, dtype=jnp.float32) * (2.0 / head_dim)
    angles = positions.astype(jnp.float32)[:, None] * jnp.power(ROPE_BASE, -powers)
    return (jnp.cos(angles), jnp.sin(angles))


def rotate(values, cos_table, sin_table):
    halfway = values.shape[-1] // 2
    first_half = values[..., :halfway]
    second_half = values[..., halfway:]
    cosine = cos_table[:, None, :]
    sine = sin_table[:, None, :]
    return jnp.concatenate(
        [first_half * cosine - second_half * sine, second_half * cosine + first_half * sine],
        axis=-1,
    )


def post_norm(raw_rows, gain_row):
    return (
        raw_rows
        * lax.rsqrt(jnp.mean(raw_rows * raw_rows, axis=-1, keepdims=True) + NORM_EPS)
        * gain_row
    )


def adamw(weight, gradient, moment_one, moment_two, rate, decay):
    moment_one = BETA_ONE * moment_one + (1.0 - BETA_ONE) * gradient
    moment_two = BETA_TWO * moment_two + (1.0 - BETA_TWO) * gradient * gradient
    fix_one = 1.0 - BETA_ONE**STEP
    fix_two = 1.0 - BETA_TWO**STEP
    update = moment_one / fix_one / (jnp.sqrt(moment_two / fix_two) + ADAM_EPS)
    return (weight * (1.0 - rate * decay) - rate * update, moment_one, moment_two)


def masked_scores(query_block, key_rows, offset, score_scale):
    scores = (
        jnp.einsum("qhd,khd->hqk", query_block, key_rows, preferred_element_type=jnp.float32)
        * score_scale
    )
    query_pos = offset + jnp.arange(query_block.shape[0], dtype=jnp.int32)
    key_pos = jnp.arange(key_rows.shape[0], dtype=jnp.int32)
    return jnp.where(key_pos[None, None, :] <= query_pos[None, :, None], scores, -jnp.inf)


def pick(index, cases):
    if all(case is cases[0] for case in cases):
        return cases[0]
    return lax.select_n(index, *cases)


def line_gather(piece):
    count = lax.axis_size("tensor")
    here = lax.axis_index("tensor")
    from_low, from_high = [piece], [piece]
    for step in range(1, count):
        rising = [(i, i + 1) for i in range(step - 1, count - 1)]
        falling = [(i + 1, i) for i in range(count - step)]
        from_low.append(lax.ppermute(from_low[-1], "tensor", rising))
        from_high.append(lax.ppermute(from_high[-1], "tensor", falling))
    return [
        pick(
            here,
            [from_low[i - owner] if i >= owner else from_high[owner - i] for i in range(count)],
        )
        for owner in range(count)
    ]


def line_scatter(parts):
    count = lax.axis_size("tensor")
    here = lax.axis_index("tensor")
    rising_sum = falling_sum = None
    for step in range(1, count):
        up_part = lax.dynamic_index_in_dim(
            parts, jnp.minimum(here + count - step, count - 1), 0, keepdims=False
        )
        down_part = lax.dynamic_index_in_dim(
            parts, jnp.maximum(here - count + step, 0), 0, keepdims=False
        )
        if rising_sum is not None:
            up_part = up_part + rising_sum.astype(jnp.float32)
            down_part = down_part + falling_sum.astype(jnp.float32)
        rising = [(i, i + 1) for i in range(step)]
        falling = [(i, i - 1) for i in range(count - step, count)]
        rising_sum = lax.ppermute(up_part.astype(jnp.bfloat16), "tensor", rising)
        falling_sum = lax.ppermute(down_part.astype(jnp.bfloat16), "tensor", falling)
    own = lax.dynamic_index_in_dim(parts, here, 0, keepdims=False)
    return own + rising_sum.astype(jnp.float32) + falling_sum.astype(jnp.float32)


def shifts(count):
    return [[(i, (i + k) % count) for i in range(count)] for k in range(1, count)]


def small_sum(values):
    total = values
    for pairs in shifts(lax.axis_size("tensor")):
        total = total + lax.ppermute(values, "tensor", pairs)
    return total


def rows_to_heads(values):
    count = lax.axis_size("tensor")
    here = lax.axis_index("tensor")
    rows, columns = values.shape
    width = columns // count
    got = [lax.dynamic_slice_in_dim(values, here * width, width, 1)]
    for k, pairs in enumerate(shifts(count), 1):
        block = lax.dynamic_slice_in_dim(values, lax.rem(here + k, count) * width, width, 1)
        got.append(lax.ppermute(block, "tensor", pairs))
    return [
        pick(here, [got[(i - owner) % count] for i in range(count)]) for owner in range(count)
    ]


def pair_swap(values, bit):
    count = lax.axis_size("dp")
    return lax.ppermute(values, "dp", [(i, i ^ bit) for i in range(count)])


def grad_body(order_ref, *refs):
    if len(refs) == 4:
        left_ref, right_ref, add_ref, out_ref = refs
    else:
        left_ref, right_ref, out_ref = refs
        add_ref = None
    product = lax.dot_general(
        left_ref[...], right_ref[...], ROW_CONTRACT, preferred_element_type=jnp.float32
    )
    if add_ref is not None:
        product = product + add_ref[...].astype(jnp.float32)
    out_ref[...] = product.astype(jnp.bfloat16)


def grad_blocks(order, left, right, add):
    blocks = order.shape[0]
    size = left.shape[1] // lax.axis_size("dp")
    depth, width = right.shape
    in_specs = [
        pl.BlockSpec((depth, size), lambda m, order_ref: (0, order_ref[m])),
        pl.BlockSpec((depth, width), lambda m, order_ref: (0, 0)),
    ]
    operands = [left, right]
    if add is not None:
        in_specs.append(pl.BlockSpec((size, width), lambda m, order_ref: (m, 0)))
        operands.append(add)
    return pl.pallas_call(
        grad_body,
        grid_spec=pltpu.PrefetchScalarGridSpec(
            num_scalar_prefetch=1,
            grid=(blocks,),
            in_specs=in_specs,
            out_specs=pl.BlockSpec((size, width), lambda m, order_ref: (m, 0)),
        ),
        out_shape=jax.ShapeDtypeStruct((blocks * size, width), jnp.bfloat16),
        compiler_params=pltpu.CompilerParams(vmem_limit_bytes=48 * MIB),
        cost_estimate=pl.CostEstimate(
            flops=2 * blocks * size * depth * width,
            bytes_accessed=2 * (depth * width + blocks * size * (depth + width)),
            transcendentals=0,
        ),
    )(order, *operands)


def owned_grad(left, right):
    count = lax.axis_size("dp")
    here = lax.axis_index("dp")
    size = left.shape[1] // count
    width = right.shape[1]
    if count & (count - 1) or count < 8 or size % 128 or width % 256:
        whole = lax.dot_general(left, right, ROW_CONTRACT, preferred_element_type=jnp.float32)
        return lax.psum_scatter(
            whole.astype(jnp.bfloat16), "dp", scatter_dimension=0, tiled=True
        ).astype(jnp.float32)
    evens = jnp.arange(0, count, 2, dtype=jnp.int32) ^ here
    sent = grad_blocks(evens ^ 1, left, right, None)
    kept = grad_blocks(evens, left, right, pair_swap(sent, 1))
    kept = kept.reshape((count // 2, size, width))
    bits = []
    bit = 2
    while bit < count:
        bits.append(bit)
        bit = bit * 2
    halves = []
    for way, columns in ((bits, slice(None, width // 2)), (bits[::-1], slice(width // 2, None))):
        live = {2 * b: kept[b, :, columns] for b in range(count // 2)}
        for place, bit in enumerate(way):
            going = [d for d in sorted(live) if d & bit]
            got = pair_swap(jnp.stack([live[d] for d in going]), bit)
            left_over = {}
            for at, d in enumerate(going):
                total = live[d ^ bit].astype(jnp.float32) + got[at].astype(jnp.float32)
                last = place == len(way) - 1
                left_over[d ^ bit] = total if last else total.astype(jnp.bfloat16)
            live = left_over
        halves.append(live[0])
    return jnp.concatenate(halves, axis=1)


def local(
    tokens,
    lengths,
    w_attn,
    w_mlp,
    norm_gains,
    moment_attn,
    square_attn,
    moment_mlp,
    square_mlp,
    moment_gains,
    square_gains,
    cotangent,
):
    rows_here, model_width = tokens.shape
    tensor_size = lax.axis_size("tensor")
    tensor_index = lax.axis_index("tensor")
    total_rows = rows_here * tensor_size
    seq_len = total_rows // lengths.shape[0]
    local_width = w_attn.shape[2]
    head_count = local_width // HDIM
    block_rows = min(512, seq_len)
    block_count = seq_len // block_rows
    score_scale = HDIM ** (-0.5)
    chunk_rows = rows_here // CHUNKS
    attn_low = w_attn.astype(jnp.bfloat16)
    mlp_low = w_mlp.astype(jnp.bfloat16)

    whole_tokens = jnp.concatenate(line_gather(tokens), axis=0)
    out_shard = jnp.concatenate(line_gather(attn_low[3]), axis=1)
    qkv_full = lax.all_gather(attn_low[:3], "dp", axis=1, tiled=True)
    out_full = lax.all_gather(out_shard, "dp", axis=0, tiled=True)
    gate_up_full = lax.all_gather(mlp_low[:2], "dp", axis=1, tiled=True)
    down_full = lax.all_gather(mlp_low[2], "dp", axis=0, tiled=True)
    gain_block = lax.all_gather(norm_gains.astype(jnp.bfloat16), "tensor", axis=1, tiled=True)
    gain_full = lax.all_gather(gain_block, "dp", axis=1, tiled=True)
    gain_values = gain_full.astype(jnp.float32)
    column_start = tensor_index * local_width
    query_gain = lax.dynamic_slice_in_dim(gain_values[2], column_start, local_width)
    key_gain = lax.dynamic_slice_in_dim(gain_values[3], column_start, local_width)
    positions = doc_positions(lengths, seq_len).reshape(total_rows)
    cos_table, sin_table = rope_tables(positions, HDIM)

    projected = jnp.einsum(
        "rd,kdf->krf", whole_tokens, qkv_full, preferred_element_type=jnp.float32
    )
    queries = projected[0]
    keys_raw = projected[1]
    value_low = projected[2].astype(jnp.bfloat16).reshape(total_rows, head_count, HDIM)
    square_sums = small_sum(
        jnp.stack([jnp.sum(queries * queries, axis=-1), jnp.sum(keys_raw * keys_raw, axis=-1)])
    )
    inverse = lax.rsqrt(square_sums / model_width + NORM_EPS)
    query_hat = queries * inverse[0][:, None]
    key_hat = keys_raw * inverse[1][:, None]
    query_norm = (query_hat * query_gain).reshape(total_rows, head_count, HDIM)
    key_norm = (key_hat * key_gain).reshape(total_rows, head_count, HDIM)
    query_low = rotate(query_norm, cos_table, sin_table).astype(jnp.bfloat16)
    key_low = rotate(key_norm, cos_table, sin_table).astype(jnp.bfloat16)
    outputs = []
    log_sums = []
    for block_index in range(block_count):
        start_row = block_index * block_rows
        stop_row = start_row + block_rows
        scores = masked_scores(
            query_low[start_row:stop_row], key_low[:stop_row], start_row, score_scale
        )
        row_peak = jnp.max(scores, axis=-1, keepdims=True)
        exp_scores = jnp.exp(scores - row_peak)
        totals = jnp.sum(exp_scores, axis=-1, keepdims=True)
        probability = exp_scores / totals
        log_sums.append(row_peak + jnp.log(totals))
        outputs.append(
            jnp.einsum(
                "hqk,khd->qhd",
                probability.astype(jnp.bfloat16),
                value_low[:stop_row],
                preferred_element_type=jnp.float32,
            )
        )
    mixed_low = (
        jnp.concatenate(outputs, axis=0).reshape(total_rows, local_width).astype(jnp.bfloat16)
    )

    def chunk_of(values, chunk):
        parted = values.reshape((tensor_size, CHUNKS, chunk_rows) + values.shape[1:])
        return parted[:, chunk].reshape((tensor_size * chunk_rows,) + values.shape[1:])

    def own_part(values):
        parted = values.reshape((tensor_size, chunk_rows) + values.shape[1:])
        return lax.dynamic_index_in_dim(parted, tensor_index, 0, keepdims=False)

    hidden_low, inner_low, act_pulls = [], [], []
    out_parts, back_raws_mlp, gains_mlp, attn_pulls, own_mixed = [], [], [], [], []
    for chunk in range(CHUNKS):
        mixed = jnp.concatenate(line_gather(chunk_of(mixed_low, chunk)), axis=1)
        own_mixed.append(own_part(mixed))
        raw_attn = lax.dot_general(
            mixed, out_full, COLUMN_CONTRACT, preferred_element_type=jnp.float32
        )
        hidden_low.append(
            (
                chunk_of(whole_tokens, chunk).astype(jnp.float32)
                + post_norm(raw_attn, gain_values[0])
            ).astype(jnp.bfloat16)
        )
        gate = jnp.dot(hidden_low[-1], gate_up_full[0], preferred_element_type=jnp.float32)
        upper = jnp.dot(hidden_low[-1], gate_up_full[1], preferred_element_type=jnp.float32)
        inner_rows, act_pull = jax.vjp(
            lambda gate_in, up_in: jax.nn.silu(gate_in) * up_in, gate, upper
        )
        act_pulls.append(act_pull)
        inner_low.append(inner_rows.astype(jnp.bfloat16))
        raw_part = lax.dot_general(
            inner_low[-1], down_full, COLUMN_CONTRACT, preferred_element_type=jnp.float32
        )
        raw_mlp = line_scatter(raw_part.reshape(tensor_size, chunk_rows, model_width))
        own_raw = own_part(raw_attn)
        own_rows = slice(chunk * chunk_rows, (chunk + 1) * chunk_rows)
        attn_normed, attn_pull = jax.vjp(post_norm, own_raw, gain_values[0])
        attn_pulls.append(attn_pull)
        mlp_normed, mlp_pull = jax.vjp(post_norm, raw_mlp, gain_values[1])
        hidden = tokens[own_rows].astype(jnp.float32) + attn_normed
        out_parts.append((hidden + mlp_normed).astype(jnp.bfloat16))
        back_raw, back_gain = mlp_pull(cotangent[own_rows].astype(jnp.float32))
        back_raws_mlp.append(back_raw.astype(jnp.bfloat16))
        gains_mlp.append(back_gain)
    out_tokens = jnp.concatenate(out_parts, axis=0)

    gathered_mlp, gate_low, upper_low = [], [], []
    back_hiddens, back_raws_attn, gains_attn, back_mixed_parts = [], [], [], []
    for chunk in range(CHUNKS):
        own_rows = slice(chunk * chunk_rows, (chunk + 1) * chunk_rows)
        gathered = jnp.concatenate(line_gather(back_raws_mlp[chunk]), axis=0)
        gathered_mlp.append(gathered)
        back_inner = jnp.dot(gathered, down_full, preferred_element_type=jnp.float32)
        back_gate, back_upper = act_pulls[chunk](back_inner)
        gate_low.append(back_gate.astype(jnp.bfloat16))
        upper_low.append(back_upper.astype(jnp.bfloat16))
        hidden_part = lax.dot_general(
            gate_low[-1], gate_up_full[0], COLUMN_CONTRACT, preferred_element_type=jnp.float32
        ) + lax.dot_general(
            upper_low[-1], gate_up_full[1], COLUMN_CONTRACT, preferred_element_type=jnp.float32
        )
        back_hidden = cotangent[own_rows].astype(jnp.float32) + line_scatter(
            hidden_part.reshape(tensor_size, chunk_rows, model_width)
        )
        back_hiddens.append(back_hidden)
        back_raw, back_gain = attn_pulls[chunk](back_hidden)
        gains_attn.append(back_gain)
        back_raws_attn.append(back_raw.astype(jnp.bfloat16))
        back_rows = jnp.dot(
            back_raws_attn[-1], out_full, preferred_element_type=jnp.float32
        ).astype(jnp.bfloat16)
        back_mixed_parts.append(rows_to_heads(back_rows))
    back_mixed = jnp.stack([jnp.stack(parts) for parts in back_mixed_parts], axis=1)
    back_mixed = back_mixed.reshape(total_rows, head_count, HDIM)
    gathered_all = jnp.concatenate(gathered_mlp, axis=0)
    hidden_all = jnp.concatenate(hidden_low, axis=0)
    down_owned = owned_grad(gathered_all, jnp.concatenate(inner_low, axis=0))
    gate_owned = owned_grad(hidden_all, jnp.concatenate(gate_low, axis=0))
    upper_owned = owned_grad(hidden_all, jnp.concatenate(upper_low, axis=0))
    output_owned = owned_grad(
        jnp.concatenate(back_raws_attn, axis=0), jnp.concatenate(own_mixed, axis=0)
    )
    output_owned = line_scatter(
        jnp.moveaxis(output_owned.reshape(-1, tensor_size, local_width), 1, 0)
    )

    query_grads = []
    key_total = jnp.zeros((seq_len, head_count, HDIM), jnp.float32)
    value_total = jnp.zeros((seq_len, head_count, HDIM), jnp.float32)
    for block_index in range(block_count):
        start_row = block_index * block_rows
        stop_row = start_row + block_rows
        scores = masked_scores(
            query_low[start_row:stop_row], key_low[:stop_row], start_row, score_scale
        )
        probability = jnp.exp(scores - log_sums[block_index])
        prob_low = probability.astype(jnp.bfloat16)
        grad_block = back_mixed[start_row:stop_row]
        back_prob = jnp.einsum(
            "qhd,khd->hqk", grad_block, value_low[:stop_row], preferred_element_type=jnp.float32
        )
        delta_rows = jnp.sum(probability * back_prob, axis=-1, keepdims=True)
        back_scores = (probability * (back_prob - delta_rows)).astype(jnp.bfloat16)
        query_grads.append(
            jnp.einsum(
                "hqk,khd->qhd", back_scores, key_low[:stop_row], preferred_element_type=jnp.float32
            )
            * score_scale
        )
        key_total = key_total.at[:stop_row].add(
            jnp.einsum(
                "hqk,qhd->khd",
                back_scores,
                query_low[start_row:stop_row],
                preferred_element_type=jnp.float32,
            )
            * score_scale
        )
        value_total = value_total.at[:stop_row].add(
            jnp.einsum("hqk,qhd->khd", prob_low, grad_block, preferred_element_type=jnp.float32)
        )
    back_query_rot = jnp.concatenate(query_grads, axis=0)
    value_back_low = value_total.reshape(total_rows, local_width).astype(jnp.bfloat16)
    _, rope_pull = jax.vjp(lambda rows_in: rotate(rows_in, cos_table, sin_table), query_norm)
    back_query_norm = rope_pull(back_query_rot)[0].reshape(total_rows, local_width)
    back_key_norm = rope_pull(key_total)[0].reshape(total_rows, local_width)
    back_query_hat = back_query_norm * query_gain
    back_key_hat = back_key_norm * key_gain
    grad_query_gain = jnp.sum(back_query_norm * query_hat, axis=0)
    grad_key_gain = jnp.sum(back_key_norm * key_hat, axis=0)
    cross_sums = small_sum(
        jnp.stack(
            [jnp.sum(back_query_hat * query_hat, axis=-1), jnp.sum(back_key_hat * key_hat, axis=-1)]
        )
    )
    query_back_low = (
        inverse[0][:, None] * (back_query_hat - query_hat * (cross_sums[0] / model_width)[:, None])
    ).astype(jnp.bfloat16)
    key_back_low = (
        inverse[1][:, None] * (back_key_hat - key_hat * (cross_sums[1] / model_width)[:, None])
    ).astype(jnp.bfloat16)
    stacked_back = jnp.stack([query_back_low, key_back_low, value_back_low])
    tokens_part = jnp.einsum(
        "krf,kdf->rd", stacked_back, qkv_full, preferred_element_type=jnp.float32
    )
    tokens_back = line_scatter(tokens_part.reshape(tensor_size, rows_here, model_width))
    qkv_owned = owned_grad(
        whole_tokens, jnp.concatenate([query_back_low, key_back_low, value_back_low], axis=1)
    )
    grad_tokens = (jnp.concatenate(back_hiddens, axis=0) + tokens_back).astype(jnp.bfloat16)

    gain_grad = jnp.zeros((4, model_width), jnp.float32)
    gain_grad = gain_grad.at[0].set(sum(gains_attn)).at[1].set(sum(gains_mlp))
    gain_grad = lax.dynamic_update_slice(
        gain_grad, jnp.stack([grad_query_gain, grad_key_gain]), (jnp.int32(2), column_start)
    )
    gain_owned = lax.psum_scatter(gain_grad, "dp", scatter_dimension=1, tiled=True)
    gain_final = lax.psum_scatter(gain_owned, "tensor", scatter_dimension=1, tiled=True)
    attn_owned = jnp.stack(
        [qkv_owned[:, k * local_width : (k + 1) * local_width] for k in range(3)] + [output_owned]
    )
    mlp_owned = jnp.stack([gate_owned, upper_owned, down_owned])
    new_attn, new_moment_attn, new_square_attn = adamw(
        w_attn, attn_owned, moment_attn, square_attn, RATE_MATRIX, DECAY_MATRIX
    )
    new_mlp, new_moment_mlp, new_square_mlp = adamw(
        w_mlp, mlp_owned, moment_mlp, square_mlp, RATE_MATRIX, DECAY_MATRIX
    )
    new_gains, new_moment_gains, new_square_gains = adamw(
        norm_gains, gain_final, moment_gains, square_gains, RATE_GAIN, 0.0
    )
    return (
        out_tokens,
        grad_tokens,
        new_attn,
        new_moment_attn,
        new_square_attn,
        new_mlp,
        new_moment_mlp,
        new_square_mlp,
        new_gains,
        new_moment_gains,
        new_square_gains,
    )


def solution(mesh):
    return jax.shard_map(
        local,
        mesh=mesh,
        in_specs=(
            P(("dp", "tensor"), None),
            P("dp", None),
            P(None, "dp", "tensor"),
            P(None, "dp", "tensor"),
            P(None, ("dp", "tensor")),
            P(None, "dp", "tensor"),
            P(None, "dp", "tensor"),
            P(None, "dp", "tensor"),
            P(None, "dp", "tensor"),
            P(None, ("dp", "tensor")),
            P(None, ("dp", "tensor")),
            P(("dp", "tensor"), None),
        ),
        out_specs=(
            P(("dp", "tensor"), None),
            P(("dp", "tensor"), None),
            P(None, "dp", "tensor"),
            P(None, "dp", "tensor"),
            P(None, "dp", "tensor"),
            P(None, "dp", "tensor"),
            P(None, "dp", "tensor"),
            P(None, "dp", "tensor"),
            P(None, ("dp", "tensor")),
            P(None, ("dp", "tensor")),
            P(None, ("dp", "tensor")),
        ),
        check_vma=False,
    )
```

```python
import jax
import jax.numpy as jnp
from jax import lax
from jax.experimental import pallas as pl
from jax.experimental.pallas import tpu as pltpu
from jax.sharding import PartitionSpec as P

HDIM = 128
STEP = 10
CHUNKS = 2
MIB = 1 << 20


NORM_EPS = 1e-06
ROPE_BASE = 500000.0
BETA_ONE = 0.9
BETA_TWO = 0.95
ADAM_EPS = 1e-08
RATE_MATRIX = 0.03
RATE_GAIN = 0.6
DECAY_MATRIX = 0.1
ROW_CONTRACT = (((0,), (0,)), ((), ()))
COLUMN_CONTRACT = (((1,), (1,)), ((), ()))


def doc_positions(lengths, seq_len):
    ends = jnp.cumsum(lengths, axis=-1, dtype=jnp.int32)
    starts = ends - lengths
    places = jnp.arange(seq_len, dtype=jnp.int32)
    inside = starts[:, None, :] <= places[None, :, None]
    begins = jnp.max(jnp.where(inside, starts[:, None, :], jnp.int32(0)), axis=-1)
    return places[None, :] - begins


def rope_tables(positions, head_dim):
    halfway = head_dim // 2
    powers = jnp.arange(halfway, dtype=jnp.float32) * (2.0 / head_dim)
    angles = positions.astype(jnp.float32)[:, None] * jnp.power(ROPE_BASE, -powers)
    return (jnp.cos(angles), jnp.sin(angles))


def post_norm(raw_rows, gain_row):
    return (
        raw_rows
        * lax.rsqrt(jnp.mean(raw_rows * raw_rows, axis=-1, keepdims=True) + NORM_EPS)
        * gain_row
    )


def adamw(weight, gradient, moment_one, moment_two, rate, decay):
    moment_one = BETA_ONE * moment_one + (1.0 - BETA_ONE) * gradient
    moment_two = BETA_TWO * moment_two + (1.0 - BETA_TWO) * gradient * gradient
    fix_one = 1.0 - BETA_ONE**STEP
    fix_two = 1.0 - BETA_TWO**STEP
    update = moment_one / fix_one / (jnp.sqrt(moment_two / fix_two) + ADAM_EPS)
    return (weight * (1.0 - rate * decay) - rate * update, moment_one, moment_two)


def pick(index, cases):
    if all(case is cases[0] for case in cases):
        return cases[0]
    return lax.select_n(index, *cases)


def after(values, *waits):
    return lax.optimization_barrier((values, waits))[0]


def chunk_scatter(part):
    return lax.psum_scatter(
        part.astype(jnp.bfloat16), "tensor", scatter_dimension=0, tiled=True
    ).astype(jnp.float32)


def line_hop(step, up, down):
    count = lax.axis_size("tensor")
    rising = [(i, i + 1) for i in range(step - 1, count - 1)]
    falling = [(i + 1, i) for i in range(count - step)]
    return lax.ppermute(up, "tensor", rising), lax.ppermute(down, "tensor", falling)


def line_pieces(piece, hops):
    count = lax.axis_size("tensor")
    here = lax.axis_index("tensor")
    low = [piece] + [hop[0] for hop in hops]
    high = [piece] + [hop[1] for hop in hops]
    return [
        pick(here, [low[i - owner] if i >= owner else high[owner - i] for i in range(count)])
        for owner in range(count)
    ]


def line_gather(piece, work=None):
    hops, given = [], ()
    pair = (piece, piece)
    for step in range(1, lax.axis_size("tensor")):
        pair = line_hop(step, *pair)
        if work is not None and step - 1 < len(work):
            given = work[step - 1](given)
            pair, given = lax.optimization_barrier((pair, given))
        hops.append(pair)
    pieces = line_pieces(piece, hops)
    return pieces if work is None else (pieces, given)


def shift_gather(piece):
    count = lax.axis_size("tensor")
    here = lax.axis_index("tensor")
    got = [piece] + [lax.ppermute(piece, "tensor", pairs) for pairs in shifts(count)]
    return [
        pick(here, [got[(i - owner) % count] for i in range(count)]) for owner in range(count)
    ]


def line_scatter(parts):
    count = lax.axis_size("tensor")
    here = lax.axis_index("tensor")
    rising_sum = falling_sum = None
    for step in range(1, count):
        up_part = lax.dynamic_index_in_dim(
            parts, jnp.minimum(here + count - step, count - 1), 0, keepdims=False
        )
        down_part = lax.dynamic_index_in_dim(
            parts, jnp.maximum(here - count + step, 0), 0, keepdims=False
        )
        if rising_sum is not None:
            up_part = up_part + rising_sum.astype(jnp.float32)
            down_part = down_part + falling_sum.astype(jnp.float32)
        rising = [(i, i + 1) for i in range(step)]
        falling = [(i, i - 1) for i in range(count - step, count)]
        rising_sum = lax.ppermute(up_part.astype(jnp.bfloat16), "tensor", rising)
        falling_sum = lax.ppermute(down_part.astype(jnp.bfloat16), "tensor", falling)
    own = lax.dynamic_index_in_dim(parts, here, 0, keepdims=False)
    return own + rising_sum.astype(jnp.float32) + falling_sum.astype(jnp.float32)


def shift_scatter(values, width):
    count = lax.axis_size("tensor")
    here = lax.axis_index("tensor")
    total = lax.dynamic_slice_in_dim(values, here * width, width, 1)
    for k, pairs in enumerate(shifts(count), 1):
        part = lax.dynamic_slice_in_dim(values, lax.rem(here + k, count) * width, width, 1)
        got = lax.ppermute(part.astype(jnp.bfloat16), "tensor", pairs)
        total = total + got.astype(jnp.float32)
    return total


def shifts(count):
    return [[(i, (i + k) % count) for i in range(count)] for k in range(1, count)]


def small_sum(values):
    total = values
    for pairs in shifts(lax.axis_size("tensor")):
        total = total + lax.ppermute(values, "tensor", pairs)
    return total


def rows_to_heads(values):
    count = lax.axis_size("tensor")
    here = lax.axis_index("tensor")
    rows, columns = values.shape
    width = columns // count
    got = [lax.dynamic_slice_in_dim(values, here * width, width, 1)]
    for k, pairs in enumerate(shifts(count), 1):
        block = lax.dynamic_slice_in_dim(values, lax.rem(here + k, count) * width, width, 1)
        got.append(lax.ppermute(block, "tensor", pairs))
    return [
        pick(here, [got[(i - owner) % count] for i in range(count)]) for owner in range(count)
    ]


def pair_swap(values, bit):
    count = lax.axis_size("dp")
    return lax.ppermute(values, "dp", [(i, i ^ bit) for i in range(count)])


def gather_gains(gains):
    tensor_count, count = lax.axis_size("tensor"), lax.axis_size("dp")
    here = lax.axis_index("tensor")
    got = [gains] + [lax.ppermute(gains, "tensor", pairs) for pairs in shifts(tensor_count)]
    block = jnp.concatenate(
        [pick(here, [got[(i - owner) % tensor_count] for i in range(tensor_count)])
         for owner in range(tensor_count)],
        axis=1,
    )
    if count & (count - 1):
        return lax.all_gather(block, "dp", axis=1, tiled=True)
    whole = block[None]
    bit = 1
    while bit < count:
        whole = jnp.concatenate([whole, pair_swap(whole, bit)], axis=0)
        bit = bit * 2
    order = jnp.arange(count, dtype=jnp.int32) ^ lax.axis_index("dp")
    return jnp.moveaxis(whole[order], 0, 1).reshape(gains.shape[0], -1)


def scatter_gains(grads):
    count, tensor_count = lax.axis_size("dp"), lax.axis_size("tensor")
    here = lax.axis_index("tensor")
    if count & (count - 1):
        block = lax.psum_scatter(grads, "dp", scatter_dimension=1, tiled=True)
    else:
        order = jnp.arange(count, dtype=jnp.int32) ^ lax.axis_index("dp")
        live = jnp.moveaxis(grads.reshape(grads.shape[0], count, -1), 1, 0)[order]
        bit = count // 2
        while bit:
            live = live[:bit] + pair_swap(live[bit:], bit)
            bit = bit // 2
        block = live[0]
    parts = jnp.moveaxis(block.reshape(block.shape[0], tensor_count, -1), 1, 0)
    total = lax.dynamic_index_in_dim(parts, here, 0, keepdims=False)
    for k, pairs in enumerate(shifts(tensor_count), 1):
        part = lax.dynamic_index_in_dim(
            parts, lax.rem(here + k, tensor_count), 0, keepdims=False
        )
        total = total + lax.ppermute(part, "tensor", pairs)
    return total


def kernel(body, grid, in_specs, out_specs, out_shape, operands, scratch=(), order=None):
    spec = pltpu.PrefetchScalarGridSpec(
        num_scalar_prefetch=0 if order is None else 1,
        grid=grid,
        in_specs=in_specs,
        out_specs=out_specs,
        scratch_shapes=scratch,
    )
    return pl.pallas_call(
        body,
        grid_spec=spec,
        out_shape=out_shape,
        compiler_params=pltpu.CompilerParams(vmem_limit_bytes=52 * MIB),
        cost_estimate=pl.CostEstimate(flops=1, bytes_accessed=1, transcendentals=0),
    )(*(() if order is None else (order,)), *operands)


def place_body(order_ref, *refs):
    step = pl.program_id(0)
    out_ref = refs[-1]
    half = out_ref.shape[1] // 2
    for side in range(2):
        own, from_x, from_y, low, high = refs[5 * side : 5 * side + 5]
        for at, piece in enumerate((own, from_x, from_y)):

            @pl.when(step == 4 * side + at)
            def _():
                out_ref[0] = piece[...]

        @pl.when(step == 4 * side + 3)
        def _():
            out_ref[0, :half] = low[...]
            out_ref[0, half:] = high[...]


def plane_one(shard):
    count = lax.axis_size("dp")
    if count != 8 or shard.shape[0] % 32:
        return (lax.all_gather(shard, "dp", axis=0, tiled=True),)
    return shard, pair_swap(shard, 2), pair_swap(shard, 4)


def plane_two(given):
    if len(given) == 1:
        return given
    shard, from_x, from_y = given
    half = shard.shape[0] // 2
    return (*given, pair_swap(from_x[:half], 4), pair_swap(from_y[half:], 2))


def plane_three(near):
    if len(near) == 1:
        return near[0]
    rows, width = near[0].shape
    far = [pair_swap(piece, 1) for piece in near]
    order = jnp.array([0, 2, 4, 6, 1, 3, 5, 7], jnp.int32) ^ lax.axis_index("dp")
    whole = kernel(
        place_body,
        (8,),
        [whole_block(piece.shape) for piece in (*near, *far)],
        pl.BlockSpec((1, rows, width), lambda step, order_ref: (order_ref[step], 0, 0)),
        jax.ShapeDtypeStruct((8, rows, width), near[0].dtype),
        (*near, *far),
        order=order,
    )
    return whole.reshape(8 * rows, width)


def whole_block(shape):
    return pl.BlockSpec(shape, lambda *at: (0,) * len(shape))


def out_norm_body(mixed_ref, weight_ref, tokens_ref, gain_ref, hidden_ref, raw_ref, all_ref):
    step = pl.program_id(0)
    tile = weight_ref.shape[0]
    product = lax.dot_general(
        mixed_ref[...].reshape(hidden_ref.shape),
        weight_ref[...],
        COLUMN_CONTRACT,
        preferred_element_type=jnp.float32,
    )
    raw_ref[...] = product
    all_ref[step] = product

    @pl.when(step == pl.num_programs(0) - 1)
    def _():
        rows, width = hidden_ref.shape
        square = jnp.zeros((rows, 1), jnp.float32)
        for at in range(width // tile):
            square = square + jnp.sum(all_ref[at] * all_ref[at], axis=-1, keepdims=True)
        scale = lax.rsqrt(square / width + NORM_EPS)
        for at in range(width // tile):
            columns = slice(at * tile, (at + 1) * tile)
            place = tokens_ref[:, 0, :, columns].reshape(rows, tile).astype(jnp.float32)
            hidden_ref[:, columns] = (
                place + all_ref[at] * scale * gain_ref[:, columns]
            ).astype(jnp.bfloat16)


def out_norm(mixed, weight, tokens, chunk, gain):
    pieces, _, piece_rows, width = tokens.shape
    rows = pieces * piece_rows
    tile = min(512, width)
    part = pl.BlockSpec((pieces, 1, piece_rows, width), lambda n: (0, chunk, 0, 0))
    return kernel(
        out_norm_body,
        (width // tile,),
        [
            part,
            pl.BlockSpec((tile, width), lambda n: (n, 0)),
            part,
            whole_block((1, width)),
        ],
        [whole_block((rows, width)), pl.BlockSpec((rows, tile), lambda n: (0, n))],
        [
            jax.ShapeDtypeStruct((rows, width), jnp.bfloat16),
            jax.ShapeDtypeStruct((rows, width), jnp.float32),
        ],
        (mixed, weight, tokens, gain),
        [pltpu.VMEM((width // tile, rows, tile), jnp.float32)],
    )


def mlp_in_body(hidden_ref, weight_ref, inner_ref, gate_ref, upper_ref):
    gate = jnp.dot(hidden_ref[...], weight_ref[0], preferred_element_type=jnp.float32)
    upper = jnp.dot(hidden_ref[...], weight_ref[1], preferred_element_type=jnp.float32)
    gate_ref[...] = gate
    upper_ref[...] = upper
    inner_ref[...] = (gate * jax.nn.sigmoid(gate) * upper).astype(jnp.bfloat16)


def mlp_in(hidden, weights):
    rows, depth = hidden.shape
    width = weights.shape[2]
    tile = min(512, width)
    out_spec = pl.BlockSpec((rows, tile), lambda n: (0, n))
    return kernel(
        mlp_in_body,
        (width // tile,),
        [whole_block((rows, depth)), pl.BlockSpec((2, depth, tile), lambda n: (0, 0, n))],
        [out_spec] * 3,
        [
            jax.ShapeDtypeStruct((rows, width), kind)
            for kind in (jnp.bfloat16, jnp.float32, jnp.float32)
        ],
        (hidden, weights),
    )


def mlp_out_body(inner_ref, weight_ref, out_ref):
    out_ref[...] = lax.dot_general(
        inner_ref[...], weight_ref[...], COLUMN_CONTRACT, preferred_element_type=jnp.float32
    ).astype(jnp.bfloat16)


def mlp_out(inner, weight):
    rows, depth = inner.shape
    width = weight.shape[-2]
    tile = min(512, width)
    if weight.ndim == 3:
        weight_spec = pl.BlockSpec((None, tile, depth), lambda n: (2, n, 0))
    else:
        weight_spec = pl.BlockSpec((tile, depth), lambda n: (n, 0))
    return kernel(
        mlp_out_body,
        (width // tile,),
        [whole_block((rows, depth)), weight_spec],
        pl.BlockSpec((rows, tile), lambda n: (0, n)),
        jax.ShapeDtypeStruct((rows, width), jnp.bfloat16),
        (inner, weight),
    )


def mlp_back_body(back_ref, weight_ref, gate_ref, upper_ref, back_gate_ref, back_upper_ref):
    back = jnp.dot(back_ref[...], weight_ref[...], preferred_element_type=jnp.float32)
    gate = gate_ref[...]
    share = jax.nn.sigmoid(gate)
    slope = share * (1.0 + gate * (1.0 - share))
    back_gate_ref[...] = (back * upper_ref[...] * slope).astype(jnp.bfloat16)
    back_upper_ref[...] = (back * (gate * share)).astype(jnp.bfloat16)


def mlp_back(back, weight, gate, upper):
    rows, depth = back.shape
    width = weight.shape[2]
    tile = min(512, width)
    spec = pl.BlockSpec((rows, tile), lambda n: (0, n))
    return kernel(
        mlp_back_body,
        (width // tile,),
        [
            whole_block((rows, depth)),
            pl.BlockSpec((None, depth, tile), lambda n: (2, 0, n)),
            spec,
            spec,
        ],
        [spec] * 2,
        [jax.ShapeDtypeStruct((rows, width), jnp.bfloat16)] * 2,
        (back, weight, gate, upper),
    )


def hidden_back_body(gate_ref, upper_ref, weight_ref, out_ref):
    out_ref[...] = (
        lax.dot_general(
            gate_ref[...], weight_ref[0], COLUMN_CONTRACT, preferred_element_type=jnp.float32
        )
        + lax.dot_general(
            upper_ref[...], weight_ref[1], COLUMN_CONTRACT, preferred_element_type=jnp.float32
        )
    ).astype(jnp.bfloat16)


def hidden_back(back_gate, back_upper, weights):
    rows, depth = back_gate.shape
    width = weights.shape[1]
    tile = min(512, width)
    return kernel(
        hidden_back_body,
        (width // tile,),
        [
            whole_block((rows, depth)),
            whole_block((rows, depth)),
            pl.BlockSpec((2, tile, depth), lambda n: (0, n, 0)),
        ],
        pl.BlockSpec((rows, tile), lambda n: (0, n)),
        jax.ShapeDtypeStruct((rows, width), jnp.bfloat16),
        (back_gate, back_upper, weights),
    )


def project_body(tokens_ref, weight_ref, out_ref, sums_ref):
    step = pl.program_id(0)
    product = jnp.dot(tokens_ref[...], weight_ref[...], preferred_element_type=jnp.float32)
    out_ref[...] = product
    sums = jnp.sum(product * product, axis=-1, keepdims=True)
    lanes = lax.broadcasted_iota(jnp.int32, sums_ref.shape, 1)

    @pl.when(step == 0)
    def _():
        sums_ref[...] = jnp.where(lanes == 0, sums, 0.0)

    @pl.when(step == 1)
    def _():
        sums_ref[...] = jnp.where(lanes == 1, sums, sums_ref[...])


def project(tokens, weight):
    rows, depth = tokens.shape
    width = weight.shape[1]
    return kernel(
        project_body,
        (3,),
        [whole_block((rows, depth)), pl.BlockSpec((depth, width // 3), lambda n: (0, n))],
        [pl.BlockSpec((rows, width // 3), lambda n: (0, n)), whole_block((rows, HDIM))],
        [
            jax.ShapeDtypeStruct((rows, width), jnp.float32),
            jax.ShapeDtypeStruct((rows, HDIM), jnp.float32),
        ],
        (tokens, weight),
    )


def turned(values, cosine, sine):
    return values * cosine + pltpu.roll(values, HDIM // 2, 1) * sine


def softmax_rows(query, key, start):
    scores = lax.dot_general(query, key, COLUMN_CONTRACT, preferred_element_type=jnp.float32)
    scores = scores * HDIM ** (-0.5)
    rows = start + lax.broadcasted_iota(jnp.int32, scores.shape, 0)
    columns = lax.broadcasted_iota(jnp.int32, scores.shape, 1)
    scores = jnp.where(columns <= rows, scores, -jnp.inf)
    weights = jnp.exp(scores - jnp.max(scores, axis=-1, keepdims=True))
    return weights / jnp.sum(weights, axis=-1, keepdims=True)


def attend_body(
    query_ref, key_ref, value_ref, scale_ref, gain_ref, cos_ref, sin_ref, low_ref, out_ref
):
    cosine, sine = cos_ref[...], sin_ref[...]
    for at, source in enumerate((query_ref, key_ref)):
        normed = source[...] * scale_ref[:, at : at + 1] * gain_ref[at : at + 1, :]
        low_ref[at] = turned(normed, cosine, sine).astype(jnp.bfloat16)
    low_ref[2] = value_ref[...].astype(jnp.bfloat16)
    rows = out_ref.shape[0]
    block = min(256, rows)
    for start in range(0, rows, block):
        stop = start + block
        share = softmax_rows(low_ref[0, start:stop], low_ref[1, :stop], start)
        out_ref[start:stop] = jnp.dot(
            share.astype(jnp.bfloat16), low_ref[2, :stop], preferred_element_type=jnp.float32
        ).astype(jnp.bfloat16)


def head_specs(rows, heads):
    return [
        pl.BlockSpec((rows, HDIM), lambda h, part=part: (0, part * heads + h)) for part in range(3)
    ]


def attend(projected, scale, gains, cosine, sine):
    rows, width = projected.shape
    heads = width // (3 * HDIM)
    return kernel(
        attend_body,
        (heads,),
        head_specs(rows, heads)
        + [
            whole_block((rows, HDIM)),
            pl.BlockSpec((2, HDIM), lambda h: (0, h)),
            whole_block((rows, HDIM)),
            whole_block((rows, HDIM)),
        ],
        [
            pl.BlockSpec((3, rows, HDIM), lambda h: (0, 0, h)),
            pl.BlockSpec((rows, HDIM), lambda h: (0, h)),
        ],
        [
            jax.ShapeDtypeStruct((3, rows, width // 3), jnp.bfloat16),
            jax.ShapeDtypeStruct((rows, width // 3), jnp.bfloat16),
        ],
        (projected, projected, projected, scale, gains, cosine, sine),
    )


def attend_back_body(
    low_ref,
    back_ref,
    query_ref,
    key_ref,
    scale_ref,
    gain_ref,
    cos_ref,
    sin_ref,
    hats_ref,
    value_out_ref,
    cross_ref,
    gain_out_ref,
    query_sum,
    key_sum,
    value_sum,
):
    rows = value_out_ref.shape[0]
    block = min(256, rows)
    for start in reversed(range(0, rows, block)):
        stop = start + block
        query, key, value = low_ref[0, start:stop], low_ref[1, :stop], low_ref[2, :stop]
        back = back_ref[start:stop]
        share = softmax_rows(query, key, start)
        back_share = lax.dot_general(
            back, value, COLUMN_CONTRACT, preferred_element_type=jnp.float32
        )
        mean = jnp.sum(share * back_share, axis=-1, keepdims=True)
        back_scores = (share * (back_share - mean)).astype(jnp.bfloat16)
        value_part = lax.dot_general(
            share.astype(jnp.bfloat16), back, ROW_CONTRACT, preferred_element_type=jnp.float32
        )
        key_part = lax.dot_general(
            back_scores, query, ROW_CONTRACT, preferred_element_type=jnp.float32
        )
        query_sum[start:stop] = jnp.dot(back_scores, key, preferred_element_type=jnp.float32)
        if stop == rows:
            value_sum[...] = value_part
            key_sum[...] = key_part
        else:
            value_sum[:stop] += value_part
            key_sum[:stop] += key_part
    value_out_ref[...] = value_sum[...].astype(jnp.bfloat16)
    cosine, sine = cos_ref[...], sin_ref[...]
    lanes = lax.broadcasted_iota(jnp.int32, cross_ref.shape, 1)
    cross = jnp.zeros(cross_ref.shape, jnp.float32)
    for at, (source, total) in enumerate(((query_ref, query_sum), (key_ref, key_sum))):
        normed = turned(total[...] * HDIM ** (-0.5), cosine, -sine)
        hat = source[...] * scale_ref[:, at : at + 1]
        gain_out_ref[at : at + 1] = jnp.sum(normed * hat, axis=0, keepdims=True)
        back_hat = normed * gain_ref[at : at + 1, :]
        hats_ref[at] = back_hat
        cross = jnp.where(lanes == at, jnp.sum(back_hat * hat, axis=-1, keepdims=True), cross)

    @pl.when(pl.program_id(0) == 0)
    def _():
        cross_ref[...] = cross

    @pl.when(pl.program_id(0) > 0)
    def _():
        cross_ref[...] += cross


def attend_back(low, back, projected, scale, gains, cosine, sine):
    rows, width = back.shape
    heads = width // HDIM
    head = pl.BlockSpec((rows, HDIM), lambda h: (0, h))
    return kernel(
        attend_back_body,
        (heads,),
        [pl.BlockSpec((3, rows, HDIM), lambda h: (0, 0, h)), head]
        + head_specs(rows, heads)[:2]
        + [
            whole_block((rows, HDIM)),
            pl.BlockSpec((2, HDIM), lambda h: (0, h)),
            whole_block((rows, HDIM)),
            whole_block((rows, HDIM)),
        ],
        [
            pl.BlockSpec((2, rows, HDIM), lambda h: (0, 0, h)),
            head,
            whole_block((rows, HDIM)),
            pl.BlockSpec((2, HDIM), lambda h: (0, h)),
        ],
        [
            jax.ShapeDtypeStruct((2, rows, width), jnp.float32),
            jax.ShapeDtypeStruct((rows, width), jnp.bfloat16),
            jax.ShapeDtypeStruct((rows, HDIM), jnp.float32),
            jax.ShapeDtypeStruct((2, width), jnp.float32),
        ],
        (low, back, projected, projected, scale, gains, cosine, sine),
        [pltpu.VMEM((rows, HDIM), jnp.float32)] * 3,
    )


def tokens_back_body(
    hats_ref, query_ref, key_ref, value_ref, scale_ref, mean_ref, weight_ref, back_ref, out_ref
):
    width = value_ref.shape[1]

    @pl.when(pl.program_id(0) == 0)
    def _():
        for at, source in enumerate((query_ref, key_ref)):
            scale = scale_ref[:, at : at + 1]
            hat = source[...] * scale
            back_ref[:, at * width : (at + 1) * width] = (
                scale * (hats_ref[at] - hat * mean_ref[:, at : at + 1])
            ).astype(jnp.bfloat16)
        back_ref[:, 2 * width :] = value_ref[...]

    out_ref[...] = lax.dot_general(
        back_ref[...], weight_ref[...], COLUMN_CONTRACT, preferred_element_type=jnp.float32
    ).astype(jnp.bfloat16)


def tokens_back_part(hats, projected, value_back, scale, mean, weight):
    rows, width = value_back.shape
    model_width = weight.shape[0]
    tile = min(512, model_width)
    return kernel(
        tokens_back_body,
        (model_width // tile,),
        [
            whole_block((2, rows, width)),
            pl.BlockSpec((rows, width), lambda n: (0, 0)),
            pl.BlockSpec((rows, width), lambda n: (0, 1)),
            whole_block((rows, width)),
            whole_block((rows, HDIM)),
            whole_block((rows, HDIM)),
            pl.BlockSpec((tile, 3 * width), lambda n: (n, 0)),
        ],
        [
            whole_block((rows, 3 * width)),
            pl.BlockSpec((rows, tile), lambda n: (0, n)),
        ],
        [
            jax.ShapeDtypeStruct((rows, 3 * width), jnp.bfloat16),
            jax.ShapeDtypeStruct((rows, model_width), jnp.bfloat16),
        ],
        (hats, projected, projected, value_back, scale, mean, weight),
    )


def product_of(left_refs, right_refs):
    total = None
    for left_ref, right_ref in zip(left_refs, right_refs):
        product = lax.dot_general(
            left_ref[...], right_ref[...], ROW_CONTRACT, preferred_element_type=jnp.float32
        )
        total = product if total is None else total + product
    return total


def sent_body(order_ref, *refs):
    parts = len(refs) // 2
    refs[-1][...] = product_of(refs[:parts], refs[parts:-1]).astype(jnp.bfloat16)


def kept_body(order_ref, *refs):
    parts = (len(refs) - 5) // 2
    got_ref = refs[2 * parts]
    x_send, y_send, x_keep, y_keep = refs[2 * parts + 1 :]
    step = pl.program_id(0)
    total = product_of(refs[:parts], refs[parts : 2 * parts]) + got_ref[...].astype(jnp.float32)
    total = total.astype(jnp.bfloat16)
    half = total.shape[1] // 2
    left, right = total[:, :half], total[:, half:]

    @pl.when(step < 2)
    def _():
        x_send[0] = left

    @pl.when((step == 1) | (step == 2))
    def _():
        y_send[0] = right

    @pl.when(step >= 2)
    def _():
        x_keep[0] = left

    @pl.when((step == 0) | (step == 3))
    def _():
        y_keep[0] = right


def quick(lefts, rights):
    count = lax.axis_size("dp")
    size = lefts[0].shape[1] // count
    return count == 8 and size % 128 == 0 and rights[0].shape[1] % 256 == 0


def grad_specs(lefts, rights, size):
    return [
        pl.BlockSpec((left.shape[0], size), lambda m, order_ref: (0, order_ref[m]))
        for left in lefts
    ] + [pl.BlockSpec(right.shape, lambda m, order_ref: (0, 0)) for right in rights]


def grad_sent(lefts, rights):
    if not quick(lefts, rights):
        return jnp.zeros((16, 128), jnp.bfloat16)
    size = lefts[0].shape[1] // 8
    width = rights[0].shape[1]
    order = jnp.array([3, 7, 5, 1], jnp.int32) ^ lax.axis_index("dp")
    return kernel(
        sent_body,
        (4,),
        grad_specs(lefts, rights, size),
        pl.BlockSpec((size, width), lambda m, order_ref: (m, 0)),
        jax.ShapeDtypeStruct((4 * size, width), jnp.bfloat16),
        (*lefts, *rights),
        order=order,
    )


def grad_kept(lefts, rights, got):
    if not quick(lefts, rights):
        return [
            sum(
                lax.dot_general(left, right, ROW_CONTRACT, preferred_element_type=jnp.float32)
                for left, right in zip(lefts, rights)
            )
        ]
    size = lefts[0].shape[1] // 8
    width = rights[0].shape[1]
    order = jnp.array([2, 6, 4, 0], jnp.int32) ^ lax.axis_index("dp")
    block = (1, size, width // 2)
    return kernel(
        kept_body,
        (4,),
        grad_specs(lefts, rights, size)
        + [pl.BlockSpec((size, width), lambda m, order_ref: (m, 0))],
        [
            pl.BlockSpec(block, lambda m, order_ref: (jnp.minimum(m, 1), 0, 0)),
            pl.BlockSpec(block, lambda m, order_ref: (m // 2, 0, 0)),
            pl.BlockSpec(block, lambda m, order_ref: (m // 3, 0, 0)),
            pl.BlockSpec(block, lambda m, order_ref: (m // 3, 0, 0)),
        ],
        [jax.ShapeDtypeStruct((2, size, width // 2), jnp.bfloat16)] * 4,
        (*lefts, *rights, got),
        order=order,
    )


def exchange_one(kept):
    if len(kept) == 1:
        return kept
    return [pair_swap(kept[0], 2), pair_swap(kept[1], 4)]


def wide(values):
    return values.astype(jnp.float32)


def exchange_two(kept, first):
    if len(kept) == 1:
        return kept
    x_next = wide(kept[2][0]) + wide(first[0][1])
    y_next = wide(kept[3][0]) + wide(first[1][0])
    return [
        wide(kept[2][1]) + wide(first[0][0]),
        wide(kept[3][1]) + wide(first[1][1]),
        pair_swap(x_next.astype(jnp.bfloat16), 4),
        pair_swap(y_next.astype(jnp.bfloat16), 2),
    ]


def exchange_end(second):
    if len(second) == 1:
        return lax.psum_scatter(
            second[0].astype(jnp.bfloat16), "dp", scatter_dimension=0, tiled=True
        ).astype(jnp.float32)
    return jnp.concatenate(
        [second[half] + second[2 + half].astype(jnp.float32) for half in range(2)], axis=1
    )


def local(
    tokens,
    lengths,
    w_attn,
    w_mlp,
    norm_gains,
    moment_attn,
    square_attn,
    moment_mlp,
    square_mlp,
    moment_gains,
    square_gains,
    cotangent,
):
    rows_here, model_width = tokens.shape
    tensor_size = lax.axis_size("tensor")
    tensor_index = lax.axis_index("tensor")
    total_rows = rows_here * tensor_size
    seq_len = total_rows // lengths.shape[0]
    local_width = w_attn.shape[2]
    chunk_rows = rows_here // CHUNKS

    qkv_shard = jnp.concatenate([w_attn[k].astype(jnp.bfloat16) for k in range(3)], axis=1)
    mlp_low = w_mlp.astype(jnp.bfloat16)
    positions = doc_positions(lengths, seq_len).reshape(total_rows)

    def second_hop(given):
        mlp_shard = after(mlp_low, given)
        return plane_two(given), lax.all_gather(mlp_shard, "dp", axis=1, tiled=True), mlp_shard

    def third_hop(given):
        cos_table, sin_table = rope_tables(positions, HDIM)
        cosine = jnp.concatenate([cos_table, cos_table], axis=1)
        sine = jnp.concatenate([-sin_table, sin_table], axis=1)
        gains = gather_gains(after(norm_gains.astype(jnp.bfloat16), given))
        return plane_three(given), cosine, sine, gains

    hop, near = lax.optimization_barrier((line_hop(1, tokens, tokens), plane_one(qkv_shard)))
    hops = [hop]
    near, mlp_full, mlp_shard = second_hop(near)
    hop, near, mlp_shard = lax.optimization_barrier((line_hop(2, *hop), near, mlp_shard))
    hops.append(hop)
    hop, given = lax.optimization_barrier((line_hop(3, *hop), third_hop(near)))
    hops.append(hop)
    qkv_full, cosine, sine, gain_full = given
    whole_tokens = jnp.concatenate(line_pieces(tokens, hops), axis=0)
    gain_values = gain_full.astype(jnp.float32)
    column_start = tensor_index * local_width
    head_gains = lax.dynamic_slice_in_dim(gain_values[2:], column_start, local_width, 1)

    def summed_lanes(lanes):
        rows = lanes.shape[0]
        flat = lax.optimization_barrier(lanes[:, :2].T.reshape(-1, HDIM))
        return small_sum(flat).reshape(2, rows)

    def in_lanes(values):
        return jnp.pad(values.T, ((0, 0), (0, HDIM - 2)))

    projected, square_lanes = project(whole_tokens, qkv_full)
    inverse = lax.rsqrt(summed_lanes(square_lanes) / model_width + NORM_EPS)
    inverse_lanes = in_lanes(inverse)
    out_piece = after(w_attn[3].astype(jnp.bfloat16), inverse_lanes)
    out_shard = jnp.concatenate(shift_gather(out_piece), axis=1)
    low_heads, mixed_low = attend(projected, inverse_lanes, head_gains, cosine, sine)
    out_shard, mixed_low = lax.optimization_barrier((out_shard, mixed_low))
    pieces, out_full = line_gather(
        mixed_low, (lambda _: plane_one(out_shard), plane_two, plane_three)
    )
    whole_mixed = jnp.concatenate(pieces, axis=1)
    mixed_parted = whole_mixed.reshape(tensor_size, CHUNKS, chunk_rows, model_width)
    tokens_parted = whole_tokens.reshape(tensor_size, CHUNKS, chunk_rows, model_width)

    def own_part(values):
        parted = values.reshape((tensor_size, chunk_rows) + values.shape[1:])
        return lax.dynamic_index_in_dim(parted, tensor_index, 0, keepdims=False)

    def own_rows(values, chunk):
        return values[chunk * chunk_rows : (chunk + 1) * chunk_rows].astype(jnp.float32)

    chunks = range(CHUNKS)
    raw_attn, hidden_low, gate = ([None] * CHUNKS for _ in range(3))
    upper, inner_low, down_part, raw_mlp = ([None] * CHUNKS for _ in range(4))
    for chunk in chunks:
        mixed = mixed_parted
        if chunk:
            mixed = after(mixed, down_part[chunk - 1])
        hidden_low[chunk], raw_attn[chunk] = out_norm(
            mixed, out_full, tokens_parted, chunk, gain_values[:1]
        )
        inner_low[chunk], gate[chunk], upper[chunk] = mlp_in(hidden_low[chunk], mlp_full)
        down_part[chunk] = mlp_out(inner_low[chunk], mlp_full)
        raw_mlp[chunk] = chunk_scatter(down_part[chunk])

    own_mixed = [
        lax.dynamic_index_in_dim(mixed_parted[:, chunk], tensor_index, 0, keepdims=False)
        for chunk in chunks
    ]
    out_parts, back_raw_mlp, gains_mlp, attn_pulls = ([None] * CHUNKS for _ in range(4))
    gathered, gate_low, upper_low, hidden_part, back_sum = ([None] * CHUNKS for _ in range(5))

    def turn(chunk, raw):
        attn_normed, attn_pulls[chunk] = jax.vjp(
            post_norm, own_part(raw_attn[chunk]), gain_values[0]
        )
        mlp_normed, mlp_pull = jax.vjp(post_norm, raw, gain_values[1])
        hidden = own_rows(tokens, chunk) + attn_normed
        out_parts[chunk] = (hidden + mlp_normed).astype(jnp.bfloat16)
        back_raw, gains_mlp[chunk] = mlp_pull(own_rows(cotangent, chunk))
        back_raw_mlp[chunk] = back_raw.astype(jnp.bfloat16)

    def backward(chunk, gathered_rows):
        gate_low[chunk], upper_low[chunk] = mlp_back(
            gathered_rows, mlp_full, gate[chunk], upper[chunk]
        )
        hidden_part[chunk] = hidden_back(gate_low[chunk], upper_low[chunk], mlp_full)
        back_sum[chunk] = chunk_scatter(hidden_part[chunk])

    turn(0, raw_mlp[0])
    gathered[0] = jnp.concatenate(line_gather(back_raw_mlp[0]), axis=0)
    for chunk in chunks:
        rows = gathered[chunk]
        following = chunk + 1 < CHUNKS
        if following:
            turn(chunk + 1, after(raw_mlp[chunk + 1], rows))
            rows = after(rows, back_raw_mlp[chunk + 1])
        if following:
            gathered[chunk + 1] = jnp.concatenate(shift_gather(back_raw_mlp[chunk + 1]), axis=0)
        backward(chunk, rows)
    out_tokens = jnp.concatenate(out_parts, axis=0)

    down_left = after(gathered, hidden_part)
    down_sent = grad_sent(down_left, inner_low)
    gate_sent = grad_sent(after(hidden_low, down_sent), gate_low)
    down_kept = grad_kept(after(down_left, gate_sent), inner_low, pair_swap(down_sent, 1))
    down_one = exchange_one(down_kept)
    upper_sent = grad_sent(after(hidden_low, down_kept), upper_low)
    gate_kept = grad_kept(after(hidden_low, upper_sent), gate_low, pair_swap(gate_sent, 1))
    upper_kept = grad_kept(
        after(hidden_low, gate_kept, down_one), upper_low, pair_swap(upper_sent, 1)
    )
    gate_one = exchange_one(gate_kept)
    upper_one = exchange_one(upper_kept)

    back_hidden, gains_attn, back_raw_attn, back_rows = ([None] * CHUNKS for _ in range(4))
    back_heads = [None] * CHUNKS
    for chunk in chunks:
        rows = after(back_sum[chunk], upper_kept if chunk else gate_kept)
        back_hidden[chunk] = own_rows(cotangent, chunk) + rows
        back_raw, gains_attn[chunk] = attn_pulls[chunk](back_hidden[chunk])
        back_raw_attn[chunk] = back_raw.astype(jnp.bfloat16)
        if chunk:
            back_raw_attn[chunk] = after(back_raw_attn[chunk], gate_one)
        back_rows[chunk] = jnp.dot(
            back_raw_attn[chunk], out_full, preferred_element_type=jnp.float32
        ).astype(jnp.bfloat16)
        back_heads[chunk] = rows_to_heads(back_rows[chunk])
    back_mixed = jnp.stack([jnp.stack(parts) for parts in back_heads], axis=1)
    back_mixed = back_mixed.reshape(total_rows, local_width)
    out_sent = grad_sent(back_raw_attn, own_mixed)
    down_two = exchange_two(down_kept, after(down_one, upper_kept))
    out_kept = grad_kept(back_raw_attn, own_mixed, pair_swap(out_sent, 1))
    out_one = exchange_one(out_kept)
    back_mixed = after(back_mixed, out_kept, down_two, upper_one)

    back_hats, value_back, cross_lanes, head_gain_grads = attend_back(
        low_heads, back_mixed, projected, inverse_lanes, head_gains, cosine, sine
    )
    gate_two = exchange_two(gate_kept, after(gate_one, back_rows))
    cross_sums = summed_lanes(after(cross_lanes, gate_two))
    mean_lanes = in_lanes(cross_sums / model_width)
    upper_two = exchange_two(upper_kept, after(upper_one, value_back))
    mean_lanes = after(mean_lanes, out_one)
    qkv_back, tokens_part = tokens_back_part(
        back_hats, projected, value_back, inverse_lanes, mean_lanes, qkv_full
    )
    tokens_back = chunk_scatter(tokens_part)
    qkv_left = [after(whole_tokens, tokens_part)]
    qkv_sent = grad_sent(qkv_left, [qkv_back])
    out_two = exchange_two(out_kept, after(out_one, tokens_part))
    qkv_kept = grad_kept(
        after(qkv_left, upper_two, out_two), [qkv_back], pair_swap(qkv_sent, 1)
    )
    qkv_one = exchange_one(qkv_kept)

    gain_grad = jnp.zeros((4, model_width), jnp.float32)
    gain_grad = gain_grad.at[0].set(sum(gains_attn)).at[1].set(sum(gains_mlp))
    gain_grad = lax.dynamic_update_slice(
        gain_grad, head_gain_grads, (jnp.int32(2), column_start)
    )
    gain_final = scatter_gains(after(gain_grad, qkv_kept))
    gate_two, upper_two, down_two = after((gate_two, upper_two, down_two), qkv_kept)
    mlp_owned = jnp.stack([exchange_end(gate_two), exchange_end(upper_two), exchange_end(down_two)])
    new_mlp, new_moment_mlp, new_square_mlp = adamw(
        w_mlp, mlp_owned, moment_mlp, square_mlp, RATE_MATRIX, DECAY_MATRIX
    )
    qkv_two = exchange_two(qkv_kept, after(qkv_one, new_mlp))
    out_owned = shift_scatter(exchange_end(after(out_two, new_mlp)), local_width)
    qkv_owned = exchange_end(qkv_two)
    attn_owned = jnp.stack(
        [qkv_owned[:, k * local_width : (k + 1) * local_width] for k in range(3)] + [out_owned]
    )
    attn_owned = lax.optimization_barrier(attn_owned)
    new_attn, new_moment_attn, new_square_attn = adamw(
        w_attn, attn_owned, moment_attn, square_attn, RATE_MATRIX, DECAY_MATRIX
    )
    new_gains, new_moment_gains, new_square_gains = adamw(
        norm_gains, gain_final, moment_gains, square_gains, RATE_GAIN, 0.0
    )
    tokens_back = after(tokens_back, new_mlp, new_attn, new_gains)
    grad_tokens = (jnp.concatenate(back_hidden, axis=0) + tokens_back).astype(jnp.bfloat16)
    return (
        out_tokens,
        grad_tokens,
        new_attn,
        new_moment_attn,
        new_square_attn,
        new_mlp,
        new_moment_mlp,
        new_square_mlp,
        new_gains,
        new_moment_gains,
        new_square_gains,
    )


def solution(mesh):
    return jax.shard_map(
        local,
        mesh=mesh,
        in_specs=(
            P(("dp", "tensor"), None),
            P("dp", None),
            P(None, "dp", "tensor"),
            P(None, "dp", "tensor"),
            P(None, ("dp", "tensor")),
            P(None, "dp", "tensor"),
            P(None, "dp", "tensor"),
            P(None, "dp", "tensor"),
            P(None, "dp", "tensor"),
            P(None, ("dp", "tensor")),
            P(None, ("dp", "tensor")),
            P(("dp", "tensor"), None),
        ),
        out_specs=(
            P(("dp", "tensor"), None),
            P(("dp", "tensor"), None),
            P(None, "dp", "tensor"),
            P(None, "dp", "tensor"),
            P(None, "dp", "tensor"),
            P(None, "dp", "tensor"),
            P(None, "dp", "tensor"),
            P(None, "dp", "tensor"),
            P(None, ("dp", "tensor")),
            P(None, ("dp", "tensor")),
            P(None, ("dp", "tensor")),
        ),
        check_vma=False,
    )
```

```python
import jax
import jax.numpy as jnp
from jax import lax
from jax.experimental import pallas as pl
from jax.experimental.pallas import tpu as pltpu
from jax.sharding import PartitionSpec as P

HDIM = 128
STEP = 10
CHUNKS = 2
MIB = 1 << 20


NORM_EPS = 1e-06
ROPE_BASE = 500000.0
BETA_ONE = 0.9
BETA_TWO = 0.95
ADAM_EPS = 1e-08
RATE_MATRIX = 0.03
RATE_GAIN = 0.6
DECAY_MATRIX = 0.1
ROW_CONTRACT = (((0,), (0,)), ((), ()))
COLUMN_CONTRACT = (((1,), (1,)), ((), ()))


def doc_positions(lengths, seq_len):
    ends = jnp.cumsum(lengths, axis=-1, dtype=jnp.int32)
    starts = ends - lengths
    places = jnp.arange(seq_len, dtype=jnp.int32)
    inside = starts[:, None, :] <= places[None, :, None]
    begins = jnp.max(jnp.where(inside, starts[:, None, :], jnp.int32(0)), axis=-1)
    return places[None, :] - begins


def rope_tables(positions, head_dim):
    halfway = head_dim // 2
    powers = jnp.arange(halfway, dtype=jnp.float32) * (2.0 / head_dim)
    angles = positions.astype(jnp.float32)[:, None] * jnp.power(ROPE_BASE, -powers)
    return (jnp.cos(angles), jnp.sin(angles))


def adamw(weight, gradient, moment_one, moment_two, rate, decay):
    moment_one = BETA_ONE * moment_one + (1.0 - BETA_ONE) * gradient
    moment_two = BETA_TWO * moment_two + (1.0 - BETA_TWO) * gradient * gradient
    fix_one = 1.0 - BETA_ONE**STEP
    fix_two = 1.0 - BETA_TWO**STEP
    update = moment_one / fix_one / (jnp.sqrt(moment_two / fix_two) + ADAM_EPS)
    return (weight * (1.0 - rate * decay) - rate * update, moment_one, moment_two)


def pick(index, cases):
    if all(case is cases[0] for case in cases):
        return cases[0]
    return lax.select_n(index, *cases)


def after(values, *waits):
    return lax.optimization_barrier((values, waits))[0]


def chunk_scatter(part):
    return lax.psum_scatter(part, "tensor", scatter_dimension=0, tiled=True)


def line_hop(step, up, down):
    count = lax.axis_size("tensor")
    rising = [(i, i + 1) for i in range(step - 1, count - 1)]
    falling = [(i + 1, i) for i in range(count - step)]
    return lax.ppermute(up, "tensor", rising), lax.ppermute(down, "tensor", falling)


def line_pieces(piece, hops):
    count = lax.axis_size("tensor")
    here = lax.axis_index("tensor")
    low = [piece] + [hop[0] for hop in hops]
    high = [piece] + [hop[1] for hop in hops]
    return [
        pick(here, [low[i - owner] if i >= owner else high[owner - i] for i in range(count)])
        for owner in range(count)
    ]


def line_gather(piece, work=()):
    hops, given, pair = [], (), (piece, piece)
    for step in range(1, lax.axis_size("tensor")):
        pair = line_hop(step, *pair)
        if step - 1 < len(work):
            given = work[step - 1](given)
            pair, given = lax.optimization_barrier((pair, given))
        hops.append(pair)
    return line_pieces(piece, hops), given


def shift_gather(piece):
    count = lax.axis_size("tensor")
    here = lax.axis_index("tensor")
    got = [piece] + [lax.ppermute(piece, "tensor", pairs) for pairs in shifts(count)]
    return [
        pick(here, [got[(i - owner) % count] for i in range(count)]) for owner in range(count)
    ]


def together(*values):
    return lax.optimization_barrier(values)


def shift_scatter(values, width):
    count = lax.axis_size("tensor")
    here = lax.axis_index("tensor")
    total = lax.dynamic_slice_in_dim(values, here * width, width, 1)
    for k, pairs in enumerate(shifts(count), 1):
        part = lax.dynamic_slice_in_dim(values, lax.rem(here + k, count) * width, width, 1)
        got = lax.ppermute(part.astype(jnp.bfloat16), "tensor", pairs)
        total = total + got.astype(jnp.float32)
    return total


def shifts(count):
    return [[(i, (i + k) % count) for i in range(count)] for k in range(1, count)]


def small_sum(values, work=lambda: ()):
    got = [lax.ppermute(values, "tensor", pairs) for pairs in shifts(lax.axis_size("tensor"))]
    got, given = together(got, work())
    return sum(got, values), given


def rows_to_heads(values, work):
    count = lax.axis_size("tensor")
    here = lax.axis_index("tensor")
    rows, columns = values.shape
    width = columns // count
    got = [lax.dynamic_slice_in_dim(values, here * width, width, 1)]
    for k, pairs in enumerate(shifts(count), 1):
        block = lax.dynamic_slice_in_dim(values, lax.rem(here + k, count) * width, width, 1)
        got.append(lax.ppermute(block, "tensor", pairs))
    got, given = together(got, work())
    parts = [
        pick(here, [got[(i - owner) % count] for i in range(count)]) for owner in range(count)
    ]
    return jnp.concatenate(parts, axis=0), given


def pair_swap(values, bit):
    count = lax.axis_size("dp")
    return lax.ppermute(values, "dp", [(i, i ^ bit) for i in range(count)])


def gains_over_tensor(gains):
    count = lax.axis_size("tensor")
    here = lax.axis_index("tensor")
    got = [gains] + [lax.ppermute(gains, "tensor", pairs) for pairs in shifts(count)]
    return jnp.concatenate(
        [pick(here, [got[(i - owner) % count] for i in range(count)]) for owner in range(count)],
        axis=1,
    )[None]


def gains_over_dp(blocks, bit):
    if lax.axis_size("dp") & (lax.axis_size("dp") - 1):
        return blocks
    return jnp.concatenate([blocks, pair_swap(blocks, bit)], axis=0)


def gains_end(blocks):
    count = lax.axis_size("dp")
    if blocks.shape[0] != count:
        return lax.all_gather(blocks[0], "dp", axis=1, tiled=True)
    order = jnp.arange(count, dtype=jnp.int32) ^ lax.axis_index("dp")
    return jnp.moveaxis(blocks[order], 0, 1).reshape(blocks.shape[1], -1)


def gains_blocks(grads):
    count = lax.axis_size("dp")
    if count & (count - 1):
        return lax.psum_scatter(grads, "dp", scatter_dimension=1, tiled=True)[None]
    order = jnp.arange(count, dtype=jnp.int32) ^ lax.axis_index("dp")
    return jnp.moveaxis(grads.reshape(grads.shape[0], count, -1), 1, 0)[order]


def gains_fold(blocks):
    bit = blocks.shape[0] // 2
    return blocks[:bit] + pair_swap(blocks[bit:], bit) if bit else blocks


def gains_owned(block):
    count = lax.axis_size("tensor")
    here = lax.axis_index("tensor")
    parts = jnp.moveaxis(block.reshape(block.shape[0], count, -1), 1, 0)
    total = lax.dynamic_index_in_dim(parts, here, 0, keepdims=False)
    for k, pairs in enumerate(shifts(count), 1):
        part = lax.dynamic_index_in_dim(parts, lax.rem(here + k, count), 0, keepdims=False)
        total = total + lax.ppermute(part, "tensor", pairs)
    return total


def kernel(body, grid, in_specs, out_specs, out_shape, operands, scratch=(), order=None):
    spec = pltpu.PrefetchScalarGridSpec(
        num_scalar_prefetch=0 if order is None else 1,
        grid=grid,
        in_specs=in_specs,
        out_specs=out_specs,
        scratch_shapes=scratch,
    )
    return pl.pallas_call(
        body,
        grid_spec=spec,
        out_shape=out_shape,
        compiler_params=pltpu.CompilerParams(vmem_limit_bytes=52 * MIB),
        cost_estimate=pl.CostEstimate(flops=1, bytes_accessed=1, transcendentals=0),
    )(*(() if order is None else (order,)), *operands)


def place_body(order_ref, *refs):
    step = pl.program_id(0)
    out_ref = refs[-1]
    half = out_ref.shape[1] // 2
    for side in range(2):
        own, from_x, from_y, low, high = refs[5 * side : 5 * side + 5]
        for at, piece in enumerate((own, from_x, from_y)):

            @pl.when(step == 4 * side + at)
            def _():
                out_ref[0] = piece[...]

        @pl.when(step == 4 * side + 3)
        def _():
            out_ref[0, :half] = low[...]
            out_ref[0, half:] = high[...]


def plane_one(shard):
    count = lax.axis_size("dp")
    if count != 8 or shard.shape[0] % 32:
        return (lax.all_gather(shard, "dp", axis=0, tiled=True),)
    return shard, pair_swap(shard, 2), pair_swap(shard, 4)


def plane_two(given):
    if len(given) == 1:
        return given
    shard, from_x, from_y = given
    half = shard.shape[0] // 2
    near = (*given, pair_swap(from_x[:half], 4), pair_swap(from_y[half:], 2))
    return (*near, *(pair_swap(piece, 1) for piece in given))


def plane_three(given):
    if len(given) == 1:
        return given[0]
    near, far = given[:5], given[5:]
    far = (*far, pair_swap(near[3], 1), pair_swap(near[4], 1))
    rows, width = near[0].shape
    order = jnp.array([0, 2, 4, 6, 1, 3, 5, 7], jnp.int32) ^ lax.axis_index("dp")
    whole = kernel(
        place_body,
        (8,),
        [whole_block(piece.shape) for piece in (*near, *far)],
        pl.BlockSpec((1, rows, width), lambda step, order_ref: (order_ref[step], 0, 0)),
        jax.ShapeDtypeStruct((8, rows, width), near[0].dtype),
        (*near, *far),
        order=order,
    )
    return whole.reshape(8 * rows, width)


def whole_block(shape):
    return pl.BlockSpec(shape, lambda *at: (0,) * len(shape))


def out_norm_body(mixed_ref, weight_ref, tokens_ref, gain_ref, hidden_ref, raw_ref, all_ref):
    step = pl.program_id(0)
    tile = weight_ref.shape[0]
    product = lax.dot_general(
        mixed_ref[...],
        weight_ref[...],
        COLUMN_CONTRACT,
        preferred_element_type=jnp.float32,
    )
    raw_ref[...] = product
    all_ref[step] = product

    @pl.when(step == pl.num_programs(0) - 1)
    def _():
        rows, width = hidden_ref.shape
        square = jnp.zeros((rows, 1), jnp.float32)
        for at in range(width // tile):
            square = square + jnp.sum(all_ref[at] * all_ref[at], axis=-1, keepdims=True)
        scale = lax.rsqrt(square / width + NORM_EPS)
        for at in range(width // tile):
            columns = slice(at * tile, (at + 1) * tile)
            place = tokens_ref[:, 0, :, columns].reshape(rows, tile).astype(jnp.float32)
            hidden_ref[:, columns] = (
                place + all_ref[at] * scale * gain_ref[:, columns]
            ).astype(jnp.bfloat16)


def out_norm(mixed, weight, tokens, chunk, gain):
    pieces, _, piece_rows, width = tokens.shape
    rows = pieces * piece_rows
    tile = min(512, width)
    part = pl.BlockSpec((pieces, 1, piece_rows, width), lambda n: (0, chunk, 0, 0))
    return kernel(
        out_norm_body,
        (width // tile,),
        [
            whole_block((rows, width)),
            pl.BlockSpec((tile, width), lambda n: (n, 0)),
            part,
            whole_block((1, width)),
        ],
        [whole_block((rows, width)), pl.BlockSpec((rows, tile), lambda n: (0, n))],
        [
            jax.ShapeDtypeStruct((rows, width), jnp.bfloat16),
            jax.ShapeDtypeStruct((rows, width), jnp.float32),
        ],
        (mixed, weight, tokens, gain),
        [pltpu.VMEM((width // tile, rows, tile), jnp.float32)],
    )


def mlp_in_body(hidden_ref, weight_ref, inner_ref, gate_ref, upper_ref):
    gate = jnp.dot(hidden_ref[...], weight_ref[0], preferred_element_type=jnp.float32)
    upper = jnp.dot(hidden_ref[...], weight_ref[1], preferred_element_type=jnp.float32)
    gate_ref[...] = gate
    upper_ref[...] = upper
    inner_ref[...] = (gate * jax.nn.sigmoid(gate) * upper).astype(jnp.bfloat16)


def mlp_in(hidden, weights):
    rows, depth = hidden.shape
    width = weights.shape[2]
    tile = min(512, width)
    out_spec = pl.BlockSpec((rows, tile), lambda n: (0, n))
    return kernel(
        mlp_in_body,
        (width // tile,),
        [whole_block((rows, depth)), pl.BlockSpec((2, depth, tile), lambda n: (0, 0, n))],
        [out_spec] * 3,
        [
            jax.ShapeDtypeStruct((rows, width), kind)
            for kind in (jnp.bfloat16, jnp.float32, jnp.float32)
        ],
        (hidden, weights),
    )


def mlp_out_body(inner_ref, weight_ref, out_ref):
    out_ref[...] = lax.dot_general(
        inner_ref[...], weight_ref[...], COLUMN_CONTRACT, preferred_element_type=jnp.float32
    ).astype(jnp.bfloat16)


def mlp_out(inner, weight):
    rows, depth = inner.shape
    width = weight.shape[-2]
    tile = min(512, width)
    if weight.ndim == 3:
        weight_spec = pl.BlockSpec((None, tile, depth), lambda n: (2, n, 0))
    else:
        weight_spec = pl.BlockSpec((tile, depth), lambda n: (n, 0))
    return kernel(
        mlp_out_body,
        (width // tile,),
        [whole_block((rows, depth)), weight_spec],
        pl.BlockSpec((rows, tile), lambda n: (0, n)),
        jax.ShapeDtypeStruct((rows, width), jnp.bfloat16),
        (inner, weight),
    )


def mlp_back_body(back_ref, weight_ref, gate_ref, upper_ref, back_gate_ref, back_upper_ref):
    back = jnp.dot(back_ref[...], weight_ref[...], preferred_element_type=jnp.float32)
    gate = gate_ref[...]
    share = jax.nn.sigmoid(gate)
    slope = share * (1.0 + gate * (1.0 - share))
    back_gate_ref[...] = (back * upper_ref[...] * slope).astype(jnp.bfloat16)
    back_upper_ref[...] = (back * (gate * share)).astype(jnp.bfloat16)


def mlp_back(back, weight, gate, upper):
    rows, depth = back.shape
    width = weight.shape[2]
    tile = min(512, width)
    spec = pl.BlockSpec((rows, tile), lambda n: (0, n))
    return kernel(
        mlp_back_body,
        (width // tile,),
        [
            whole_block((rows, depth)),
            pl.BlockSpec((None, depth, tile), lambda n: (2, 0, n)),
            spec,
            spec,
        ],
        [spec] * 2,
        [jax.ShapeDtypeStruct((rows, width), jnp.bfloat16)] * 2,
        (back, weight, gate, upper),
    )


def hidden_back_body(gate_ref, upper_ref, weight_ref, out_ref):
    out_ref[...] = (
        lax.dot_general(
            gate_ref[...], weight_ref[0], COLUMN_CONTRACT, preferred_element_type=jnp.float32
        )
        + lax.dot_general(
            upper_ref[...], weight_ref[1], COLUMN_CONTRACT, preferred_element_type=jnp.float32
        )
    ).astype(jnp.bfloat16)


def hidden_back(back_gate, back_upper, weights):
    rows, depth = back_gate.shape
    width = weights.shape[1]
    tile = min(512, width)
    return kernel(
        hidden_back_body,
        (width // tile,),
        [
            whole_block((rows, depth)),
            whole_block((rows, depth)),
            pl.BlockSpec((2, tile, depth), lambda n: (0, n, 0)),
        ],
        pl.BlockSpec((rows, tile), lambda n: (0, n)),
        jax.ShapeDtypeStruct((rows, width), jnp.bfloat16),
        (back_gate, back_upper, weights),
    )


def project_body(tokens_ref, weight_ref, out_ref, sums_ref):
    step = pl.program_id(0)
    product = jnp.dot(tokens_ref[...], weight_ref[...], preferred_element_type=jnp.float32)
    out_ref[...] = product
    sums = jnp.sum(product * product, axis=-1, keepdims=True)
    lanes = lax.broadcasted_iota(jnp.int32, sums_ref.shape, 1)

    @pl.when(step == 0)
    def _():
        sums_ref[...] = jnp.where(lanes == 0, sums, 0.0)

    @pl.when(step == 1)
    def _():
        sums_ref[...] = jnp.where(lanes == 1, sums, sums_ref[...])


def project(tokens, weight):
    rows, depth = tokens.shape
    width = weight.shape[1]
    return kernel(
        project_body,
        (3,),
        [whole_block((rows, depth)), pl.BlockSpec((depth, width // 3), lambda n: (0, n))],
        [pl.BlockSpec((rows, width // 3), lambda n: (0, n)), whole_block((rows, HDIM))],
        [
            jax.ShapeDtypeStruct((rows, width), jnp.float32),
            jax.ShapeDtypeStruct((rows, HDIM), jnp.float32),
        ],
        (tokens, weight),
    )


def turned(values, cosine, sine):
    return values * cosine + pltpu.roll(values, HDIM // 2, 1) * sine


def softmax_rows(query, key, start):
    scores = lax.dot_general(query, key, COLUMN_CONTRACT, preferred_element_type=jnp.float32)
    scores = scores * HDIM ** (-0.5)
    rows = start + lax.broadcasted_iota(jnp.int32, scores.shape, 0)
    columns = lax.broadcasted_iota(jnp.int32, scores.shape, 1)
    scores = jnp.where(columns <= rows, scores, -jnp.inf)
    weights = jnp.exp(scores - jnp.max(scores, axis=-1, keepdims=True))
    return weights / jnp.sum(weights, axis=-1, keepdims=True)


def attend_body(
    query_ref, key_ref, value_ref, scale_ref, gain_ref, cos_ref, sin_ref, low_ref, out_ref
):
    cosine, sine = cos_ref[...], sin_ref[...]
    for at, source in enumerate((query_ref, key_ref)):
        normed = source[...] * scale_ref[:, at : at + 1] * gain_ref[at : at + 1, :]
        low_ref[at] = turned(normed, cosine, sine).astype(jnp.bfloat16)
    low_ref[2] = value_ref[...].astype(jnp.bfloat16)
    rows = out_ref.shape[0]
    block = min(256, rows)
    for start in range(0, rows, block):
        stop = start + block
        share = softmax_rows(low_ref[0, start:stop], low_ref[1, :stop], start)
        out_ref[start:stop] = jnp.dot(
            share.astype(jnp.bfloat16), low_ref[2, :stop], preferred_element_type=jnp.float32
        ).astype(jnp.bfloat16)


def head_specs(rows, heads):
    return [
        pl.BlockSpec((rows, HDIM), lambda h, part=part: (0, part * heads + h)) for part in range(3)
    ]


def attend(projected, scale, gains, cosine, sine):
    rows, width = projected.shape
    heads = width // (3 * HDIM)
    return kernel(
        attend_body,
        (heads,),
        head_specs(rows, heads)
        + [
            whole_block((rows, HDIM)),
            pl.BlockSpec((2, HDIM), lambda h: (0, h)),
            whole_block((rows, HDIM)),
            whole_block((rows, HDIM)),
        ],
        [
            pl.BlockSpec((3, rows, HDIM), lambda h: (0, 0, h)),
            pl.BlockSpec((rows, HDIM), lambda h: (0, h)),
        ],
        [
            jax.ShapeDtypeStruct((3, rows, width // 3), jnp.bfloat16),
            jax.ShapeDtypeStruct((rows, width // 3), jnp.bfloat16),
        ],
        (projected, projected, projected, scale, gains, cosine, sine),
    )


def attend_back_body(
    low_ref,
    back_ref,
    query_ref,
    key_ref,
    scale_ref,
    gain_ref,
    cos_ref,
    sin_ref,
    hats_ref,
    value_out_ref,
    cross_ref,
    gain_out_ref,
    query_sum,
    key_sum,
    value_sum,
):
    rows = value_out_ref.shape[0]
    block = min(256, rows)
    for start in reversed(range(0, rows, block)):
        stop = start + block
        query, key, value = low_ref[0, start:stop], low_ref[1, :stop], low_ref[2, :stop]
        back = back_ref[start:stop]
        share = softmax_rows(query, key, start)
        back_share = lax.dot_general(
            back, value, COLUMN_CONTRACT, preferred_element_type=jnp.float32
        )
        mean = jnp.sum(share * back_share, axis=-1, keepdims=True)
        back_scores = (share * (back_share - mean)).astype(jnp.bfloat16)
        value_part = lax.dot_general(
            share.astype(jnp.bfloat16), back, ROW_CONTRACT, preferred_element_type=jnp.float32
        )
        key_part = lax.dot_general(
            back_scores, query, ROW_CONTRACT, preferred_element_type=jnp.float32
        )
        query_sum[start:stop] = jnp.dot(back_scores, key, preferred_element_type=jnp.float32)
        if stop == rows:
            value_sum[...] = value_part
            key_sum[...] = key_part
        else:
            value_sum[:stop] += value_part
            key_sum[:stop] += key_part
    value_out_ref[...] = value_sum[...].astype(jnp.bfloat16)
    cosine, sine = cos_ref[...], sin_ref[...]
    lanes = lax.broadcasted_iota(jnp.int32, cross_ref.shape, 1)
    cross = jnp.zeros(cross_ref.shape, jnp.float32)
    for at, (source, total) in enumerate(((query_ref, query_sum), (key_ref, key_sum))):
        normed = turned(total[...] * HDIM ** (-0.5), cosine, -sine)
        hat = source[...] * scale_ref[:, at : at + 1]
        gain_out_ref[at : at + 1] = jnp.sum(normed * hat, axis=0, keepdims=True)
        back_hat = normed * gain_ref[at : at + 1, :]
        hats_ref[at] = back_hat
        cross = jnp.where(lanes == at, jnp.sum(back_hat * hat, axis=-1, keepdims=True), cross)

    @pl.when(pl.program_id(0) == 0)
    def _():
        cross_ref[...] = cross

    @pl.when(pl.program_id(0) > 0)
    def _():
        cross_ref[...] += cross


def attend_back(low, back, projected, scale, gains, cosine, sine):
    rows, width = back.shape
    heads = width // HDIM
    head = pl.BlockSpec((rows, HDIM), lambda h: (0, h))
    return kernel(
        attend_back_body,
        (heads,),
        [pl.BlockSpec((3, rows, HDIM), lambda h: (0, 0, h)), head]
        + head_specs(rows, heads)[:2]
        + [
            whole_block((rows, HDIM)),
            pl.BlockSpec((2, HDIM), lambda h: (0, h)),
            whole_block((rows, HDIM)),
            whole_block((rows, HDIM)),
        ],
        [
            pl.BlockSpec((2, rows, HDIM), lambda h: (0, 0, h)),
            head,
            whole_block((rows, HDIM)),
            pl.BlockSpec((2, HDIM), lambda h: (0, h)),
        ],
        [
            jax.ShapeDtypeStruct((2, rows, width), jnp.float32),
            jax.ShapeDtypeStruct((rows, width), jnp.bfloat16),
            jax.ShapeDtypeStruct((rows, HDIM), jnp.float32),
            jax.ShapeDtypeStruct((2, width), jnp.float32),
        ],
        (low, back, projected, projected, scale, gains, cosine, sine),
        [pltpu.VMEM((rows, HDIM), jnp.float32)] * 3,
    )


def tokens_back_body(
    hats_ref, query_ref, key_ref, value_ref, scale_ref, mean_ref, weight_ref, back_ref, out_ref
):
    width = value_ref.shape[1]

    @pl.when(pl.program_id(0) == 0)
    def _():
        for at, source in enumerate((query_ref, key_ref)):
            scale = scale_ref[:, at : at + 1]
            hat = source[...] * scale
            back_ref[:, at * width : (at + 1) * width] = (
                scale * (hats_ref[at] - hat * mean_ref[:, at : at + 1])
            ).astype(jnp.bfloat16)
        back_ref[:, 2 * width :] = value_ref[...]

    out_ref[...] = lax.dot_general(
        back_ref[...], weight_ref[...], COLUMN_CONTRACT, preferred_element_type=jnp.float32
    ).astype(jnp.bfloat16)


def tokens_back_part(hats, projected, value_back, scale, mean, weight):
    rows, width = value_back.shape
    model_width = weight.shape[0]
    tile = min(512, model_width)
    return kernel(
        tokens_back_body,
        (model_width // tile,),
        [
            whole_block((2, rows, width)),
            pl.BlockSpec((rows, width), lambda n: (0, 0)),
            pl.BlockSpec((rows, width), lambda n: (0, 1)),
            whole_block((rows, width)),
            whole_block((rows, HDIM)),
            whole_block((rows, HDIM)),
            pl.BlockSpec((tile, 3 * width), lambda n: (n, 0)),
        ],
        [
            whole_block((rows, 3 * width)),
            pl.BlockSpec((rows, tile), lambda n: (0, n)),
        ],
        [
            jax.ShapeDtypeStruct((rows, 3 * width), jnp.bfloat16),
            jax.ShapeDtypeStruct((rows, model_width), jnp.bfloat16),
        ],
        (hats, projected, projected, value_back, scale, mean, weight),
    )


def norm_parts(raw):
    scale = lax.rsqrt(jnp.mean(raw * raw, axis=-1, keepdims=True) + NORM_EPS)
    return scale, raw * scale


def norm_back(scale, hat, back, gain):
    back_hat = back * gain
    return scale * (back_hat - hat * jnp.mean(back_hat * hat, axis=-1, keepdims=True))


def turn_body(
    place_ref, raw_mlp_ref, raw_ref, tokens_ref, back_ref, gains_ref, out_ref, low_ref, gain_out_ref
):
    _, attn_hat = norm_parts(raw_ref[...])
    scale, hat = norm_parts(raw_mlp_ref[...].astype(jnp.float32))
    hidden = tokens_ref[...].astype(jnp.float32) + attn_hat * gains_ref[0:1]
    out_ref[...] = (hidden + hat * gains_ref[1:2]).astype(jnp.bfloat16)
    back = back_ref[...].astype(jnp.float32)
    low_ref[...] = norm_back(scale, hat, back, gains_ref[1:2]).astype(jnp.bfloat16)
    gain_out_ref[...] = jnp.sum(back * hat, axis=0, keepdims=True)


def turn_rows(raw_mlp, raw_attn, tokens, back, chunk, gains):
    rows, width = raw_mlp.shape
    chunk_spec = pl.BlockSpec((rows, width), lambda n, place_ref: (chunk, 0))
    first = pl.BlockSpec((rows, width), lambda n, place_ref: (0, 0))
    return kernel(
        turn_body,
        (1,),
        [
            first,
            pl.BlockSpec((rows, width), lambda n, place_ref: (place_ref[0], 0)),
            chunk_spec,
            chunk_spec,
            whole_block(gains.shape),
        ],
        [first, first, whole_block((1, width))],
        [
            jax.ShapeDtypeStruct((rows, width), jnp.bfloat16),
            jax.ShapeDtypeStruct((rows, width), jnp.bfloat16),
            jax.ShapeDtypeStruct((1, width), jnp.float32),
        ],
        (raw_mlp, raw_attn, tokens, back, gains),
        order=lax.axis_index("tensor")[None],
    )


def output_back_body(
    place_ref,
    sum_ref,
    raw_ref,
    back_ref,
    gains_ref,
    weight_ref,
    hidden_ref,
    low_ref,
    gain_out_ref,
    rows_ref,
):
    @pl.when(pl.program_id(0) == 0)
    def _():
        scale, hat = norm_parts(raw_ref[...])
        back = back_ref[...].astype(jnp.float32) + sum_ref[...].astype(jnp.float32)
        hidden_ref[...] = back
        gain_out_ref[...] = jnp.sum(back * hat, axis=0, keepdims=True)
        low_ref[...] = norm_back(scale, hat, back, gains_ref[0:1]).astype(jnp.bfloat16)

    rows_ref[...] = jnp.dot(
        low_ref[...], weight_ref[...], preferred_element_type=jnp.float32
    ).astype(jnp.bfloat16)


def output_back_rows(summed, raw_attn, back, chunk, gains, weight):
    rows, width = summed.shape
    tile = min(512, width)
    first = pl.BlockSpec((rows, width), lambda n, place_ref: (0, 0))
    return kernel(
        output_back_body,
        (width // tile,),
        [
            first,
            pl.BlockSpec((rows, width), lambda n, place_ref: (place_ref[0], 0)),
            pl.BlockSpec((rows, width), lambda n, place_ref: (chunk, 0)),
            whole_block(gains.shape),
            pl.BlockSpec((width, tile), lambda n, place_ref: (0, n)),
        ],
        [
            first,
            first,
            whole_block((1, width)),
            pl.BlockSpec((rows, tile), lambda n, place_ref: (0, n)),
        ],
        [
            jax.ShapeDtypeStruct((rows, width), jnp.float32),
            jax.ShapeDtypeStruct((rows, width), jnp.bfloat16),
            jax.ShapeDtypeStruct((1, width), jnp.float32),
            jax.ShapeDtypeStruct((rows, width), jnp.bfloat16),
        ],
        (summed, raw_attn, back, gains, weight),
        order=lax.axis_index("tensor")[None],
    )


def product_of(left_refs, right_refs):
    total = None
    for left_ref, right_ref in zip(left_refs, right_refs):
        product = lax.dot_general(
            left_ref[...], right_ref[...], ROW_CONTRACT, preferred_element_type=jnp.float32
        )
        total = product if total is None else total + product
    return total


def sent_body(order_ref, *refs):
    parts = len(refs) // 2
    refs[-1][...] = product_of(refs[:parts], refs[parts:-1]).astype(jnp.bfloat16)


def kept_body(order_ref, *refs):
    parts = (len(refs) - 5) // 2
    got_ref = refs[2 * parts]
    x_send, y_send, x_keep, y_keep = refs[2 * parts + 1 :]
    step = pl.program_id(0)
    total = product_of(refs[:parts], refs[parts : 2 * parts]) + got_ref[...].astype(jnp.float32)
    total = total.astype(jnp.bfloat16)
    half = total.shape[1] // 2
    left, right = total[:, :half], total[:, half:]

    @pl.when(step < 2)
    def _():
        x_send[0] = left

    @pl.when((step == 1) | (step == 2))
    def _():
        y_send[0] = right

    @pl.when(step >= 2)
    def _():
        x_keep[0] = left

    @pl.when((step == 0) | (step == 3))
    def _():
        y_keep[0] = right


def quick(lefts, rights):
    count = lax.axis_size("dp")
    size = lefts[0].shape[1] // count
    return count == 8 and size % 128 == 0 and rights[0].shape[1] % 256 == 0


def grad_specs(lefts, rights, size):
    return [
        pl.BlockSpec((left.shape[0], size), lambda m, order_ref: (0, order_ref[m]))
        for left in lefts
    ] + [pl.BlockSpec(right.shape, lambda m, order_ref: (0, 0)) for right in rights]


def grad_sent(lefts, rights):
    if not quick(lefts, rights):
        return jnp.zeros((16, 128), jnp.bfloat16)
    size = lefts[0].shape[1] // 8
    width = rights[0].shape[1]
    order = jnp.array([3, 7, 5, 1], jnp.int32) ^ lax.axis_index("dp")
    return kernel(
        sent_body,
        (4,),
        grad_specs(lefts, rights, size),
        pl.BlockSpec((size, width), lambda m, order_ref: (m, 0)),
        jax.ShapeDtypeStruct((4 * size, width), jnp.bfloat16),
        (*lefts, *rights),
        order=order,
    )


def grad_kept(lefts, rights, got):
    if not quick(lefts, rights):
        return [
            sum(
                lax.dot_general(left, right, ROW_CONTRACT, preferred_element_type=jnp.float32)
                for left, right in zip(lefts, rights)
            )
        ]
    size = lefts[0].shape[1] // 8
    width = rights[0].shape[1]
    order = jnp.array([2, 6, 4, 0], jnp.int32) ^ lax.axis_index("dp")
    block = (1, size, width // 2)
    return kernel(
        kept_body,
        (4,),
        grad_specs(lefts, rights, size)
        + [pl.BlockSpec((size, width), lambda m, order_ref: (m, 0))],
        [
            pl.BlockSpec(block, lambda m, order_ref: (jnp.minimum(m, 1), 0, 0)),
            pl.BlockSpec(block, lambda m, order_ref: (m // 2, 0, 0)),
            pl.BlockSpec(block, lambda m, order_ref: (m // 3, 0, 0)),
            pl.BlockSpec(block, lambda m, order_ref: (m // 3, 0, 0)),
        ],
        [jax.ShapeDtypeStruct((2, size, width // 2), jnp.bfloat16)] * 4,
        (*lefts, *rights, got),
        order=order,
    )


def exchange_one(kept):
    if len(kept) == 1:
        return kept
    return [pair_swap(kept[0], 2), pair_swap(kept[1], 4)]


def wide(values):
    return values.astype(jnp.float32)


def exchange_two(kept, first):
    if len(kept) == 1:
        return kept
    x_next = wide(kept[2][0]) + wide(first[0][1])
    y_next = wide(kept[3][0]) + wide(first[1][0])
    return [
        pair_swap(x_next.astype(jnp.bfloat16), 4),
        pair_swap(y_next.astype(jnp.bfloat16), 2),
    ]


def exchange_end(kept, first, second):
    if len(kept) == 1:
        return lax.psum_scatter(
            kept[0].astype(jnp.bfloat16), "dp", scatter_dimension=0, tiled=True
        ).astype(jnp.float32)
    halves = [
        wide(kept[2][1]) + wide(first[0][0]) + wide(second[0]),
        wide(kept[3][1]) + wide(first[1][1]) + wide(second[1]),
    ]
    return jnp.concatenate(halves, axis=1)


def local(
    tokens,
    lengths,
    w_attn,
    w_mlp,
    norm_gains,
    moment_attn,
    square_attn,
    moment_mlp,
    square_mlp,
    moment_gains,
    square_gains,
    cotangent,
):
    rows_here, model_width = tokens.shape
    tensor_size = lax.axis_size("tensor")
    tensor_index = lax.axis_index("tensor")
    total_rows = rows_here * tensor_size
    seq_len = total_rows // lengths.shape[0]
    local_width = w_attn.shape[2]
    chunk_rows = rows_here // CHUNKS

    qkv_shard = jnp.concatenate([w_attn[k].astype(jnp.bfloat16) for k in range(3)], axis=1)
    mlp_low = w_mlp.astype(jnp.bfloat16)
    positions = doc_positions(lengths, seq_len).reshape(total_rows)

    gains_low = norm_gains.astype(jnp.bfloat16)
    hop, near, gains, mlp_low = lax.optimization_barrier(
        (line_hop(1, tokens, tokens), plane_one(qkv_shard), gains_over_tensor(gains_low), mlp_low)
    )
    hops = [hop]
    mlp_shard = after(mlp_low, near)
    mlp_full = lax.all_gather(mlp_shard, "dp", axis=1, tiled=True)
    hop, near, gains, mlp_shard = lax.optimization_barrier(
        (line_hop(2, *hop), plane_two(near), gains_over_dp(gains, 1), mlp_shard)
    )
    hops.append(hop)
    cos_table, sin_table = rope_tables(positions, HDIM)
    cosine = jnp.concatenate([cos_table, cos_table], axis=1)
    sine = jnp.concatenate([-sin_table, sin_table], axis=1)
    hop, qkv_full, gains, cosine, sine = lax.optimization_barrier(
        (line_hop(3, *hop), plane_three(near), gains_over_dp(gains, 2), cosine, sine)
    )
    hops.append(hop)
    whole_tokens = jnp.concatenate(line_pieces(tokens, hops), axis=0)
    bit = 4
    while bit < lax.axis_size("dp"):
        gains = gains_over_dp(gains, bit)
        bit = bit * 2
    gain_full = gains_end(gains)
    gain_values = gain_full.astype(jnp.float32)
    column_start = tensor_index * local_width
    head_gains = lax.dynamic_slice_in_dim(gain_values[2:], column_start, local_width, 1)

    def summed_lanes(lanes, work=lambda: ()):
        flat = lax.optimization_barrier(lanes[:, :2].T.reshape(-1, HDIM))
        total, given = small_sum(flat, work)
        return total.reshape(2, lanes.shape[0]), given

    def in_lanes(values):
        return jnp.pad(values.T, ((0, 0), (0, HDIM - 2)))

    projected, square_lanes = project(whole_tokens, qkv_full)
    inverse = lax.rsqrt(summed_lanes(square_lanes)[0] / model_width + NORM_EPS)
    inverse_lanes = in_lanes(inverse)
    out_piece = after(w_attn[3].astype(jnp.bfloat16), whole_tokens)
    out_shard = jnp.concatenate(shift_gather(out_piece), axis=1)
    inverse_lanes, out_shard = lax.optimization_barrier((inverse_lanes, out_shard))
    low_heads, mixed_low = attend(projected, inverse_lanes, head_gains, cosine, sine)
    mixed_pieces = mixed_low.reshape(tensor_size, CHUNKS, chunk_rows, local_width)

    def mixed_chunk(chunk):
        return mixed_pieces[:, chunk].reshape(tensor_size * chunk_rows, local_width)

    tokens_parted = whole_tokens.reshape(tensor_size, CHUNKS, chunk_rows, model_width)

    def own_part(values):
        parted = values.reshape((tensor_size, chunk_rows) + values.shape[1:])
        return lax.dynamic_index_in_dim(parted, tensor_index, 0, keepdims=False)

    chunks = range(CHUNKS)
    mixed, raw_attn, hidden_low, gate = ([None] * CHUNKS for _ in range(4))
    upper, inner_low, down_part, raw_mlp = ([None] * CHUNKS for _ in range(4))

    def forward(chunk):
        def first(_):
            hidden_low[chunk], raw_attn[chunk] = out_norm(
                mixed[chunk], out_full, tokens_parted, chunk, gain_values[:1]
            )
            return hidden_low[chunk], raw_attn[chunk]

        def second(given):
            hidden_low[chunk], raw_attn[chunk] = given
            outs = mlp_in(hidden_low[chunk], mlp_full)
            inner_low[chunk], gate[chunk], upper[chunk] = outs
            return outs

        def third(given):
            inner_low[chunk], gate[chunk], upper[chunk] = given
            down_part[chunk] = mlp_out(inner_low[chunk], mlp_full)
            return down_part[chunk]

        return first, second, third

    pieces, out_full = lax.optimization_barrier(
        (line_gather(mixed_chunk(0))[0], plane_three(plane_two(plane_one(out_shard))))
    )
    for chunk in chunks:
        mixed[chunk] = jnp.concatenate(pieces, axis=1)
        if chunk + 1 < CHUNKS:
            piece = after(mixed_chunk(chunk + 1), out_full if chunk == 0 else mixed[chunk])
            pieces, down_part[chunk] = line_gather(piece, forward(chunk))
        else:
            given = ()
            for work in forward(chunk):
                given = work(given)
        raw_mlp[chunk] = chunk_scatter(down_part[chunk])

    own_mixed = [own_part(mixed[chunk]) for chunk in chunks]
    out_parts, back_raw_mlp, gains_mlp = ([None] * CHUNKS for _ in range(3))
    gathered, gate_low, upper_low, hidden_part, back_sum = ([None] * CHUNKS for _ in range(5))

    def turn(chunk, raw):
        out_parts[chunk], back_raw_mlp[chunk], gains_mlp[chunk] = turn_rows(
            raw, raw_attn[chunk], tokens, cotangent, chunk, gain_values
        )

    def gather_rows(chunk, hops):
        pieces = line_pieces(back_raw_mlp[chunk], hops)
        gathered[chunk] = jnp.concatenate(pieces, axis=0)

    def back_inner(chunk):
        return mlp_back(gathered[chunk], mlp_full, gate[chunk], upper[chunk])

    def back_hidden_part(chunk):
        return hidden_back(gate_low[chunk], upper_low[chunk], mlp_full)

    turn(0, raw_mlp[0])
    early_one = line_hop(1, back_raw_mlp[0], back_raw_mlp[0])
    early_two, late_raw = together(line_hop(2, *early_one), raw_mlp[1])
    turn(1, late_raw)
    early_three, late_one = together(
        line_hop(3, *early_two), line_hop(1, back_raw_mlp[1], back_raw_mlp[1])
    )
    gather_rows(0, (early_one, early_two, early_three))
    late_two, (gate_low[0], upper_low[0]) = together(line_hop(2, *late_one), back_inner(0))
    late_three, hidden_part[0] = together(line_hop(3, *late_two), back_hidden_part(0))
    back_sum[0] = chunk_scatter(hidden_part[0])
    gather_rows(1, (late_one, late_two, late_three))
    gate_low[1], upper_low[1] = back_inner(1)
    hidden_part[1] = back_hidden_part(1)
    back_sum[1] = chunk_scatter(hidden_part[1])
    out_tokens = jnp.concatenate(out_parts, axis=0)

    back_hidden, gains_attn, back_raw_attn, back_rows = ([None] * CHUNKS for _ in range(4))

    def output_back(chunk, rows):
        outs = output_back_rows(rows, raw_attn[chunk], cotangent, chunk, gain_values, out_full)
        back_hidden[chunk], back_raw_attn[chunk], gains_attn[chunk], back_rows[chunk] = outs

    down_left = after(gathered, hidden_part)
    down_sent = grad_sent(down_left, inner_low)
    gate_sent = grad_sent(after(hidden_low, down_sent), gate_low)
    for chunk in chunks[:-1]:
        output_back(chunk, after(back_sum[chunk], gate_sent))
    down_kept = grad_kept(
        after(down_left, gate_sent, back_rows[:-1]), inner_low, pair_swap(down_sent, 1)
    )
    down_one = exchange_one(down_kept)
    upper_sent = grad_sent(after(hidden_low, down_kept), upper_low)
    gate_kept = grad_kept(after(hidden_low, upper_sent), gate_low, pair_swap(gate_sent, 1))
    output_back(CHUNKS - 1, after(back_sum[-1], gate_kept))
    gate_one = exchange_one(after(gate_kept, back_rows))
    back_mixed, (down_one, upper_kept, out_sent) = rows_to_heads(
        jnp.concatenate(back_rows, axis=0),
        lambda: (
            down_one,
            grad_kept(after(hidden_low, back_rows), upper_low, pair_swap(upper_sent, 1)),
            grad_sent(back_raw_attn, own_mixed),
        ),
    )
    upper_one = exchange_one(upper_kept)
    back_hats, value_back, cross_lanes, head_gain_grads = attend_back(
        low_heads, back_mixed, projected, inverse_lanes, head_gains, cosine, sine
    )
    cross_lanes = after(cross_lanes, gate_one)
    down_two = exchange_two(down_kept, after(down_one, cross_lanes))
    cross_sums, out_kept = summed_lanes(
        cross_lanes,
        lambda: grad_kept(
            after(back_raw_attn, cross_lanes), own_mixed, pair_swap(out_sent, 1)
        ),
    )
    out_one = exchange_one(out_kept)
    mean_lanes = in_lanes(cross_sums / model_width)
    qkv_back, tokens_part = tokens_back_part(
        back_hats, projected, value_back, inverse_lanes, mean_lanes, qkv_full
    )
    tokens_back = chunk_scatter(tokens_part)
    gain_grad = jnp.zeros((4, model_width), jnp.float32)
    gain_grad = gain_grad.at[0].set(sum(gains_attn)[0]).at[1].set(sum(gains_mlp)[0])
    gain_grad = lax.dynamic_update_slice(
        gain_grad, head_gain_grads, (jnp.int32(2), column_start)
    )
    gains = gains_blocks(gain_grad)
    qkv_left, gains = after(([whole_tokens], gains), tokens_part)
    while gains.shape[0] > 8:
        gains = gains_fold(gains)

    down_two, upper_one, qkv_sent, gains = together(
        down_two,
        upper_one,
        grad_sent(qkv_left, [qkv_back]),
        gains_fold(gains),
    )
    gate_two, upper_two, out_one, qkv_kept, gains = together(
        exchange_two(gate_kept, after(gate_one, qkv_sent)),
        exchange_two(upper_kept, upper_one),
        out_one,
        grad_kept(qkv_left, [qkv_back], pair_swap(qkv_sent, 1)),
        gains_fold(gains),
    )
    mlp_owned = jnp.stack(
        [
            exchange_end(gate_kept, gate_one, gate_two),
            exchange_end(upper_kept, upper_one, upper_two),
            exchange_end(down_kept, down_one, down_two),
        ]
    )
    out_two, qkv_one, (new_mlp, new_moment_mlp, new_square_mlp), gains = together(
        exchange_two(out_kept, out_one),
        exchange_one(qkv_kept),
        adamw(w_mlp, mlp_owned, moment_mlp, square_mlp, RATE_MATRIX, DECAY_MATRIX),
        gains_fold(gains),
    )
    qkv_two, out_owned, gain_final = together(
        exchange_two(qkv_kept, qkv_one),
        shift_scatter(exchange_end(out_kept, out_one, out_two), local_width),
        gains_owned(gains[0]),
    )
    qkv_owned = exchange_end(qkv_kept, qkv_one, qkv_two)
    attn_owned = jnp.stack(
        [qkv_owned[:, k * local_width : (k + 1) * local_width] for k in range(3)] + [out_owned]
    )
    attn_owned = lax.optimization_barrier(attn_owned)
    new_attn, new_moment_attn, new_square_attn = adamw(
        w_attn, attn_owned, moment_attn, square_attn, RATE_MATRIX, DECAY_MATRIX
    )
    new_gains, new_moment_gains, new_square_gains = adamw(
        norm_gains, gain_final, moment_gains, square_gains, RATE_GAIN, 0.0
    )
    tokens_back = after(tokens_back, new_mlp, new_attn, new_gains)
    grad_tokens = (jnp.concatenate(back_hidden, axis=0) + tokens_back.astype(jnp.float32)).astype(jnp.bfloat16)
    return (
        out_tokens,
        grad_tokens,
        new_attn,
        new_moment_attn,
        new_square_attn,
        new_mlp,
        new_moment_mlp,
        new_square_mlp,
        new_gains,
        new_moment_gains,
        new_square_gains,
    )


def solution(mesh):
    return jax.shard_map(
        local,
        mesh=mesh,
        in_specs=(
            P(("dp", "tensor"), None),
            P("dp", None),
            P(None, "dp", "tensor"),
            P(None, "dp", "tensor"),
            P(None, ("dp", "tensor")),
            P(None, "dp", "tensor"),
            P(None, "dp", "tensor"),
            P(None, "dp", "tensor"),
            P(None, "dp", "tensor"),
            P(None, ("dp", "tensor")),
            P(None, ("dp", "tensor")),
            P(("dp", "tensor"), None),
        ),
        out_specs=(
            P(("dp", "tensor"), None),
            P(("dp", "tensor"), None),
            P(None, "dp", "tensor"),
            P(None, "dp", "tensor"),
            P(None, "dp", "tensor"),
            P(None, "dp", "tensor"),
            P(None, "dp", "tensor"),
            P(None, "dp", "tensor"),
            P(None, ("dp", "tensor")),
            P(None, ("dp", "tensor")),
            P(None, ("dp", "tensor")),
        ),
        check_vma=False,
    )
```

```python
import jax
import jax.numpy as jnp
from jax import lax
from jax.experimental import pallas as pl
from jax.experimental.pallas import tpu as pltpu
from jax.sharding import PartitionSpec as P

HDIM = 128
STEP = 10
CHUNKS = 2
MIB = 1 << 20


NORM_EPS = 1e-06
ROPE_BASE = 500000.0
BETA_ONE = 0.9
BETA_TWO = 0.95
ADAM_EPS = 1e-08
RATE_MATRIX = 0.03
RATE_GAIN = 0.6
DECAY_MATRIX = 0.1
ROW_CONTRACT = (((0,), (0,)), ((), ()))
COLUMN_CONTRACT = (((1,), (1,)), ((), ()))


def doc_positions(lengths, seq_len):
    ends = jnp.cumsum(lengths, axis=-1, dtype=jnp.int32)
    starts = ends - lengths
    places = jnp.arange(seq_len, dtype=jnp.int32)
    inside = starts[:, None, :] <= places[None, :, None]
    begins = jnp.max(jnp.where(inside, starts[:, None, :], jnp.int32(0)), axis=-1)
    return places[None, :] - begins


def rope_tables(positions, head_dim):
    halfway = head_dim // 2
    powers = jnp.arange(halfway, dtype=jnp.float32) * (2.0 / head_dim)
    angles = positions.astype(jnp.float32)[:, None] * jnp.power(ROPE_BASE, -powers)
    return (jnp.cos(angles), jnp.sin(angles))


def adamw(weight, gradient, moment_one, moment_two, rate, decay):
    moment_one = BETA_ONE * moment_one + (1.0 - BETA_ONE) * gradient
    moment_two = BETA_TWO * moment_two + (1.0 - BETA_TWO) * gradient * gradient
    fix_one = 1.0 - BETA_ONE**STEP
    fix_two = 1.0 - BETA_TWO**STEP
    update = moment_one / fix_one / (jnp.sqrt(moment_two / fix_two) + ADAM_EPS)
    return (weight * (1.0 - rate * decay) - rate * update, moment_one, moment_two)


def pick(index, cases):
    if all(case is cases[0] for case in cases):
        return cases[0]
    return lax.select_n(index, *cases)


def after(values, *waits):
    return lax.optimization_barrier((values, waits))[0]


def chunk_scatter(part):
    return lax.psum_scatter(part, "tensor", scatter_dimension=0, tiled=True)


def line_hop(step, up, down):
    count = lax.axis_size("tensor")
    rising = [(i, i + 1) for i in range(step - 1, count - 1)]
    falling = [(i + 1, i) for i in range(count - step)]
    return lax.ppermute(up, "tensor", rising), lax.ppermute(down, "tensor", falling)


def line_pieces(piece, hops):
    count = lax.axis_size("tensor")
    here = lax.axis_index("tensor")
    low = [piece] + [hop[0] for hop in hops]
    high = [piece] + [hop[1] for hop in hops]
    return [
        pick(here, [low[i - owner] if i >= owner else high[owner - i] for i in range(count)])
        for owner in range(count)
    ]


def line_gather(piece, work=()):
    hops, given, pair = [], (), (piece, piece)
    for step in range(1, lax.axis_size("tensor")):
        pair = line_hop(step, *pair)
        if step - 1 < len(work):
            given = work[step - 1](given)
            pair, given = lax.optimization_barrier((pair, given))
        hops.append(pair)
    return line_pieces(piece, hops), given


def shift_gather(piece):
    count = lax.axis_size("tensor")
    here = lax.axis_index("tensor")
    got = [piece] + [lax.ppermute(piece, "tensor", pairs) for pairs in shifts(count)]
    return [
        pick(here, [got[(i - owner) % count] for i in range(count)]) for owner in range(count)
    ]


def together(*values):
    return lax.optimization_barrier(values)


def shift_scatter(values, width):
    count = lax.axis_size("tensor")
    here = lax.axis_index("tensor")
    total = lax.dynamic_slice_in_dim(values, here * width, width, 1)
    for k, pairs in enumerate(shifts(count), 1):
        part = lax.dynamic_slice_in_dim(values, lax.rem(here + k, count) * width, width, 1)
        got = lax.ppermute(part.astype(jnp.bfloat16), "tensor", pairs)
        total = total + got.astype(jnp.float32)
    return total


def shifts(count):
    return [[(i, (i + k) % count) for i in range(count)] for k in range(1, count)]


def small_sum(values, work=lambda: ()):
    got = [lax.ppermute(values, "tensor", pairs) for pairs in shifts(lax.axis_size("tensor"))]
    got, given = together(got, work())
    return sum(got, values), given


def rows_to_heads(values, work):
    count = lax.axis_size("tensor")
    here = lax.axis_index("tensor")
    rows, columns = values.shape
    width = columns // count
    got = [lax.dynamic_slice_in_dim(values, here * width, width, 1)]
    for k, pairs in enumerate(shifts(count), 1):
        block = lax.dynamic_slice_in_dim(values, lax.rem(here + k, count) * width, width, 1)
        got.append(lax.ppermute(block, "tensor", pairs))
    got, given = together(got, work())
    parts = [
        pick(here, [got[(i - owner) % count] for i in range(count)]) for owner in range(count)
    ]
    return jnp.concatenate(parts, axis=0), given


def pair_swap(values, bit):
    count = lax.axis_size("dp")
    return lax.ppermute(values, "dp", [(i, i ^ bit) for i in range(count)])


def gains_over_tensor(gains):
    count = lax.axis_size("tensor")
    here = lax.axis_index("tensor")
    got = [gains] + [lax.ppermute(gains, "tensor", pairs) for pairs in shifts(count)]
    return jnp.concatenate(
        [pick(here, [got[(i - owner) % count] for i in range(count)]) for owner in range(count)],
        axis=1,
    )[None]


def gains_over_dp(blocks, bit):
    if lax.axis_size("dp") & (lax.axis_size("dp") - 1):
        return blocks
    return jnp.concatenate([blocks, pair_swap(blocks, bit)], axis=0)


def gains_end(blocks):
    count = lax.axis_size("dp")
    if blocks.shape[0] != count:
        return lax.all_gather(blocks[0], "dp", axis=1, tiled=True)
    order = jnp.arange(count, dtype=jnp.int32) ^ lax.axis_index("dp")
    return jnp.moveaxis(blocks[order], 0, 1).reshape(blocks.shape[1], -1)


def gains_blocks(grads):
    count = lax.axis_size("dp")
    if count & (count - 1):
        return lax.psum_scatter(grads, "dp", scatter_dimension=1, tiled=True)[None]
    order = jnp.arange(count, dtype=jnp.int32) ^ lax.axis_index("dp")
    return jnp.moveaxis(grads.reshape(grads.shape[0], count, -1), 1, 0)[order]


def gains_fold(blocks):
    if blocks.shape[0] % 2:
        return blocks
    return blocks[0::2] + pair_swap(blocks[1::2], 1)


def gains_rest(blocks):
    step = max(1, lax.axis_size("dp") // blocks.shape[0])
    return [blocks[0]] + [pair_swap(blocks[d], step * d) for d in range(1, blocks.shape[0])]


def gains_owned(block):
    count = lax.axis_size("tensor")
    here = lax.axis_index("tensor")
    parts = jnp.moveaxis(block.reshape(block.shape[0], count, -1), 1, 0)
    total = lax.dynamic_index_in_dim(parts, here, 0, keepdims=False)
    for k, pairs in enumerate(shifts(count), 1):
        part = lax.dynamic_index_in_dim(parts, lax.rem(here + k, count), 0, keepdims=False)
        total = total + lax.ppermute(part, "tensor", pairs)
    return total


def kernel(body, grid, in_specs, out_specs, out_shape, operands, scratch=(), order=None):
    spec = pltpu.PrefetchScalarGridSpec(
        num_scalar_prefetch=0 if order is None else 1,
        grid=grid,
        in_specs=in_specs,
        out_specs=out_specs,
        scratch_shapes=scratch,
    )
    return pl.pallas_call(
        body,
        grid_spec=spec,
        out_shape=out_shape,
        compiler_params=pltpu.CompilerParams(vmem_limit_bytes=52 * MIB),
        cost_estimate=pl.CostEstimate(flops=1, bytes_accessed=1, transcendentals=0),
    )(*(() if order is None else (order,)), *operands)


def place_body(order_ref, *refs):
    step = pl.program_id(0)
    out_ref = refs[-1]
    half = out_ref.shape[1] // 2
    for side in range(2):
        own, from_x, from_y, low, high = refs[5 * side : 5 * side + 5]
        for at, piece in enumerate((own, from_x, from_y)):

            @pl.when(step == 4 * side + at)
            def _():
                out_ref[0] = piece[...]

        @pl.when(step == 4 * side + 3)
        def _():
            out_ref[0, :half] = low[...]
            out_ref[0, half:] = high[...]


def plane_one(shard):
    count = lax.axis_size("dp")
    if count != 8 or shard.shape[0] % 32:
        return (lax.all_gather(shard, "dp", axis=0, tiled=True),)
    return shard, pair_swap(shard, 2), pair_swap(shard, 4)


def plane_two(given):
    if len(given) == 1:
        return given
    shard, from_x, from_y = given
    half = shard.shape[0] // 2
    near = (*given, pair_swap(from_x[:half], 4), pair_swap(from_y[half:], 2))
    return (*near, *(pair_swap(piece, 1) for piece in given))


def plane_three(given):
    if len(given) == 1:
        return given[0]
    near, far = given[:5], given[5:]
    far = (*far, pair_swap(near[3], 1), pair_swap(near[4], 1))
    rows, width = near[0].shape
    order = jnp.array([0, 2, 4, 6, 1, 3, 5, 7], jnp.int32) ^ lax.axis_index("dp")
    whole = kernel(
        place_body,
        (8,),
        [whole_block(piece.shape) for piece in (*near, *far)],
        pl.BlockSpec((1, rows, width), lambda step, order_ref: (order_ref[step], 0, 0)),
        jax.ShapeDtypeStruct((8, rows, width), near[0].dtype),
        (*near, *far),
        order=order,
    )
    return whole.reshape(8 * rows, width)


def whole_block(shape):
    return pl.BlockSpec(shape, lambda *at: (0,) * len(shape))


def out_norm_body(mixed_ref, weight_ref, tokens_ref, gain_ref, hidden_ref, raw_ref, all_ref):
    step = pl.program_id(0)
    tile = weight_ref.shape[0]
    product = lax.dot_general(
        mixed_ref[...],
        weight_ref[...],
        COLUMN_CONTRACT,
        preferred_element_type=jnp.float32,
    )
    raw_ref[...] = product
    all_ref[step] = product

    @pl.when(step == pl.num_programs(0) - 1)
    def _():
        rows, width = hidden_ref.shape
        square = jnp.zeros((rows, 1), jnp.float32)
        for at in range(width // tile):
            square = square + jnp.sum(all_ref[at] * all_ref[at], axis=-1, keepdims=True)
        scale = lax.rsqrt(square / width + NORM_EPS)
        for at in range(width // tile):
            columns = slice(at * tile, (at + 1) * tile)
            place = tokens_ref[:, 0, :, columns].reshape(rows, tile).astype(jnp.float32)
            hidden_ref[:, columns] = (
                place + all_ref[at] * scale * gain_ref[:, columns]
            ).astype(jnp.bfloat16)


def out_norm(mixed, weight, tokens, chunk, gain):
    pieces, _, piece_rows, width = tokens.shape
    rows = pieces * piece_rows
    tile = min(512, width)
    part = pl.BlockSpec((pieces, 1, piece_rows, width), lambda n: (0, chunk, 0, 0))
    return kernel(
        out_norm_body,
        (width // tile,),
        [
            whole_block((rows, width)),
            pl.BlockSpec((tile, width), lambda n: (n, 0)),
            part,
            whole_block((1, width)),
        ],
        [whole_block((rows, width)), pl.BlockSpec((rows, tile), lambda n: (0, n))],
        [
            jax.ShapeDtypeStruct((rows, width), jnp.bfloat16),
            jax.ShapeDtypeStruct((rows, width), jnp.float32),
        ],
        (mixed, weight, tokens, gain),
        [pltpu.VMEM((width // tile, rows, tile), jnp.float32)],
    )


def mlp_in_body(hidden_ref, weight_ref, inner_ref, gate_ref, upper_ref):
    gate = jnp.dot(hidden_ref[...], weight_ref[0], preferred_element_type=jnp.float32)
    upper = jnp.dot(hidden_ref[...], weight_ref[1], preferred_element_type=jnp.float32)
    gate_ref[...] = gate
    upper_ref[...] = upper
    inner_ref[...] = (gate * jax.nn.sigmoid(gate) * upper).astype(jnp.bfloat16)


def mlp_in(hidden, weights):
    rows, depth = hidden.shape
    width = weights.shape[2]
    tile = min(512, width)
    out_spec = pl.BlockSpec((rows, tile), lambda n: (0, n))
    return kernel(
        mlp_in_body,
        (width // tile,),
        [whole_block((rows, depth)), pl.BlockSpec((2, depth, tile), lambda n: (0, 0, n))],
        [out_spec] * 3,
        [
            jax.ShapeDtypeStruct((rows, width), kind)
            for kind in (jnp.bfloat16, jnp.float32, jnp.float32)
        ],
        (hidden, weights),
    )


def mlp_out_body(inner_ref, weight_ref, out_ref):
    out_ref[...] = lax.dot_general(
        inner_ref[...], weight_ref[...], COLUMN_CONTRACT, preferred_element_type=jnp.float32
    ).astype(jnp.bfloat16)


def mlp_out(inner, weight):
    rows, depth = inner.shape
    width = weight.shape[-2]
    tile = min(512, width)
    if weight.ndim == 3:
        weight_spec = pl.BlockSpec((None, tile, depth), lambda n: (2, n, 0))
    else:
        weight_spec = pl.BlockSpec((tile, depth), lambda n: (n, 0))
    return kernel(
        mlp_out_body,
        (width // tile,),
        [whole_block((rows, depth)), weight_spec],
        pl.BlockSpec((rows, tile), lambda n: (0, n)),
        jax.ShapeDtypeStruct((rows, width), jnp.bfloat16),
        (inner, weight),
    )


def mlp_back_body(back_ref, weight_ref, gate_ref, upper_ref, back_gate_ref, back_upper_ref):
    back = jnp.dot(back_ref[...], weight_ref[...], preferred_element_type=jnp.float32)
    gate = gate_ref[...]
    share = jax.nn.sigmoid(gate)
    slope = share * (1.0 + gate * (1.0 - share))
    back_gate_ref[...] = (back * upper_ref[...] * slope).astype(jnp.bfloat16)
    back_upper_ref[...] = (back * (gate * share)).astype(jnp.bfloat16)


def mlp_back(back, weight, gate, upper):
    rows, depth = back.shape
    width = weight.shape[2]
    tile = min(512, width)
    spec = pl.BlockSpec((rows, tile), lambda n: (0, n))
    return kernel(
        mlp_back_body,
        (width // tile,),
        [
            whole_block((rows, depth)),
            pl.BlockSpec((None, depth, tile), lambda n: (2, 0, n)),
            spec,
            spec,
        ],
        [spec] * 2,
        [jax.ShapeDtypeStruct((rows, width), jnp.bfloat16)] * 2,
        (back, weight, gate, upper),
    )


def hidden_back_body(gate_ref, upper_ref, weight_ref, out_ref):
    out_ref[...] = (
        lax.dot_general(
            gate_ref[...], weight_ref[0], COLUMN_CONTRACT, preferred_element_type=jnp.float32
        )
        + lax.dot_general(
            upper_ref[...], weight_ref[1], COLUMN_CONTRACT, preferred_element_type=jnp.float32
        )
    ).astype(jnp.bfloat16)


def hidden_back(back_gate, back_upper, weights):
    rows, depth = back_gate.shape
    width = weights.shape[1]
    tile = min(512, width)
    return kernel(
        hidden_back_body,
        (width // tile,),
        [
            whole_block((rows, depth)),
            whole_block((rows, depth)),
            pl.BlockSpec((2, tile, depth), lambda n: (0, n, 0)),
        ],
        pl.BlockSpec((rows, tile), lambda n: (0, n)),
        jax.ShapeDtypeStruct((rows, width), jnp.bfloat16),
        (back_gate, back_upper, weights),
    )


def project_body(tokens_ref, weight_ref, out_ref, sums_ref):
    step = pl.program_id(0)
    product = jnp.dot(tokens_ref[...], weight_ref[...], preferred_element_type=jnp.float32)
    out_ref[...] = product
    sums = jnp.sum(product * product, axis=-1, keepdims=True)
    lanes = lax.broadcasted_iota(jnp.int32, sums_ref.shape, 1)

    @pl.when(step == 0)
    def _():
        sums_ref[...] = jnp.where(lanes == 0, sums, 0.0)

    @pl.when(step == 1)
    def _():
        sums_ref[...] = jnp.where(lanes == 1, sums, sums_ref[...])


def project(tokens, weight):
    rows, depth = tokens.shape
    width = weight.shape[1]
    return kernel(
        project_body,
        (3,),
        [whole_block((rows, depth)), pl.BlockSpec((depth, width // 3), lambda n: (0, n))],
        [pl.BlockSpec((rows, width // 3), lambda n: (0, n)), whole_block((rows, HDIM))],
        [
            jax.ShapeDtypeStruct((rows, width), jnp.float32),
            jax.ShapeDtypeStruct((rows, HDIM), jnp.float32),
        ],
        (tokens, weight),
    )


def turned(values, cosine, sine):
    return values * cosine + pltpu.roll(values, HDIM // 2, 1) * sine


def softmax_rows(query, key, start):
    scores = lax.dot_general(query, key, COLUMN_CONTRACT, preferred_element_type=jnp.float32)
    scores = scores * HDIM ** (-0.5)
    rows = start + lax.broadcasted_iota(jnp.int32, scores.shape, 0)
    columns = lax.broadcasted_iota(jnp.int32, scores.shape, 1)
    scores = jnp.where(columns <= rows, scores, -jnp.inf)
    weights = jnp.exp(scores - jnp.max(scores, axis=-1, keepdims=True))
    return weights / jnp.sum(weights, axis=-1, keepdims=True)


def attend_body(
    query_ref, key_ref, value_ref, scale_ref, gain_ref, cos_ref, sin_ref, low_ref, out_ref
):
    cosine, sine = cos_ref[...], sin_ref[...]
    for at, source in enumerate((query_ref, key_ref)):
        normed = source[...] * scale_ref[:, at : at + 1] * gain_ref[at : at + 1, :]
        low_ref[at] = turned(normed, cosine, sine).astype(jnp.bfloat16)
    low_ref[2] = value_ref[...].astype(jnp.bfloat16)
    rows = out_ref.shape[0]
    block = min(256, rows)
    for start in range(0, rows, block):
        stop = start + block
        share = softmax_rows(low_ref[0, start:stop], low_ref[1, :stop], start)
        out_ref[start:stop] = jnp.dot(
            share.astype(jnp.bfloat16), low_ref[2, :stop], preferred_element_type=jnp.float32
        ).astype(jnp.bfloat16)


def head_specs(rows, heads):
    return [
        pl.BlockSpec((rows, HDIM), lambda h, part=part: (0, part * heads + h)) for part in range(3)
    ]


def attend(projected, scale, gains, cosine, sine):
    rows, width = projected.shape
    heads = width // (3 * HDIM)
    return kernel(
        attend_body,
        (heads,),
        head_specs(rows, heads)
        + [
            whole_block((rows, HDIM)),
            pl.BlockSpec((2, HDIM), lambda h: (0, h)),
            whole_block((rows, HDIM)),
            whole_block((rows, HDIM)),
        ],
        [
            pl.BlockSpec((3, rows, HDIM), lambda h: (0, 0, h)),
            pl.BlockSpec((rows, HDIM), lambda h: (0, h)),
        ],
        [
            jax.ShapeDtypeStruct((3, rows, width // 3), jnp.bfloat16),
            jax.ShapeDtypeStruct((rows, width // 3), jnp.bfloat16),
        ],
        (projected, projected, projected, scale, gains, cosine, sine),
    )


def attend_back_body(
    low_ref,
    back_ref,
    query_ref,
    key_ref,
    scale_ref,
    gain_ref,
    cos_ref,
    sin_ref,
    hats_ref,
    value_out_ref,
    cross_ref,
    gain_out_ref,
    query_sum,
    key_sum,
    value_sum,
):
    rows = value_out_ref.shape[0]
    block = min(256, rows)
    for start in reversed(range(0, rows, block)):
        stop = start + block
        query, key, value = low_ref[0, start:stop], low_ref[1, :stop], low_ref[2, :stop]
        back = back_ref[start:stop]
        share = softmax_rows(query, key, start)
        back_share = lax.dot_general(
            back, value, COLUMN_CONTRACT, preferred_element_type=jnp.float32
        )
        mean = jnp.sum(share * back_share, axis=-1, keepdims=True)
        back_scores = (share * (back_share - mean)).astype(jnp.bfloat16)
        value_part = lax.dot_general(
            share.astype(jnp.bfloat16), back, ROW_CONTRACT, preferred_element_type=jnp.float32
        )
        key_part = lax.dot_general(
            back_scores, query, ROW_CONTRACT, preferred_element_type=jnp.float32
        )
        query_sum[start:stop] = jnp.dot(back_scores, key, preferred_element_type=jnp.float32)
        if stop == rows:
            value_sum[...] = value_part
            key_sum[...] = key_part
        else:
            value_sum[:stop] += value_part
            key_sum[:stop] += key_part
    value_out_ref[...] = value_sum[...].astype(jnp.bfloat16)
    cosine, sine = cos_ref[...], sin_ref[...]
    lanes = lax.broadcasted_iota(jnp.int32, cross_ref.shape, 1)
    cross = jnp.zeros(cross_ref.shape, jnp.float32)
    for at, (source, total) in enumerate(((query_ref, query_sum), (key_ref, key_sum))):
        normed = turned(total[...] * HDIM ** (-0.5), cosine, -sine)
        hat = source[...] * scale_ref[:, at : at + 1]
        gain_out_ref[at : at + 1] = jnp.sum(normed * hat, axis=0, keepdims=True)
        back_hat = normed * gain_ref[at : at + 1, :]
        hats_ref[at] = back_hat
        cross = jnp.where(lanes == at, jnp.sum(back_hat * hat, axis=-1, keepdims=True), cross)

    @pl.when(pl.program_id(0) == 0)
    def _():
        cross_ref[...] = cross

    @pl.when(pl.program_id(0) > 0)
    def _():
        cross_ref[...] += cross


def attend_back(low, back, projected, scale, gains, cosine, sine):
    rows, width = back.shape
    heads = width // HDIM
    head = pl.BlockSpec((rows, HDIM), lambda h: (0, h))
    return kernel(
        attend_back_body,
        (heads,),
        [pl.BlockSpec((3, rows, HDIM), lambda h: (0, 0, h)), head]
        + head_specs(rows, heads)[:2]
        + [
            whole_block((rows, HDIM)),
            pl.BlockSpec((2, HDIM), lambda h: (0, h)),
            whole_block((rows, HDIM)),
            whole_block((rows, HDIM)),
        ],
        [
            pl.BlockSpec((2, rows, HDIM), lambda h: (0, 0, h)),
            head,
            whole_block((rows, HDIM)),
            pl.BlockSpec((2, HDIM), lambda h: (0, h)),
        ],
        [
            jax.ShapeDtypeStruct((2, rows, width), jnp.float32),
            jax.ShapeDtypeStruct((rows, width), jnp.bfloat16),
            jax.ShapeDtypeStruct((rows, HDIM), jnp.float32),
            jax.ShapeDtypeStruct((2, width), jnp.float32),
        ],
        (low, back, projected, projected, scale, gains, cosine, sine),
        [pltpu.VMEM((rows, HDIM), jnp.float32)] * 3,
    )


def tokens_back_body(
    hats_ref, query_ref, key_ref, value_ref, scale_ref, mean_ref, weight_ref, back_ref, out_ref
):
    width = value_ref.shape[1]

    @pl.when(pl.program_id(0) == 0)
    def _():
        for at, source in enumerate((query_ref, key_ref)):
            scale = scale_ref[:, at : at + 1]
            hat = source[...] * scale
            back_ref[:, at * width : (at + 1) * width] = (
                scale * (hats_ref[at] - hat * mean_ref[:, at : at + 1])
            ).astype(jnp.bfloat16)
        back_ref[:, 2 * width :] = value_ref[...]

    out_ref[...] = lax.dot_general(
        back_ref[...], weight_ref[...], COLUMN_CONTRACT, preferred_element_type=jnp.float32
    ).astype(jnp.bfloat16)


def tokens_back_part(hats, projected, value_back, scale, mean, weight):
    rows, width = value_back.shape
    model_width = weight.shape[0]
    tile = min(512, model_width)
    return kernel(
        tokens_back_body,
        (model_width // tile,),
        [
            whole_block((2, rows, width)),
            pl.BlockSpec((rows, width), lambda n: (0, 0)),
            pl.BlockSpec((rows, width), lambda n: (0, 1)),
            whole_block((rows, width)),
            whole_block((rows, HDIM)),
            whole_block((rows, HDIM)),
            pl.BlockSpec((tile, 3 * width), lambda n: (n, 0)),
        ],
        [
            whole_block((rows, 3 * width)),
            pl.BlockSpec((rows, tile), lambda n: (0, n)),
        ],
        [
            jax.ShapeDtypeStruct((rows, 3 * width), jnp.bfloat16),
            jax.ShapeDtypeStruct((rows, model_width), jnp.bfloat16),
        ],
        (hats, projected, projected, value_back, scale, mean, weight),
    )


def norm_parts(raw):
    scale = lax.rsqrt(jnp.mean(raw * raw, axis=-1, keepdims=True) + NORM_EPS)
    return scale, raw * scale


def norm_back(scale, hat, back, gain):
    back_hat = back * gain
    return scale * (back_hat - hat * jnp.mean(back_hat * hat, axis=-1, keepdims=True))


def turn_body(
    place_ref, raw_mlp_ref, raw_ref, tokens_ref, back_ref, gains_ref, out_ref, low_ref, gain_out_ref
):
    _, attn_hat = norm_parts(raw_ref[...])
    scale, hat = norm_parts(raw_mlp_ref[...].astype(jnp.float32))
    hidden = tokens_ref[...].astype(jnp.float32) + attn_hat * gains_ref[0:1]
    out_ref[...] = (hidden + hat * gains_ref[1:2]).astype(jnp.bfloat16)
    back = back_ref[...].astype(jnp.float32)
    low_ref[...] = norm_back(scale, hat, back, gains_ref[1:2]).astype(jnp.bfloat16)
    gain_out_ref[...] = jnp.sum(back * hat, axis=0, keepdims=True)


def turn_rows(raw_mlp, raw_attn, tokens, back, chunk, gains):
    rows, width = raw_mlp.shape
    chunk_spec = pl.BlockSpec((rows, width), lambda n, place_ref: (chunk, 0))
    first = pl.BlockSpec((rows, width), lambda n, place_ref: (0, 0))
    return kernel(
        turn_body,
        (1,),
        [
            first,
            pl.BlockSpec((rows, width), lambda n, place_ref: (place_ref[0], 0)),
            chunk_spec,
            chunk_spec,
            whole_block(gains.shape),
        ],
        [first, first, whole_block((1, width))],
        [
            jax.ShapeDtypeStruct((rows, width), jnp.bfloat16),
            jax.ShapeDtypeStruct((rows, width), jnp.bfloat16),
            jax.ShapeDtypeStruct((1, width), jnp.float32),
        ],
        (raw_mlp, raw_attn, tokens, back, gains),
        order=lax.axis_index("tensor")[None],
    )


def output_back_body(
    place_ref,
    sum_ref,
    raw_ref,
    back_ref,
    gains_ref,
    weight_ref,
    hidden_ref,
    low_ref,
    gain_out_ref,
    rows_ref,
):
    @pl.when(pl.program_id(0) == 0)
    def _():
        scale, hat = norm_parts(raw_ref[...])
        back = back_ref[...].astype(jnp.float32) + sum_ref[...].astype(jnp.float32)
        hidden_ref[...] = back
        gain_out_ref[...] = jnp.sum(back * hat, axis=0, keepdims=True)
        low_ref[...] = norm_back(scale, hat, back, gains_ref[0:1]).astype(jnp.bfloat16)

    rows_ref[...] = jnp.dot(
        low_ref[...], weight_ref[...], preferred_element_type=jnp.float32
    ).astype(jnp.bfloat16)


def output_back_rows(summed, raw_attn, back, chunk, gains, weight):
    rows, width = summed.shape
    tile = min(512, width)
    first = pl.BlockSpec((rows, width), lambda n, place_ref: (0, 0))
    return kernel(
        output_back_body,
        (width // tile,),
        [
            first,
            pl.BlockSpec((rows, width), lambda n, place_ref: (place_ref[0], 0)),
            pl.BlockSpec((rows, width), lambda n, place_ref: (chunk, 0)),
            whole_block(gains.shape),
            pl.BlockSpec((width, tile), lambda n, place_ref: (0, n)),
        ],
        [
            first,
            first,
            whole_block((1, width)),
            pl.BlockSpec((rows, tile), lambda n, place_ref: (0, n)),
        ],
        [
            jax.ShapeDtypeStruct((rows, width), jnp.float32),
            jax.ShapeDtypeStruct((rows, width), jnp.bfloat16),
            jax.ShapeDtypeStruct((1, width), jnp.float32),
            jax.ShapeDtypeStruct((rows, width), jnp.bfloat16),
        ],
        (summed, raw_attn, back, gains, weight),
        order=lax.axis_index("tensor")[None],
    )


def product_of(left_refs, right_refs):
    total = None
    for left_ref, right_ref in zip(left_refs, right_refs):
        product = lax.dot_general(
            left_ref[...], right_ref[...], ROW_CONTRACT, preferred_element_type=jnp.float32
        )
        total = product if total is None else total + product
    return total


def sent_body(order_ref, *refs):
    parts = len(refs) // 2
    refs[-1][...] = product_of(refs[:parts], refs[parts:-1]).astype(jnp.bfloat16)


def kept_body(order_ref, *refs):
    parts = (len(refs) - 5) // 2
    got_ref = refs[2 * parts]
    x_send, y_send, x_keep, y_keep = refs[2 * parts + 1 :]
    step = pl.program_id(0)
    total = product_of(refs[:parts], refs[parts : 2 * parts]) + got_ref[...].astype(jnp.float32)
    total = total.astype(jnp.bfloat16)
    half = total.shape[1] // 2
    left, right = total[:, :half], total[:, half:]

    @pl.when(step < 2)
    def _():
        x_send[0] = left

    @pl.when((step == 1) | (step == 2))
    def _():
        y_send[0] = right

    @pl.when(step >= 2)
    def _():
        x_keep[0] = left

    @pl.when((step == 0) | (step == 3))
    def _():
        y_keep[0] = right


def quick(lefts, rights):
    count = lax.axis_size("dp")
    size = lefts[0].shape[1] // count
    return count == 8 and size % 128 == 0 and rights[0].shape[1] % 256 == 0


def grad_specs(lefts, rights, size):
    return [
        pl.BlockSpec((left.shape[0], size), lambda m, order_ref: (0, order_ref[m]))
        for left in lefts
    ] + [pl.BlockSpec(right.shape, lambda m, order_ref: (0, 0)) for right in rights]


def grad_sent(lefts, rights):
    if not quick(lefts, rights):
        return jnp.zeros((16, 128), jnp.bfloat16)
    size = lefts[0].shape[1] // 8
    width = rights[0].shape[1]
    order = jnp.array([3, 7, 5, 1], jnp.int32) ^ lax.axis_index("dp")
    return kernel(
        sent_body,
        (4,),
        grad_specs(lefts, rights, size),
        pl.BlockSpec((size, width), lambda m, order_ref: (m, 0)),
        jax.ShapeDtypeStruct((4 * size, width), jnp.bfloat16),
        (*lefts, *rights),
        order=order,
    )


def grad_kept(lefts, rights, got):
    if not quick(lefts, rights):
        return [
            sum(
                lax.dot_general(left, right, ROW_CONTRACT, preferred_element_type=jnp.float32)
                for left, right in zip(lefts, rights)
            )
        ]
    size = lefts[0].shape[1] // 8
    width = rights[0].shape[1]
    order = jnp.array([2, 6, 4, 0], jnp.int32) ^ lax.axis_index("dp")
    block = (1, size, width // 2)
    return kernel(
        kept_body,
        (4,),
        grad_specs(lefts, rights, size)
        + [pl.BlockSpec((size, width), lambda m, order_ref: (m, 0))],
        [
            pl.BlockSpec(block, lambda m, order_ref: (jnp.minimum(m, 1), 0, 0)),
            pl.BlockSpec(block, lambda m, order_ref: (m // 2, 0, 0)),
            pl.BlockSpec(block, lambda m, order_ref: (m // 3, 0, 0)),
            pl.BlockSpec(block, lambda m, order_ref: (m // 3, 0, 0)),
        ],
        [jax.ShapeDtypeStruct((2, size, width // 2), jnp.bfloat16)] * 4,
        (*lefts, *rights, got),
        order=order,
    )


def exchange_one(kept):
    if len(kept) == 1:
        return kept
    return [pair_swap(kept[0], 2), pair_swap(kept[1], 4)]


def wide(values):
    return values.astype(jnp.float32)


def exchange_two(kept, first):
    if len(kept) == 1:
        return kept
    x_next = wide(kept[2][0]) + wide(first[0][1])
    y_next = wide(kept[3][0]) + wide(first[1][0])
    return [
        pair_swap(x_next.astype(jnp.bfloat16), 4),
        pair_swap(y_next.astype(jnp.bfloat16), 2),
    ]


def exchange_end(kept, first, second):
    if len(kept) == 1:
        return lax.psum_scatter(
            kept[0].astype(jnp.bfloat16), "dp", scatter_dimension=0, tiled=True
        ).astype(jnp.float32)
    halves = [
        wide(kept[2][1]) + wide(first[0][0]) + wide(second[0]),
        wide(kept[3][1]) + wide(first[1][1]) + wide(second[1]),
    ]
    return jnp.concatenate(halves, axis=1)


def local(
    tokens,
    lengths,
    w_attn,
    w_mlp,
    norm_gains,
    moment_attn,
    square_attn,
    moment_mlp,
    square_mlp,
    moment_gains,
    square_gains,
    cotangent,
):
    rows_here, model_width = tokens.shape
    tensor_size = lax.axis_size("tensor")
    tensor_index = lax.axis_index("tensor")
    total_rows = rows_here * tensor_size
    seq_len = total_rows // lengths.shape[0]
    local_width = w_attn.shape[2]
    chunk_rows = rows_here // CHUNKS

    qkv_shard = jnp.concatenate([w_attn[k].astype(jnp.bfloat16) for k in range(3)], axis=1)
    mlp_low = w_mlp.astype(jnp.bfloat16)
    qkv_shard = after(qkv_shard, mlp_low)
    positions = doc_positions(lengths, seq_len).reshape(total_rows)

    gains_low = norm_gains.astype(jnp.bfloat16)
    hop, near, gains = lax.optimization_barrier(
        (line_hop(1, tokens, tokens), plane_one(qkv_shard), gains_over_tensor(gains_low))
    )
    hops = [hop]
    mlp_shard = after(mlp_low, near)
    mlp_full = lax.all_gather(mlp_shard, "dp", axis=1, tiled=True)
    hop, near, gains, mlp_shard = lax.optimization_barrier(
        (line_hop(2, *hop), plane_two(near), gains_over_dp(gains, 1), mlp_shard)
    )
    hops.append(hop)
    cos_table, sin_table = rope_tables(positions, HDIM)
    cosine = jnp.concatenate([cos_table, cos_table], axis=1)
    sine = jnp.concatenate([-sin_table, sin_table], axis=1)
    hop, qkv_full, gains, cosine, sine = lax.optimization_barrier(
        (line_hop(3, *hop), plane_three(near), gains_over_dp(gains, 2), cosine, sine)
    )
    hops.append(hop)
    whole_tokens = jnp.concatenate(line_pieces(tokens, hops), axis=0)
    bit = 4
    while bit < lax.axis_size("dp"):
        gains = gains_over_dp(gains, bit)
        bit = bit * 2
    gain_full = gains_end(gains)
    gain_values = gain_full.astype(jnp.float32)
    column_start = tensor_index * local_width
    head_gains = lax.dynamic_slice_in_dim(gain_values[2:], column_start, local_width, 1)

    def summed_lanes(lanes, work=lambda: ()):
        flat = lax.optimization_barrier(lanes[:, :2].T.reshape(-1, HDIM))
        total, given = small_sum(flat, work)
        return total.reshape(2, lanes.shape[0]), given

    def in_lanes(values):
        return jnp.pad(values.T, ((0, 0), (0, HDIM - 2)))

    projected, square_lanes = project(whole_tokens, qkv_full)
    inverse = lax.rsqrt(summed_lanes(square_lanes)[0] / model_width + NORM_EPS)
    inverse_lanes = in_lanes(inverse)
    out_piece = after(w_attn[3].astype(jnp.bfloat16), whole_tokens)
    out_shard = jnp.concatenate(shift_gather(out_piece), axis=1)
    inverse_lanes, out_shard = lax.optimization_barrier((inverse_lanes, out_shard))
    low_heads, mixed_low = attend(projected, inverse_lanes, head_gains, cosine, sine)
    mixed_pieces = mixed_low.reshape(tensor_size, CHUNKS, chunk_rows, local_width)

    def mixed_chunk(chunk):
        return mixed_pieces[:, chunk].reshape(tensor_size * chunk_rows, local_width)

    tokens_parted = whole_tokens.reshape(tensor_size, CHUNKS, chunk_rows, model_width)

    def own_part(values):
        parted = values.reshape((tensor_size, chunk_rows) + values.shape[1:])
        return lax.dynamic_index_in_dim(parted, tensor_index, 0, keepdims=False)

    chunks = range(CHUNKS)
    mixed, raw_attn, hidden_low, gate = ([None] * CHUNKS for _ in range(4))
    upper, inner_low, down_part, raw_mlp = ([None] * CHUNKS for _ in range(4))

    def forward(chunk):
        def first(_):
            hidden_low[chunk], raw_attn[chunk] = out_norm(
                mixed[chunk], out_full, tokens_parted, chunk, gain_values[:1]
            )
            return hidden_low[chunk], raw_attn[chunk]

        def second(given):
            hidden_low[chunk], raw_attn[chunk] = given
            outs = mlp_in(hidden_low[chunk], mlp_full)
            inner_low[chunk], gate[chunk], upper[chunk] = outs
            return outs

        def third(given):
            inner_low[chunk], gate[chunk], upper[chunk] = given
            down_part[chunk] = mlp_out(inner_low[chunk], mlp_full)
            return down_part[chunk]

        return first, second, third

    pieces, out_full = lax.optimization_barrier(
        (line_gather(mixed_chunk(0))[0], plane_three(plane_two(plane_one(out_shard))))
    )
    for chunk in chunks:
        mixed[chunk] = jnp.concatenate(pieces, axis=1)
        if chunk + 1 < CHUNKS:
            piece = after(mixed_chunk(chunk + 1), out_full if chunk == 0 else mixed[chunk])
            pieces, down_part[chunk] = line_gather(piece, forward(chunk))
        else:
            given = ()
            for work in forward(chunk):
                given = work(given)
        raw_mlp[chunk] = chunk_scatter(down_part[chunk])

    own_mixed = [own_part(mixed[chunk]) for chunk in chunks]
    out_parts, back_raw_mlp, gains_mlp = ([None] * CHUNKS for _ in range(3))
    gathered, gate_low, upper_low, hidden_part, back_sum = ([None] * CHUNKS for _ in range(5))

    def turn(chunk, raw):
        out_parts[chunk], back_raw_mlp[chunk], gains_mlp[chunk] = turn_rows(
            raw, raw_attn[chunk], tokens, cotangent, chunk, gain_values
        )

    def gather_rows(chunk, hops):
        pieces = line_pieces(back_raw_mlp[chunk], hops)
        gathered[chunk] = jnp.concatenate(pieces, axis=0)

    def back_inner(chunk):
        return mlp_back(gathered[chunk], mlp_full, gate[chunk], upper[chunk])

    def back_hidden_part(chunk):
        return hidden_back(gate_low[chunk], upper_low[chunk], mlp_full)

    turn(0, raw_mlp[0])
    early_one = line_hop(1, back_raw_mlp[0], back_raw_mlp[0])
    early_two, late_raw = together(line_hop(2, *early_one), raw_mlp[1])
    turn(1, late_raw)
    early_three, late_one = together(
        line_hop(3, *early_two), line_hop(1, back_raw_mlp[1], back_raw_mlp[1])
    )
    gather_rows(0, (early_one, early_two, early_three))
    late_two, (gate_low[0], upper_low[0]) = together(line_hop(2, *late_one), back_inner(0))
    late_three, hidden_part[0] = together(line_hop(3, *late_two), back_hidden_part(0))
    back_sum[0] = chunk_scatter(hidden_part[0])
    gather_rows(1, (late_one, late_two, late_three))
    gate_low[1], upper_low[1] = back_inner(1)
    hidden_part[1] = back_hidden_part(1)
    back_sum[1] = chunk_scatter(hidden_part[1])
    out_tokens = jnp.concatenate(out_parts, axis=0)

    back_hidden, gains_attn, back_raw_attn, back_rows = ([None] * CHUNKS for _ in range(4))

    def output_back(chunk, rows):
        outs = output_back_rows(rows, raw_attn[chunk], cotangent, chunk, gain_values, out_full)
        back_hidden[chunk], back_raw_attn[chunk], gains_attn[chunk], back_rows[chunk] = outs

    down_left = after(gathered, hidden_part)
    down_sent = grad_sent(down_left, inner_low)
    gate_sent = grad_sent(after(hidden_low, down_sent), gate_low)
    for chunk in chunks[:-1]:
        output_back(chunk, after(back_sum[chunk], gate_sent))
    down_kept = grad_kept(
        after(down_left, gate_sent, back_rows[:-1]), inner_low, pair_swap(down_sent, 1)
    )
    down_one = exchange_one(down_kept)
    upper_sent = grad_sent(after(hidden_low, down_kept), upper_low)
    gate_kept = grad_kept(after(hidden_low, upper_sent), gate_low, pair_swap(gate_sent, 1))
    output_back(CHUNKS - 1, after(back_sum[-1], gate_kept))
    gate_one = exchange_one(after(gate_kept, back_rows))
    back_mixed, (down_one, upper_kept, out_sent) = rows_to_heads(
        jnp.concatenate(back_rows, axis=0),
        lambda: (
            down_one,
            grad_kept(after(hidden_low, back_rows), upper_low, pair_swap(upper_sent, 1)),
            grad_sent(back_raw_attn, own_mixed),
        ),
    )
    upper_one = exchange_one(upper_kept)
    back_hats, value_back, cross_lanes, head_gain_grads = attend_back(
        low_heads, back_mixed, projected, inverse_lanes, head_gains, cosine, sine
    )
    cross_lanes = after(cross_lanes, gate_one)
    down_two = exchange_two(down_kept, after(down_one, cross_lanes))
    cross_sums, out_kept = summed_lanes(
        cross_lanes,
        lambda: grad_kept(
            after(back_raw_attn, cross_lanes), own_mixed, pair_swap(out_sent, 1)
        ),
    )
    out_one = exchange_one(out_kept)
    mean_lanes = in_lanes(cross_sums / model_width)
    qkv_back, tokens_part = tokens_back_part(
        back_hats, projected, value_back, inverse_lanes, mean_lanes, qkv_full
    )
    tokens_back = chunk_scatter(tokens_part)
    gain_grad = jnp.zeros((4, model_width), jnp.float32)
    gain_grad = gain_grad.at[0].set(sum(gains_attn)[0]).at[1].set(sum(gains_mlp)[0])
    gain_grad = lax.dynamic_update_slice(
        gain_grad, head_gain_grads, (jnp.int32(2), column_start)
    )
    gains = gains_blocks(gain_grad)
    qkv_left, gains = after(([whole_tokens], gains), tokens_part)
    qkv_sent = grad_sent(after(qkv_left, upper_one), [qkv_back])
    down_two, qkv_kept, gains = together(
        down_two,
        grad_kept(qkv_left, [qkv_back], pair_swap(qkv_sent, 1)),
        gains_fold(gains),
    )
    gate_two, upper_two, out_one = together(
        exchange_two(gate_kept, after(gate_one, qkv_kept)),
        exchange_two(upper_kept, after(upper_one, qkv_kept)),
        out_one,
    )
    mlp_owned = jnp.stack(
        [
            exchange_end(gate_kept, gate_one, gate_two),
            exchange_end(upper_kept, upper_one, upper_two),
            exchange_end(down_kept, down_one, down_two),
        ]
    )
    out_two, qkv_one, (new_mlp, new_moment_mlp, new_square_mlp), gains = together(
        exchange_two(out_kept, out_one),
        exchange_one(qkv_kept),
        adamw(w_mlp, mlp_owned, moment_mlp, square_mlp, RATE_MATRIX, DECAY_MATRIX),
        gains_rest(gains),
    )
    qkv_two, out_owned, gain_final = together(
        exchange_two(qkv_kept, qkv_one),
        shift_scatter(exchange_end(out_kept, out_one, out_two), local_width),
        gains_owned(sum(gains[1:], gains[0])),
    )
    qkv_owned = exchange_end(qkv_kept, qkv_one, qkv_two)
    attn_owned = jnp.stack(
        [qkv_owned[:, k * local_width : (k + 1) * local_width] for k in range(3)] + [out_owned]
    )
    attn_owned = lax.optimization_barrier(attn_owned)
    new_attn, new_moment_attn, new_square_attn = adamw(
        w_attn, attn_owned, moment_attn, square_attn, RATE_MATRIX, DECAY_MATRIX
    )
    new_gains, new_moment_gains, new_square_gains = adamw(
        norm_gains, gain_final, moment_gains, square_gains, RATE_GAIN, 0.0
    )
    tokens_back = after(tokens_back, new_mlp, new_attn, new_gains)
    grad_tokens = (jnp.concatenate(back_hidden, axis=0) + tokens_back.astype(jnp.float32)).astype(jnp.bfloat16)
    return (
        out_tokens,
        grad_tokens,
        new_attn,
        new_moment_attn,
        new_square_attn,
        new_mlp,
        new_moment_mlp,
        new_square_mlp,
        new_gains,
        new_moment_gains,
        new_square_gains,
    )


def solution(mesh):
    return jax.shard_map(
        local,
        mesh=mesh,
        in_specs=(
            P(("dp", "tensor"), None),
            P("dp", None),
            P(None, "dp", "tensor"),
            P(None, "dp", "tensor"),
            P(None, ("dp", "tensor")),
            P(None, "dp", "tensor"),
            P(None, "dp", "tensor"),
            P(None, "dp", "tensor"),
            P(None, "dp", "tensor"),
            P(None, ("dp", "tensor")),
            P(None, ("dp", "tensor")),
            P(("dp", "tensor"), None),
        ),
        out_specs=(
            P(("dp", "tensor"), None),
            P(("dp", "tensor"), None),
            P(None, "dp", "tensor"),
            P(None, "dp", "tensor"),
            P(None, "dp", "tensor"),
            P(None, "dp", "tensor"),
            P(None, "dp", "tensor"),
            P(None, "dp", "tensor"),
            P(None, ("dp", "tensor")),
            P(None, ("dp", "tensor")),
            P(None, ("dp", "tensor")),
        ),
        check_vma=False,
    )
```

```python
import jax
import jax.numpy as jnp
from jax import lax
from jax.experimental import pallas as pl
from jax.experimental.pallas import tpu as pltpu
from jax.sharding import PartitionSpec as P

HDIM = 128
STEP = 10
CHUNKS = 2
MIB = 1 << 20


NORM_EPS = 1e-06
ROPE_BASE = 500000.0
BETA_ONE = 0.9
BETA_TWO = 0.95
ADAM_EPS = 1e-08
RATE_MATRIX = 0.03
RATE_GAIN = 0.6
DECAY_MATRIX = 0.1
ROW_CONTRACT = (((0,), (0,)), ((), ()))
COLUMN_CONTRACT = (((1,), (1,)), ((), ()))


def doc_positions(lengths, seq_len):
    ends = jnp.cumsum(lengths, axis=-1, dtype=jnp.int32)
    starts = ends - lengths
    places = jnp.arange(seq_len, dtype=jnp.int32)
    inside = starts[:, None, :] <= places[None, :, None]
    begins = jnp.max(jnp.where(inside, starts[:, None, :], jnp.int32(0)), axis=-1)
    return places[None, :] - begins


def rope_tables(positions, head_dim):
    halfway = head_dim // 2
    powers = jnp.arange(halfway, dtype=jnp.float32) * (2.0 / head_dim)
    angles = positions.astype(jnp.float32)[:, None] * jnp.power(ROPE_BASE, -powers)
    return (jnp.cos(angles), jnp.sin(angles))


def adamw(weight, gradient, moment_one, moment_two, rate, decay):
    moment_one = BETA_ONE * moment_one + (1.0 - BETA_ONE) * gradient
    moment_two = BETA_TWO * moment_two + (1.0 - BETA_TWO) * gradient * gradient
    fix_one = 1.0 - BETA_ONE**STEP
    fix_two = 1.0 - BETA_TWO**STEP
    update = moment_one / fix_one / (jnp.sqrt(moment_two / fix_two) + ADAM_EPS)
    return (weight * (1.0 - rate * decay) - rate * update, moment_one, moment_two)


def pick(index, cases):
    if all(case is cases[0] for case in cases):
        return cases[0]
    return lax.select_n(index, *cases)


def after(values, *waits):
    return lax.optimization_barrier((values, waits))[0]


def chunk_scatter(part):
    return lax.psum_scatter(part, "tensor", scatter_dimension=0, tiled=True)


def line_hop(step, up, down):
    count = lax.axis_size("tensor")
    rising = [(i, i + 1) for i in range(step - 1, count - 1)]
    falling = [(i + 1, i) for i in range(count - step)]
    return lax.ppermute(up, "tensor", rising), lax.ppermute(down, "tensor", falling)


def line_pieces(piece, hops):
    count = lax.axis_size("tensor")
    here = lax.axis_index("tensor")
    low = [piece] + [hop[0] for hop in hops]
    high = [piece] + [hop[1] for hop in hops]
    return [
        pick(here, [low[i - owner] if i >= owner else high[owner - i] for i in range(count)])
        for owner in range(count)
    ]


def line_gather(piece, work=()):
    hops, given, pair = [], (), (piece, piece)
    for step in range(1, lax.axis_size("tensor")):
        pair = line_hop(step, *pair)
        if step - 1 < len(work):
            given = work[step - 1](given)
            pair, given = lax.optimization_barrier((pair, given))
        hops.append(pair)
    return line_pieces(piece, hops), given


def shift_gather(piece):
    count = lax.axis_size("tensor")
    here = lax.axis_index("tensor")
    got = [piece] + [lax.ppermute(piece, "tensor", pairs) for pairs in shifts(count)]
    return [
        pick(here, [got[(i - owner) % count] for i in range(count)]) for owner in range(count)
    ]


def together(*values):
    return lax.optimization_barrier(values)


def shift_scatter(values, width):
    count = lax.axis_size("tensor")
    here = lax.axis_index("tensor")
    total = lax.dynamic_slice_in_dim(values, here * width, width, 1)
    for k, pairs in enumerate(shifts(count), 1):
        part = lax.dynamic_slice_in_dim(values, lax.rem(here + k, count) * width, width, 1)
        got = lax.ppermute(part.astype(jnp.bfloat16), "tensor", pairs)
        total = total + got.astype(jnp.float32)
    return total


def shifts(count):
    return [[(i, (i + k) % count) for i in range(count)] for k in range(1, count)]


def small_sum(values, work=lambda: ()):
    got = [lax.ppermute(values, "tensor", pairs) for pairs in shifts(lax.axis_size("tensor"))]
    got, given = together(got, work())
    return sum(got, values), given


def rows_to_heads(values, work):
    count = lax.axis_size("tensor")
    here = lax.axis_index("tensor")
    rows, columns = values.shape
    width = columns // count
    got = [lax.dynamic_slice_in_dim(values, here * width, width, 1)]
    for k, pairs in enumerate(shifts(count), 1):
        block = lax.dynamic_slice_in_dim(values, lax.rem(here + k, count) * width, width, 1)
        got.append(lax.ppermute(block, "tensor", pairs))
    got, given = together(got, work())
    parts = [
        pick(here, [got[(i - owner) % count] for i in range(count)]) for owner in range(count)
    ]
    return jnp.concatenate(parts, axis=0), given


def pair_swap(values, bit):
    count = lax.axis_size("dp")
    return lax.ppermute(values, "dp", [(i, i ^ bit) for i in range(count)])


def gains_over_tensor(gains):
    count = lax.axis_size("tensor")
    here = lax.axis_index("tensor")
    got = [gains] + [lax.ppermute(gains, "tensor", pairs) for pairs in shifts(count)]
    return jnp.concatenate(
        [pick(here, [got[(i - owner) % count] for i in range(count)]) for owner in range(count)],
        axis=1,
    )[None]


def gains_over_dp(blocks, bit):
    if lax.axis_size("dp") & (lax.axis_size("dp") - 1):
        return blocks
    return jnp.concatenate([blocks, pair_swap(blocks, bit)], axis=0)


def gains_end(blocks):
    count = lax.axis_size("dp")
    if blocks.shape[0] != count:
        return lax.all_gather(blocks[0], "dp", axis=1, tiled=True)
    order = jnp.arange(count, dtype=jnp.int32) ^ lax.axis_index("dp")
    return jnp.moveaxis(blocks[order], 0, 1).reshape(blocks.shape[1], -1)


def gains_blocks(grads):
    count = lax.axis_size("dp")
    if count & (count - 1):
        return lax.psum_scatter(grads, "dp", scatter_dimension=1, tiled=True)[None]
    order = jnp.arange(count, dtype=jnp.int32) ^ lax.axis_index("dp")
    return jnp.moveaxis(grads.reshape(grads.shape[0], count, -1), 1, 0)[order]


def gains_fold(blocks):
    if blocks.shape[0] % 2:
        return blocks
    return blocks[0::2] + pair_swap(blocks[1::2], 1)


def gains_rest(blocks):
    step = max(1, lax.axis_size("dp") // blocks.shape[0])
    return [blocks[0]] + [pair_swap(blocks[d], step * d) for d in range(1, blocks.shape[0])]


def gains_owned(block):
    count = lax.axis_size("tensor")
    here = lax.axis_index("tensor")
    parts = jnp.moveaxis(block.reshape(block.shape[0], count, -1), 1, 0)
    total = lax.dynamic_index_in_dim(parts, here, 0, keepdims=False)
    for k, pairs in enumerate(shifts(count), 1):
        part = lax.dynamic_index_in_dim(parts, lax.rem(here + k, count), 0, keepdims=False)
        total = total + lax.ppermute(part, "tensor", pairs)
    return total


def kernel(body, grid, in_specs, out_specs, out_shape, operands, scratch=(), order=None):
    spec = pltpu.PrefetchScalarGridSpec(
        num_scalar_prefetch=0 if order is None else 1,
        grid=grid,
        in_specs=in_specs,
        out_specs=out_specs,
        scratch_shapes=scratch,
    )
    return pl.pallas_call(
        body,
        grid_spec=spec,
        out_shape=out_shape,
        compiler_params=pltpu.CompilerParams(vmem_limit_bytes=52 * MIB),
        cost_estimate=pl.CostEstimate(flops=1, bytes_accessed=1, transcendentals=0),
    )(*(() if order is None else (order,)), *operands)


def place_body(order_ref, *refs):
    step = pl.program_id(0)
    out_ref = refs[-1]
    half = out_ref.shape[1] // 2
    for side in range(2):
        own, from_x, from_y, low, high = refs[5 * side : 5 * side + 5]
        for at, piece in enumerate((own, from_x, from_y)):

            @pl.when(step == 4 * side + at)
            def _():
                out_ref[0] = piece[...]

        @pl.when(step == 4 * side + 3)
        def _():
            out_ref[0, :half] = low[...]
            out_ref[0, half:] = high[...]


def plane_one(shard):
    count = lax.axis_size("dp")
    if count != 8 or shard.shape[0] % 32:
        return (lax.all_gather(shard, "dp", axis=0, tiled=True),)
    return shard, pair_swap(shard, 2), pair_swap(shard, 4)


def plane_two(given):
    if len(given) == 1:
        return given
    shard, from_x, from_y = given
    half = shard.shape[0] // 2
    near = (*given, pair_swap(from_x[:half], 4), pair_swap(from_y[half:], 2))
    return (*near, *(pair_swap(piece, 1) for piece in given))


def plane_three(given):
    if len(given) == 1:
        return given[0]
    near, far = given[:5], given[5:]
    far = (*far, pair_swap(near[3], 1), pair_swap(near[4], 1))
    rows, width = near[0].shape
    order = jnp.array([0, 2, 4, 6, 1, 3, 5, 7], jnp.int32) ^ lax.axis_index("dp")
    whole = kernel(
        place_body,
        (8,),
        [whole_block(piece.shape) for piece in (*near, *far)],
        pl.BlockSpec((1, rows, width), lambda step, order_ref: (order_ref[step], 0, 0)),
        jax.ShapeDtypeStruct((8, rows, width), near[0].dtype),
        (*near, *far),
        order=order,
    )
    return whole.reshape(8 * rows, width)


def whole_block(shape):
    return pl.BlockSpec(shape, lambda *at: (0,) * len(shape))


def out_norm_body(mixed_ref, weight_ref, tokens_ref, gain_ref, hidden_ref, raw_ref, all_ref):
    step = pl.program_id(0)
    tile = weight_ref.shape[0]
    product = lax.dot_general(
        mixed_ref[...],
        weight_ref[...],
        COLUMN_CONTRACT,
        preferred_element_type=jnp.float32,
    )
    raw_ref[...] = product
    all_ref[step] = product

    @pl.when(step == pl.num_programs(0) - 1)
    def _():
        rows, width = hidden_ref.shape
        square = jnp.zeros((rows, 1), jnp.float32)
        for at in range(width // tile):
            square = square + jnp.sum(all_ref[at] * all_ref[at], axis=-1, keepdims=True)
        scale = lax.rsqrt(square / width + NORM_EPS)
        for at in range(width // tile):
            columns = slice(at * tile, (at + 1) * tile)
            place = tokens_ref[:, 0, :, columns].reshape(rows, tile).astype(jnp.float32)
            hidden_ref[:, columns] = (
                place + all_ref[at] * scale * gain_ref[:, columns]
            ).astype(jnp.bfloat16)


def out_norm(mixed, weight, tokens, chunk, gain):
    pieces, _, piece_rows, width = tokens.shape
    rows = pieces * piece_rows
    tile = min(512, width)
    part = pl.BlockSpec((pieces, 1, piece_rows, width), lambda n: (0, chunk, 0, 0))
    return kernel(
        out_norm_body,
        (width // tile,),
        [
            whole_block((rows, width)),
            pl.BlockSpec((tile, width), lambda n: (n, 0)),
            part,
            whole_block((1, width)),
        ],
        [whole_block((rows, width)), pl.BlockSpec((rows, tile), lambda n: (0, n))],
        [
            jax.ShapeDtypeStruct((rows, width), jnp.bfloat16),
            jax.ShapeDtypeStruct((rows, width), jnp.float32),
        ],
        (mixed, weight, tokens, gain),
        [pltpu.VMEM((width // tile, rows, tile), jnp.float32)],
    )


def mlp_in_body(hidden_ref, weight_ref, inner_ref, gate_ref, upper_ref):
    gate = jnp.dot(hidden_ref[...], weight_ref[0], preferred_element_type=jnp.float32)
    upper = jnp.dot(hidden_ref[...], weight_ref[1], preferred_element_type=jnp.float32)
    gate_ref[...] = gate
    upper_ref[...] = upper
    inner_ref[...] = (gate * jax.nn.sigmoid(gate) * upper).astype(jnp.bfloat16)


def mlp_in(hidden, weights):
    rows, depth = hidden.shape
    width = weights.shape[2]
    tile = min(512, width)
    out_spec = pl.BlockSpec((rows, tile), lambda n: (0, n))
    return kernel(
        mlp_in_body,
        (width // tile,),
        [whole_block((rows, depth)), pl.BlockSpec((2, depth, tile), lambda n: (0, 0, n))],
        [out_spec] * 3,
        [
            jax.ShapeDtypeStruct((rows, width), kind)
            for kind in (jnp.bfloat16, jnp.float32, jnp.float32)
        ],
        (hidden, weights),
    )


def mlp_out_body(inner_ref, weight_ref, out_ref):
    out_ref[...] = lax.dot_general(
        inner_ref[...], weight_ref[...], COLUMN_CONTRACT, preferred_element_type=jnp.float32
    ).astype(jnp.bfloat16)


def mlp_out(inner, weight):
    rows, depth = inner.shape
    width = weight.shape[-2]
    tile = min(512, width)
    if weight.ndim == 3:
        weight_spec = pl.BlockSpec((None, tile, depth), lambda n: (2, n, 0))
    else:
        weight_spec = pl.BlockSpec((tile, depth), lambda n: (n, 0))
    return kernel(
        mlp_out_body,
        (width // tile,),
        [whole_block((rows, depth)), weight_spec],
        pl.BlockSpec((rows, tile), lambda n: (0, n)),
        jax.ShapeDtypeStruct((rows, width), jnp.bfloat16),
        (inner, weight),
    )


def mlp_back_body(back_ref, weight_ref, gate_ref, upper_ref, back_gate_ref, back_upper_ref):
    back = jnp.dot(back_ref[...], weight_ref[...], preferred_element_type=jnp.float32)
    gate = gate_ref[...]
    share = jax.nn.sigmoid(gate)
    slope = share * (1.0 + gate * (1.0 - share))
    back_gate_ref[...] = (back * upper_ref[...] * slope).astype(jnp.bfloat16)
    back_upper_ref[...] = (back * (gate * share)).astype(jnp.bfloat16)


def mlp_back(back, weight, gate, upper):
    rows, depth = back.shape
    width = weight.shape[2]
    tile = min(512, width)
    spec = pl.BlockSpec((rows, tile), lambda n: (0, n))
    return kernel(
        mlp_back_body,
        (width // tile,),
        [
            whole_block((rows, depth)),
            pl.BlockSpec((None, depth, tile), lambda n: (2, 0, n)),
            spec,
            spec,
        ],
        [spec] * 2,
        [jax.ShapeDtypeStruct((rows, width), jnp.bfloat16)] * 2,
        (back, weight, gate, upper),
    )


def hidden_back_body(gate_ref, upper_ref, weight_ref, out_ref):
    out_ref[...] = (
        lax.dot_general(
            gate_ref[...], weight_ref[0], COLUMN_CONTRACT, preferred_element_type=jnp.float32
        )
        + lax.dot_general(
            upper_ref[...], weight_ref[1], COLUMN_CONTRACT, preferred_element_type=jnp.float32
        )
    ).astype(jnp.bfloat16)


def hidden_back(back_gate, back_upper, weights):
    rows, depth = back_gate.shape
    width = weights.shape[1]
    tile = min(512, width)
    return kernel(
        hidden_back_body,
        (width // tile,),
        [
            whole_block((rows, depth)),
            whole_block((rows, depth)),
            pl.BlockSpec((2, tile, depth), lambda n: (0, n, 0)),
        ],
        pl.BlockSpec((rows, tile), lambda n: (0, n)),
        jax.ShapeDtypeStruct((rows, width), jnp.bfloat16),
        (back_gate, back_upper, weights),
    )


def project_body(tokens_ref, weight_ref, out_ref, sums_ref):
    step = pl.program_id(0)
    product = jnp.dot(tokens_ref[...], weight_ref[...], preferred_element_type=jnp.float32)
    out_ref[...] = product
    sums = jnp.sum(product * product, axis=-1, keepdims=True)
    lanes = lax.broadcasted_iota(jnp.int32, sums_ref.shape, 1)

    @pl.when(step == 0)
    def _():
        sums_ref[...] = jnp.where(lanes == 0, sums, 0.0)

    @pl.when(step == 1)
    def _():
        sums_ref[...] = jnp.where(lanes == 1, sums, sums_ref[...])


def project(tokens, weight):
    rows, depth = tokens.shape
    width = weight.shape[1]
    return kernel(
        project_body,
        (3,),
        [whole_block((rows, depth)), pl.BlockSpec((depth, width // 3), lambda n: (0, n))],
        [pl.BlockSpec((rows, width // 3), lambda n: (0, n)), whole_block((rows, HDIM))],
        [
            jax.ShapeDtypeStruct((rows, width), jnp.float32),
            jax.ShapeDtypeStruct((rows, HDIM), jnp.float32),
        ],
        (tokens, weight),
    )


def turned(values, cosine, sine):
    return values * cosine + pltpu.roll(values, HDIM // 2, 1) * sine


def softmax_rows(query, key, start):
    scores = lax.dot_general(query, key, COLUMN_CONTRACT, preferred_element_type=jnp.float32)
    scores = scores * HDIM ** (-0.5)
    rows = start + lax.broadcasted_iota(jnp.int32, scores.shape, 0)
    columns = lax.broadcasted_iota(jnp.int32, scores.shape, 1)
    scores = jnp.where(columns <= rows, scores, -jnp.inf)
    weights = jnp.exp(scores - jnp.max(scores, axis=-1, keepdims=True))
    return weights / jnp.sum(weights, axis=-1, keepdims=True)


def attend_body(
    query_ref, key_ref, value_ref, scale_ref, gain_ref, cos_ref, sin_ref, low_ref, out_ref
):
    cosine, sine = cos_ref[...], sin_ref[...]
    for at, source in enumerate((query_ref, key_ref)):
        normed = source[...] * scale_ref[:, at : at + 1] * gain_ref[at : at + 1, :]
        low_ref[at] = turned(normed, cosine, sine).astype(jnp.bfloat16)
    low_ref[2] = value_ref[...].astype(jnp.bfloat16)
    rows = out_ref.shape[0]
    block = min(256, rows)
    for start in range(0, rows, block):
        stop = start + block
        share = softmax_rows(low_ref[0, start:stop], low_ref[1, :stop], start)
        out_ref[start:stop] = jnp.dot(
            share.astype(jnp.bfloat16), low_ref[2, :stop], preferred_element_type=jnp.float32
        ).astype(jnp.bfloat16)


def head_specs(rows, heads):
    return [
        pl.BlockSpec((rows, HDIM), lambda h, part=part: (0, part * heads + h)) for part in range(3)
    ]


def attend(projected, scale, gains, cosine, sine):
    rows, width = projected.shape
    heads = width // (3 * HDIM)
    return kernel(
        attend_body,
        (heads,),
        head_specs(rows, heads)
        + [
            whole_block((rows, HDIM)),
            pl.BlockSpec((2, HDIM), lambda h: (0, h)),
            whole_block((rows, HDIM)),
            whole_block((rows, HDIM)),
        ],
        [
            pl.BlockSpec((3, rows, HDIM), lambda h: (0, 0, h)),
            pl.BlockSpec((rows, HDIM), lambda h: (0, h)),
        ],
        [
            jax.ShapeDtypeStruct((3, rows, width // 3), jnp.bfloat16),
            jax.ShapeDtypeStruct((rows, width // 3), jnp.bfloat16),
        ],
        (projected, projected, projected, scale, gains, cosine, sine),
    )


def attend_back_body(
    low_ref,
    back_ref,
    query_ref,
    key_ref,
    scale_ref,
    gain_ref,
    cos_ref,
    sin_ref,
    hats_ref,
    value_out_ref,
    cross_ref,
    gain_out_ref,
    query_sum,
    key_sum,
    value_sum,
):
    rows = value_out_ref.shape[0]
    block = min(256, rows)
    for start in reversed(range(0, rows, block)):
        stop = start + block
        query, key, value = low_ref[0, start:stop], low_ref[1, :stop], low_ref[2, :stop]
        back = back_ref[start:stop]
        share = softmax_rows(query, key, start)
        back_share = lax.dot_general(
            back, value, COLUMN_CONTRACT, preferred_element_type=jnp.float32
        )
        mean = jnp.sum(share * back_share, axis=-1, keepdims=True)
        back_scores = (share * (back_share - mean)).astype(jnp.bfloat16)
        value_part = lax.dot_general(
            share.astype(jnp.bfloat16), back, ROW_CONTRACT, preferred_element_type=jnp.float32
        )
        key_part = lax.dot_general(
            back_scores, query, ROW_CONTRACT, preferred_element_type=jnp.float32
        )
        query_sum[start:stop] = jnp.dot(back_scores, key, preferred_element_type=jnp.float32)
        if stop == rows:
            value_sum[...] = value_part
            key_sum[...] = key_part
        else:
            value_sum[:stop] += value_part
            key_sum[:stop] += key_part
    value_out_ref[...] = value_sum[...].astype(jnp.bfloat16)
    cosine, sine = cos_ref[...], sin_ref[...]
    lanes = lax.broadcasted_iota(jnp.int32, cross_ref.shape, 1)
    cross = jnp.zeros(cross_ref.shape, jnp.float32)
    for at, (source, total) in enumerate(((query_ref, query_sum), (key_ref, key_sum))):
        normed = turned(total[...] * HDIM ** (-0.5), cosine, -sine)
        hat = source[...] * scale_ref[:, at : at + 1]
        gain_out_ref[at : at + 1] = jnp.sum(normed * hat, axis=0, keepdims=True)
        back_hat = normed * gain_ref[at : at + 1, :]
        hats_ref[at] = back_hat
        cross = jnp.where(lanes == at, jnp.sum(back_hat * hat, axis=-1, keepdims=True), cross)

    @pl.when(pl.program_id(0) == 0)
    def _():
        cross_ref[...] = cross

    @pl.when(pl.program_id(0) > 0)
    def _():
        cross_ref[...] += cross


def attend_back(low, back, projected, scale, gains, cosine, sine):
    rows, width = back.shape
    heads = width // HDIM
    head = pl.BlockSpec((rows, HDIM), lambda h: (0, h))
    return kernel(
        attend_back_body,
        (heads,),
        [pl.BlockSpec((3, rows, HDIM), lambda h: (0, 0, h)), head]
        + head_specs(rows, heads)[:2]
        + [
            whole_block((rows, HDIM)),
            pl.BlockSpec((2, HDIM), lambda h: (0, h)),
            whole_block((rows, HDIM)),
            whole_block((rows, HDIM)),
        ],
        [
            pl.BlockSpec((2, rows, HDIM), lambda h: (0, 0, h)),
            head,
            whole_block((rows, HDIM)),
            pl.BlockSpec((2, HDIM), lambda h: (0, h)),
        ],
        [
            jax.ShapeDtypeStruct((2, rows, width), jnp.float32),
            jax.ShapeDtypeStruct((rows, width), jnp.bfloat16),
            jax.ShapeDtypeStruct((rows, HDIM), jnp.float32),
            jax.ShapeDtypeStruct((2, width), jnp.float32),
        ],
        (low, back, projected, projected, scale, gains, cosine, sine),
        [pltpu.VMEM((rows, HDIM), jnp.float32)] * 3,
    )


def tokens_back_body(
    hats_ref, query_ref, key_ref, value_ref, scale_ref, mean_ref, weight_ref, back_ref, out_ref
):
    width = value_ref.shape[1]

    @pl.when(pl.program_id(0) == 0)
    def _():
        for at, source in enumerate((query_ref, key_ref)):
            scale = scale_ref[:, at : at + 1]
            hat = source[...] * scale
            back_ref[:, at * width : (at + 1) * width] = (
                scale * (hats_ref[at] - hat * mean_ref[:, at : at + 1])
            ).astype(jnp.bfloat16)
        back_ref[:, 2 * width :] = value_ref[...]

    out_ref[...] = lax.dot_general(
        back_ref[...], weight_ref[...], COLUMN_CONTRACT, preferred_element_type=jnp.float32
    ).astype(jnp.bfloat16)


def tokens_back_part(hats, projected, value_back, scale, mean, weight):
    rows, width = value_back.shape
    model_width = weight.shape[0]
    tile = min(512, model_width)
    return kernel(
        tokens_back_body,
        (model_width // tile,),
        [
            whole_block((2, rows, width)),
            pl.BlockSpec((rows, width), lambda n: (0, 0)),
            pl.BlockSpec((rows, width), lambda n: (0, 1)),
            whole_block((rows, width)),
            whole_block((rows, HDIM)),
            whole_block((rows, HDIM)),
            pl.BlockSpec((tile, 3 * width), lambda n: (n, 0)),
        ],
        [
            whole_block((rows, 3 * width)),
            pl.BlockSpec((rows, tile), lambda n: (0, n)),
        ],
        [
            jax.ShapeDtypeStruct((rows, 3 * width), jnp.bfloat16),
            jax.ShapeDtypeStruct((rows, model_width), jnp.bfloat16),
        ],
        (hats, projected, projected, value_back, scale, mean, weight),
    )


def norm_parts(raw):
    scale = lax.rsqrt(jnp.mean(raw * raw, axis=-1, keepdims=True) + NORM_EPS)
    return scale, raw * scale


def norm_back(scale, hat, back, gain):
    back_hat = back * gain
    return scale * (back_hat - hat * jnp.mean(back_hat * hat, axis=-1, keepdims=True))


def turn_body(
    place_ref, raw_mlp_ref, raw_ref, tokens_ref, back_ref, gains_ref, out_ref, low_ref, gain_out_ref
):
    _, attn_hat = norm_parts(raw_ref[...])
    scale, hat = norm_parts(raw_mlp_ref[...].astype(jnp.float32))
    hidden = tokens_ref[...].astype(jnp.float32) + attn_hat * gains_ref[0:1]
    out_ref[...] = (hidden + hat * gains_ref[1:2]).astype(jnp.bfloat16)
    back = back_ref[...].astype(jnp.float32)
    low_ref[...] = norm_back(scale, hat, back, gains_ref[1:2]).astype(jnp.bfloat16)
    gain_out_ref[...] = jnp.sum(back * hat, axis=0, keepdims=True)


def turn_rows(raw_mlp, raw_attn, tokens, back, chunk, gains):
    rows, width = raw_mlp.shape
    chunk_spec = pl.BlockSpec((rows, width), lambda n, place_ref: (chunk, 0))
    first = pl.BlockSpec((rows, width), lambda n, place_ref: (0, 0))
    return kernel(
        turn_body,
        (1,),
        [
            first,
            pl.BlockSpec((rows, width), lambda n, place_ref: (place_ref[0], 0)),
            chunk_spec,
            chunk_spec,
            whole_block(gains.shape),
        ],
        [first, first, whole_block((1, width))],
        [
            jax.ShapeDtypeStruct((rows, width), jnp.bfloat16),
            jax.ShapeDtypeStruct((rows, width), jnp.bfloat16),
            jax.ShapeDtypeStruct((1, width), jnp.float32),
        ],
        (raw_mlp, raw_attn, tokens, back, gains),
        order=lax.axis_index("tensor")[None],
    )


def output_back_body(
    place_ref,
    sum_ref,
    raw_ref,
    back_ref,
    gains_ref,
    weight_ref,
    hidden_ref,
    low_ref,
    gain_out_ref,
    rows_ref,
):
    @pl.when(pl.program_id(0) == 0)
    def _():
        scale, hat = norm_parts(raw_ref[...])
        back = back_ref[...].astype(jnp.float32) + sum_ref[...].astype(jnp.float32)
        hidden_ref[...] = back
        gain_out_ref[...] = jnp.sum(back * hat, axis=0, keepdims=True)
        low_ref[...] = norm_back(scale, hat, back, gains_ref[0:1]).astype(jnp.bfloat16)

    rows_ref[...] = jnp.dot(
        low_ref[...], weight_ref[...], preferred_element_type=jnp.float32
    ).astype(jnp.bfloat16)


def output_back_rows(summed, raw_attn, back, chunk, gains, weight):
    rows, width = summed.shape
    tile = min(512, width)
    first = pl.BlockSpec((rows, width), lambda n, place_ref: (0, 0))
    return kernel(
        output_back_body,
        (width // tile,),
        [
            first,
            pl.BlockSpec((rows, width), lambda n, place_ref: (place_ref[0], 0)),
            pl.BlockSpec((rows, width), lambda n, place_ref: (chunk, 0)),
            whole_block(gains.shape),
            pl.BlockSpec((width, tile), lambda n, place_ref: (0, n)),
        ],
        [
            first,
            first,
            whole_block((1, width)),
            pl.BlockSpec((rows, tile), lambda n, place_ref: (0, n)),
        ],
        [
            jax.ShapeDtypeStruct((rows, width), jnp.float32),
            jax.ShapeDtypeStruct((rows, width), jnp.bfloat16),
            jax.ShapeDtypeStruct((1, width), jnp.float32),
            jax.ShapeDtypeStruct((rows, width), jnp.bfloat16),
        ],
        (summed, raw_attn, back, gains, weight),
        order=lax.axis_index("tensor")[None],
    )


def product_of(left_refs, right_refs):
    total = None
    for left_ref, right_ref in zip(left_refs, right_refs):
        product = lax.dot_general(
            left_ref[...], right_ref[...], ROW_CONTRACT, preferred_element_type=jnp.float32
        )
        total = product if total is None else total + product
    return total


def sent_body(order_ref, *refs):
    parts = len(refs) // 2
    refs[-1][...] = product_of(refs[:parts], refs[parts:-1]).astype(jnp.bfloat16)


def kept_body(order_ref, *refs):
    parts = (len(refs) - 5) // 2
    got_ref = refs[2 * parts]
    x_send, y_send, x_keep, y_keep = refs[2 * parts + 1 :]
    step = pl.program_id(0)
    total = product_of(refs[:parts], refs[parts : 2 * parts]) + got_ref[...].astype(jnp.float32)
    total = total.astype(jnp.bfloat16)
    half = total.shape[1] // 2
    left, right = total[:, :half], total[:, half:]

    @pl.when(step < 2)
    def _():
        x_send[0] = left

    @pl.when((step == 1) | (step == 2))
    def _():
        y_send[0] = right

    @pl.when(step >= 2)
    def _():
        x_keep[0] = left

    @pl.when((step == 0) | (step == 3))
    def _():
        y_keep[0] = right


def quick(lefts, rights):
    count = lax.axis_size("dp")
    size = lefts[0].shape[1] // count
    return count == 8 and size % 128 == 0 and rights[0].shape[1] % 256 == 0


def grad_specs(lefts, rights, size):
    return [
        pl.BlockSpec((left.shape[0], size), lambda m, order_ref: (0, order_ref[m]))
        for left in lefts
    ] + [pl.BlockSpec(right.shape, lambda m, order_ref: (0, 0)) for right in rights]


def grad_sent(lefts, rights):
    if not quick(lefts, rights):
        return jnp.zeros((16, 128), jnp.bfloat16)
    size = lefts[0].shape[1] // 8
    width = rights[0].shape[1]
    order = jnp.array([3, 7, 5, 1], jnp.int32) ^ lax.axis_index("dp")
    return kernel(
        sent_body,
        (4,),
        grad_specs(lefts, rights, size),
        pl.BlockSpec((size, width), lambda m, order_ref: (m, 0)),
        jax.ShapeDtypeStruct((4 * size, width), jnp.bfloat16),
        (*lefts, *rights),
        order=order,
    )


def grad_kept(lefts, rights, got):
    if not quick(lefts, rights):
        return [
            sum(
                lax.dot_general(left, right, ROW_CONTRACT, preferred_element_type=jnp.float32)
                for left, right in zip(lefts, rights)
            )
        ]
    size = lefts[0].shape[1] // 8
    width = rights[0].shape[1]
    order = jnp.array([2, 6, 4, 0], jnp.int32) ^ lax.axis_index("dp")
    block = (1, size, width // 2)
    return kernel(
        kept_body,
        (4,),
        grad_specs(lefts, rights, size)
        + [pl.BlockSpec((size, width), lambda m, order_ref: (m, 0))],
        [
            pl.BlockSpec(block, lambda m, order_ref: (jnp.minimum(m, 1), 0, 0)),
            pl.BlockSpec(block, lambda m, order_ref: (m // 2, 0, 0)),
            pl.BlockSpec(block, lambda m, order_ref: (m // 3, 0, 0)),
            pl.BlockSpec(block, lambda m, order_ref: (m // 3, 0, 0)),
        ],
        [jax.ShapeDtypeStruct((2, size, width // 2), jnp.bfloat16)] * 4,
        (*lefts, *rights, got),
        order=order,
    )


def exchange_one(kept):
    if len(kept) == 1:
        return kept
    return [pair_swap(kept[0], 2), pair_swap(kept[1], 4)]


def wide(values):
    return values.astype(jnp.float32)


def exchange_two(kept, first):
    if len(kept) == 1:
        return kept
    x_next = wide(kept[2][0]) + wide(first[0][1])
    y_next = wide(kept[3][0]) + wide(first[1][0])
    return [
        pair_swap(x_next.astype(jnp.bfloat16), 4),
        pair_swap(y_next.astype(jnp.bfloat16), 2),
    ]


def exchange_end(kept, first, second):
    if len(kept) == 1:
        return lax.psum_scatter(
            kept[0].astype(jnp.bfloat16), "dp", scatter_dimension=0, tiled=True
        ).astype(jnp.float32)
    halves = [
        wide(kept[2][1]) + wide(first[0][0]) + wide(second[0]),
        wide(kept[3][1]) + wide(first[1][1]) + wide(second[1]),
    ]
    return jnp.concatenate(halves, axis=1)


def local(
    tokens,
    lengths,
    w_attn,
    w_mlp,
    norm_gains,
    moment_attn,
    square_attn,
    moment_mlp,
    square_mlp,
    moment_gains,
    square_gains,
    cotangent,
):
    rows_here, model_width = tokens.shape
    tensor_size = lax.axis_size("tensor")
    tensor_index = lax.axis_index("tensor")
    total_rows = rows_here * tensor_size
    seq_len = total_rows // lengths.shape[0]
    local_width = w_attn.shape[2]
    chunk_rows = rows_here // CHUNKS

    qkv_shard = jnp.concatenate([w_attn[k].astype(jnp.bfloat16) for k in range(3)], axis=1)
    mlp_low = w_mlp.astype(jnp.bfloat16)
    qkv_shard = after(qkv_shard, mlp_low)
    positions = doc_positions(lengths, seq_len).reshape(total_rows)

    gains_low = norm_gains.astype(jnp.bfloat16)
    hop, near, gains = lax.optimization_barrier(
        (line_hop(1, tokens, tokens), plane_one(qkv_shard), gains_over_tensor(gains_low))
    )
    hops = [hop]
    mlp_shard = after(mlp_low, near)
    mlp_full = lax.all_gather(mlp_shard, "dp", axis=1, tiled=True)
    hop, near, gains, mlp_shard = lax.optimization_barrier(
        (line_hop(2, *hop), plane_two(near), gains_over_dp(gains, 1), mlp_shard)
    )
    hops.append(hop)
    cos_table, sin_table = rope_tables(positions, HDIM)
    cosine = jnp.concatenate([cos_table, cos_table], axis=1)
    sine = jnp.concatenate([-sin_table, sin_table], axis=1)
    hop, qkv_full, gains, cosine, sine = lax.optimization_barrier(
        (line_hop(3, *hop), plane_three(near), gains_over_dp(gains, 2), cosine, sine)
    )
    hops.append(hop)
    whole_tokens = jnp.concatenate(line_pieces(tokens, hops), axis=0)
    bit = 4
    while bit < lax.axis_size("dp"):
        gains = gains_over_dp(gains, bit)
        bit = bit * 2
    gain_full = gains_end(gains)
    gain_values = gain_full.astype(jnp.float32)
    column_start = tensor_index * local_width
    head_gains = lax.dynamic_slice_in_dim(gain_values[2:], column_start, local_width, 1)

    def summed_lanes(lanes, work=lambda: ()):
        flat = lax.optimization_barrier(lanes[:, :2].T.reshape(-1, HDIM))
        total, given = small_sum(flat, work)
        return total.reshape(2, lanes.shape[0]), given

    def in_lanes(values):
        return jnp.pad(values.T, ((0, 0), (0, HDIM - 2)))

    projected, square_lanes = project(whole_tokens, qkv_full)
    inverse = lax.rsqrt(summed_lanes(square_lanes)[0] / model_width + NORM_EPS)
    inverse_lanes = in_lanes(inverse)
    out_piece = after(w_attn[3].astype(jnp.bfloat16), whole_tokens)
    out_shard = jnp.concatenate(shift_gather(out_piece), axis=1)
    inverse_lanes, out_shard = lax.optimization_barrier((inverse_lanes, out_shard))
    low_heads, mixed_low = attend(projected, inverse_lanes, head_gains, cosine, sine)
    mixed_pieces = mixed_low.reshape(tensor_size, CHUNKS, chunk_rows, local_width)

    def mixed_chunk(chunk):
        return mixed_pieces[:, chunk].reshape(tensor_size * chunk_rows, local_width)

    tokens_parted = whole_tokens.reshape(tensor_size, CHUNKS, chunk_rows, model_width)

    def own_part(values):
        parted = values.reshape((tensor_size, chunk_rows) + values.shape[1:])
        return lax.dynamic_index_in_dim(parted, tensor_index, 0, keepdims=False)

    chunks = range(CHUNKS)
    mixed, raw_attn, hidden_low, gate = ([None] * CHUNKS for _ in range(4))
    upper, inner_low, down_part, raw_mlp = ([None] * CHUNKS for _ in range(4))

    def forward(chunk):
        def first(_):
            hidden_low[chunk], raw_attn[chunk] = out_norm(
                mixed[chunk], out_full, tokens_parted, chunk, gain_values[:1]
            )
            return hidden_low[chunk], raw_attn[chunk]

        def second(given):
            hidden_low[chunk], raw_attn[chunk] = given
            outs = mlp_in(hidden_low[chunk], mlp_full)
            inner_low[chunk], gate[chunk], upper[chunk] = outs
            return outs

        def third(given):
            inner_low[chunk], gate[chunk], upper[chunk] = given
            down_part[chunk] = mlp_out(inner_low[chunk], mlp_full)
            return down_part[chunk]

        return first, second, third

    pieces, out_full = lax.optimization_barrier(
        (line_gather(mixed_chunk(0))[0], plane_three(plane_two(plane_one(out_shard))))
    )
    for chunk in chunks:
        mixed[chunk] = jnp.concatenate(pieces, axis=1)
        if chunk + 1 < CHUNKS:
            piece = after(mixed_chunk(chunk + 1), out_full if chunk == 0 else mixed[chunk])
            pieces, down_part[chunk] = line_gather(piece, forward(chunk))
        else:
            given = ()
            for work in forward(chunk):
                given = work(given)
        raw_mlp[chunk] = chunk_scatter(down_part[chunk])

    own_mixed = [own_part(mixed[chunk]) for chunk in chunks]
    out_parts, back_raw_mlp, gains_mlp = ([None] * CHUNKS for _ in range(3))
    gathered, gate_low, upper_low, hidden_part, back_sum = ([None] * CHUNKS for _ in range(5))

    def turn(chunk, raw):
        out_parts[chunk], back_raw_mlp[chunk], gains_mlp[chunk] = turn_rows(
            raw, raw_attn[chunk], tokens, cotangent, chunk, gain_values
        )

    def gather_rows(chunk, hops):
        pieces = line_pieces(back_raw_mlp[chunk], hops)
        gathered[chunk] = jnp.concatenate(pieces, axis=0)

    def back_inner(chunk):
        return mlp_back(gathered[chunk], mlp_full, gate[chunk], upper[chunk])

    def back_hidden_part(chunk):
        return hidden_back(gate_low[chunk], upper_low[chunk], mlp_full)

    turn(0, raw_mlp[0])
    early_one = line_hop(1, back_raw_mlp[0], back_raw_mlp[0])
    early_two, late_raw = together(line_hop(2, *early_one), raw_mlp[1])
    turn(1, late_raw)
    early_three, late_one = together(
        line_hop(3, *early_two), line_hop(1, back_raw_mlp[1], back_raw_mlp[1])
    )
    gather_rows(0, (early_one, early_two, early_three))
    late_two, (gate_low[0], upper_low[0]) = together(line_hop(2, *late_one), back_inner(0))
    late_three, hidden_part[0] = together(line_hop(3, *late_two), back_hidden_part(0))
    back_sum[0] = chunk_scatter(hidden_part[0])
    gather_rows(1, (late_one, late_two, late_three))
    gate_low[1], upper_low[1] = back_inner(1)
    hidden_part[1] = back_hidden_part(1)
    back_sum[1] = chunk_scatter(hidden_part[1])
    out_tokens = jnp.concatenate(out_parts, axis=0)

    back_hidden, gains_attn, back_raw_attn, back_rows = ([None] * CHUNKS for _ in range(4))

    def output_back(chunk, rows):
        outs = output_back_rows(rows, raw_attn[chunk], cotangent, chunk, gain_values, out_full)
        back_hidden[chunk], back_raw_attn[chunk], gains_attn[chunk], back_rows[chunk] = outs

    down_left = after(gathered, hidden_part)
    down_sent = grad_sent(down_left, inner_low)
    gate_sent = grad_sent(after(hidden_low, down_sent), gate_low)
    for chunk in chunks[:-1]:
        output_back(chunk, after(back_sum[chunk], gate_sent))
    down_kept = grad_kept(
        after(down_left, gate_sent, back_rows[:-1]), inner_low, pair_swap(down_sent, 1)
    )
    down_one = exchange_one(down_kept)
    upper_sent = grad_sent(after(hidden_low, down_kept), upper_low)
    gate_kept = grad_kept(after(hidden_low, upper_sent), gate_low, pair_swap(gate_sent, 1))
    output_back(CHUNKS - 1, after(back_sum[-1], gate_kept))
    gate_one = exchange_one(after(gate_kept, back_rows))
    back_mixed, (down_one, upper_kept, out_sent) = rows_to_heads(
        jnp.concatenate(back_rows, axis=0),
        lambda: (
            down_one,
            grad_kept(after(hidden_low, back_rows), upper_low, pair_swap(upper_sent, 1)),
            grad_sent(back_raw_attn, own_mixed),
        ),
    )
    upper_one = exchange_one(upper_kept)
    back_hats, value_back, cross_lanes, head_gain_grads = attend_back(
        low_heads, back_mixed, projected, inverse_lanes, head_gains, cosine, sine
    )
    cross_lanes = after(cross_lanes, gate_one)
    down_two = exchange_two(down_kept, after(down_one, cross_lanes))
    cross_sums, out_kept = summed_lanes(
        cross_lanes,
        lambda: grad_kept(
            after(back_raw_attn, cross_lanes), own_mixed, pair_swap(out_sent, 1)
        ),
    )
    out_one = exchange_one(out_kept)
    mean_lanes = in_lanes(cross_sums / model_width)
    qkv_back, tokens_part = tokens_back_part(
        back_hats, projected, value_back, inverse_lanes, mean_lanes, qkv_full
    )
    tokens_back = chunk_scatter(tokens_part)
    gain_grad = jnp.zeros((4, model_width), jnp.float32)
    gain_grad = gain_grad.at[0].set(sum(gains_attn)[0]).at[1].set(sum(gains_mlp)[0])
    gain_grad = lax.dynamic_update_slice(
        gain_grad, head_gain_grads, (jnp.int32(2), column_start)
    )
    gains = gains_blocks(gain_grad)
    qkv_left, gains = after(([whole_tokens], gains), tokens_part)
    qkv_sent = grad_sent(after(qkv_left, upper_one), [qkv_back])
    down_two, qkv_kept, gains = together(
        down_two,
        grad_kept(qkv_left, [qkv_back], pair_swap(qkv_sent, 1)),
        gains_fold(gains),
    )
    gate_two, upper_two, out_one = together(
        exchange_two(gate_kept, after(gate_one, qkv_kept)),
        exchange_two(upper_kept, after(upper_one, qkv_kept)),
        out_one,
    )
    mlp_owned = jnp.stack(
        [
            exchange_end(gate_kept, gate_one, gate_two),
            exchange_end(upper_kept, upper_one, upper_two),
            exchange_end(down_kept, down_one, down_two),
        ]
    )
    out_two, qkv_one, (new_mlp, new_moment_mlp, new_square_mlp), gains = together(
        exchange_two(out_kept, out_one),
        exchange_one(qkv_kept),
        adamw(w_mlp, mlp_owned, moment_mlp, square_mlp, RATE_MATRIX, DECAY_MATRIX),
        gains_rest(gains),
    )
    qkv_two, out_owned, gain_final = together(
        exchange_two(qkv_kept, qkv_one),
        shift_scatter(exchange_end(out_kept, out_one, out_two), local_width),
        gains_owned(sum(gains[1:], gains[0])),
    )
    qkv_owned = exchange_end(qkv_kept, qkv_one, qkv_two)
    attn_owned = jnp.stack(
        [qkv_owned[:, k * local_width : (k + 1) * local_width] for k in range(3)] + [out_owned]
    )
    attn_owned = lax.optimization_barrier(attn_owned)
    new_attn, new_moment_attn, new_square_attn = adamw(
        w_attn, attn_owned, moment_attn, square_attn, RATE_MATRIX, DECAY_MATRIX
    )
    new_gains, new_moment_gains, new_square_gains = adamw(
        norm_gains, gain_final, moment_gains, square_gains, RATE_GAIN, 0.0
    )
    tokens_back = after(tokens_back, new_mlp)
    grad_tokens = (jnp.concatenate(back_hidden, axis=0) + tokens_back.astype(jnp.float32)).astype(jnp.bfloat16)
    return (
        out_tokens,
        grad_tokens,
        new_attn,
        new_moment_attn,
        new_square_attn,
        new_mlp,
        new_moment_mlp,
        new_square_mlp,
        new_gains,
        new_moment_gains,
        new_square_gains,
    )


def solution(mesh):
    return jax.shard_map(
        local,
        mesh=mesh,
        in_specs=(
            P(("dp", "tensor"), None),
            P("dp", None),
            P(None, "dp", "tensor"),
            P(None, "dp", "tensor"),
            P(None, ("dp", "tensor")),
            P(None, "dp", "tensor"),
            P(None, "dp", "tensor"),
            P(None, "dp", "tensor"),
            P(None, "dp", "tensor"),
            P(None, ("dp", "tensor")),
            P(None, ("dp", "tensor")),
            P(("dp", "tensor"), None),
        ),
        out_specs=(
            P(("dp", "tensor"), None),
            P(("dp", "tensor"), None),
            P(None, "dp", "tensor"),
            P(None, "dp", "tensor"),
            P(None, "dp", "tensor"),
            P(None, "dp", "tensor"),
            P(None, "dp", "tensor"),
            P(None, "dp", "tensor"),
            P(None, ("dp", "tensor")),
            P(None, ("dp", "tensor")),
            P(None, ("dp", "tensor")),
        ),
        check_vma=False,
    )
```
